32 devices in a mesh: seq: 8 (over z, y), grp: 4 (over x, core).
Axes of the slice: x: 2, y: 2, z: 4, core: 2. Of those that a mesh axis runs over, the one named last changes fastest.
Arguments:
- tokens: bfloat16 [2, 8192, 2048], P(None, 'seq'), may hold values from -6 to 6
- cotangent: bfloat16 [2, 8192, 2048], P(None, 'seq'), may hold values from -6 to 6
- lengths: int32 [2, 6], replicated, may hold values from 1 to 7872, as said below
- attention_norm_gain: bfloat16 [2048], replicated, may hold values from 0.099609375 to 1.8984375
- feedforward_norm_gain: bfloat16 [2048], replicated, may hold values from 0.099609375 to 1.8984375
- query_weight: bfloat16 [2048, 2048], P('seq', 'grp'), may hold values from -0.125 to 0.125
- keyvalue_weight: bfloat16 [2048, 2, 512], P('seq', None, 'grp'), may hold values from -0.125 to 0.125
- output_weight: bfloat16 [2048, 2048], P('grp', 'seq'), may hold values from -1 to 1
- gate_up_weight: bfloat16 [2048, 2, 8192], P('seq', None, 'grp'), may hold values from -0.125 to 0.125
- down_weight: bfloat16 [8192, 2048], P('grp', 'seq'), may hold values from -0.0625 to 0.0625
- adapter_width_factor: bfloat16 [4, 2048, 8], P(None, 'seq'), may hold values from -0.125 to 0.125
- query_up_factor: bfloat16 [8, 2048], P(None, 'grp'), may hold values from -1 to 1
- keyvalue_up_factor: bfloat16 [2, 8, 512], P(None, None, 'grp'), may hold values from -1 to 1
- output_input_factor: bfloat16 [2048, 8], P('grp'), may hold values from -1 to 1
- query_feature_weight: bfloat16 [32, 64, 64], P('grp'), may hold values from -0.75 to 0.75
- key_feature_weight: bfloat16 [8, 64, 64], P('grp'), may hold values from -0.75 to 0.75
Outputs:
- block_out: bfloat16 [2, 8192, 2048], P(None, ('seq', 'grp'))
- grad_tokens: float32 [2, 8192, 2048], P(None, ('seq', 'grp'))
- grad_lora_in: float32 [4, 2048, 8], P(None, ('seq', 'grp'))
- grad_lora_q_up: float32 [8, 2048], P(None, 'grp')
- grad_lora_kv_up: float32 [2, 8, 512], P(None, None, 'grp')
- grad_lora_o_in: float32 [2048, 8], P('grp')
- grad_feat_query: float32 [32, 64, 64], P('grp')
- grad_feat_key: float32 [8, 64, 64], P('grp')
The draws below stay inside these ranges and needn't reach their ends.
Inputs may be any that keep to these rules, and one draw needn't show every extreme that they name: `lengths`: each micro-batch packs its 6 sequences in order, each starting at a multiple of 64 slots, and their whole blocks of 64 slots fill exactly 8192 slots; in one micro-batch, which one varies, one sequence starts within the first 1024 slots and ends within the last 1024.
All inputs are finite; a program needn't handle non-finite values.
Results may differ from the reference program's by a relative error of at most 0.02.
Values may be sent and summed in bfloat16 or wider, within the bound.
No kernel may reach another device: no remote copies, remote signals or barrier semaphores. Data moves between devices by JAX's collectives and lax.ppermute only.
A program may use at most 264 MiB of HBM per device.

```python
import jax
import jax.numpy as jnp
from jax import lax

MODEL_WIDTH = 2048
QUERY_HEADS = 32
KEYVALUE_HEADS = 8
HEAD_SIZE = 64
FF = 8192
ADAPTER_RANK = 8
STRETCH = 64
NSEQ = 6
MB = 2
TOK_DEV = 1024
GQ = 4
TOKENS = 8192


def draw_lengths(key, part):
    key = jax.random.fold_in(key, 11)
    per_device = TOK_DEV // STRETCH
    total = TOKENS // STRETCH
    key_pos, key_short, key_expo, key_extra, key_which, key_fill = jax.random.split(key, 6)
    places = jnp.arange(NSEQ, dtype=jnp.int32)[None, :]
    low_pos = max(0, NSEQ - per_device)
    high_pos = min(NSEQ - 1, per_device - 1)
    long_pick = jax.random.randint(key_pos, (1, 1), low_pos, high_pos + 1)
    before_most = (per_device - 1) // jnp.maximum(long_pick, 1)
    after_most = (per_device - 1) // jnp.maximum(NSEQ - 1 - long_pick, 1)
    most_short = jnp.where(places < long_pick, before_most, after_most)
    raw_short = jax.random.randint(key_short, (1, NSEQ), 0, 1 << 20)
    shorts = 1 + raw_short % most_short
    is_long = places == long_pick
    shorts = jnp.where(is_long, 0, shorts)
    span_blocks = jnp.where(is_long, total - jnp.sum(shorts, axis=1, keepdims=True), shorts)
    expo = jax.random.randint(key_expo, (1, NSEQ), 0, 6)
    heft = jnp.left_shift(jnp.ones((1, NSEQ), jnp.int32), expo)
    spare = total - NSEQ
    shares = 1 + heft * spare // jnp.sum(heft, axis=1, keepdims=True)
    extra = total - jnp.sum(shares, axis=1, keepdims=True)
    extra_pick = jax.random.randint(key_extra, (1, 1), 0, NSEQ)
    heavy_blocks = shares + jnp.where(places == extra_pick, extra, 0)
    which = jax.random.randint(key_which, (), 0, MB)
    batch_rows = jnp.arange(MB, dtype=jnp.int32)[:, None]
    blocks = jnp.where(batch_rows == which, span_blocks, heavy_blocks)
    fill = jax.random.randint(key_fill, (MB, NSEQ), 1, STRETCH + 1)
    return ((blocks - 1) * STRETCH + fill).astype(jnp.int32)


def levels(own_key, extent, shards, smallest, high):
    def one(axis_at, shards_of):
        draws = jax.random.uniform(jax.random.fold_in(jax.random.fold_in(own_key, 6), axis_at), (shards_of,), jnp.float32, smallest / len(shards), high / len(shards))
        return jnp.repeat(jnp.exp(draws), extent[axis_at] // shards_of).reshape((-1,) + (1,) * (len(extent) - axis_at - 1))

    level = one(*shards[0])
    for cut in shards[1:]:
        level = level * one(*cut)
    return level


def gaussian(own_key, shape, deviation, bound, shards=(), kind=jnp.bfloat16):
    array = deviation * jax.random.normal(own_key, shape, jnp.float32)
    if shards:
        array = array * levels(own_key, shape, shards, -0.22, 0.18)
    return jnp.clip(array, -bound, bound).astype(kind)


def setup_inputs(seed: int = 0) -> dict:
    streams_of = jax.random.split(jax.random.key(seed), 17)
    return {
        "tokens": gaussian(streams_of[0], (MB, TOKENS, MODEL_WIDTH), 1.0, 6.0, ((1, 8),)),
        "cotangent": gaussian(streams_of[1], (MB, TOKENS, MODEL_WIDTH), 1.0, 6.0, ((1, 8),)),
        "lengths": draw_lengths(jax.random.fold_in(streams_of[16], 71), 0),
        "attention_norm_gain": jnp.clip(1.0 + 0.18 * jax.random.normal(streams_of[3], (MODEL_WIDTH,), jnp.float32), 0.099609375, 1.8984375).astype(jnp.bfloat16),
        "feedforward_norm_gain": jnp.clip(1.0 + 0.18 * jax.random.normal(streams_of[4], (MODEL_WIDTH,), jnp.float32), 0.099609375, 1.8984375).astype(jnp.bfloat16),
        "query_weight": gaussian(streams_of[5], (MODEL_WIDTH, QUERY_HEADS * HEAD_SIZE), MODEL_WIDTH ** -0.5, 0.125, ((0, 8), (1, 4))),
        "keyvalue_weight": gaussian(streams_of[6], (MODEL_WIDTH, 2, KEYVALUE_HEADS * HEAD_SIZE), MODEL_WIDTH ** -0.5, 0.125, ((0, 8), (2, 4))),
        "output_weight": gaussian(streams_of[7], (QUERY_HEADS * HEAD_SIZE, MODEL_WIDTH), (QUERY_HEADS * HEAD_SIZE // 64) ** -0.5, 1.0, ((0, 4), (1, 8))),
        "gate_up_weight": gaussian(streams_of[8], (MODEL_WIDTH, 2, FF), MODEL_WIDTH ** -0.5, 0.125, ((0, 8), (2, 4))),
        "down_weight": gaussian(streams_of[9], (FF, MODEL_WIDTH), FF ** -0.5, 0.0625, ((0, 4), (1, 8))),
        "adapter_width_factor": gaussian(streams_of[10], (4, MODEL_WIDTH, ADAPTER_RANK), MODEL_WIDTH ** -0.5, 0.125, ((1, 8),)),
        "query_up_factor": gaussian(streams_of[11], (ADAPTER_RANK, QUERY_HEADS * HEAD_SIZE), (4 * ADAPTER_RANK) ** -0.5, 1.0, ((1, 4),)),
        "keyvalue_up_factor": gaussian(streams_of[12], (2, ADAPTER_RANK, KEYVALUE_HEADS * HEAD_SIZE), (4 * ADAPTER_RANK) ** -0.5, 1.0, ((2, 4),)),
        "output_input_factor": gaussian(streams_of[13], (QUERY_HEADS * HEAD_SIZE, ADAPTER_RANK), (QUERY_HEADS * HEAD_SIZE // 64) ** -0.5, 1.0, ((0, 4),)),
        "query_feature_weight": gaussian(streams_of[14], (QUERY_HEADS, HEAD_SIZE, HEAD_SIZE), HEAD_SIZE ** -0.5, 0.75, ((0, 4),)),
        "key_feature_weight": gaussian(streams_of[15], (KEYVALUE_HEADS, HEAD_SIZE, HEAD_SIZE), HEAD_SIZE ** -0.5, 0.75, ((0, 4),)),
    }


EPS = 1e-05
ADAPTER_SCALE = 2.0
PRECISE_MODE = lax.Precision.HIGHEST

@jax.custom_vjp
def low(v):
    return lax.optimization_barrier(v.astype(jnp.bfloat16)).astype(jnp.float32)

@jax.custom_vjp
def low_back(v):
    return v

def low_keep(v):
    return (low(v), None)

def low_pass(kept, grad):
    return (grad,)

def back_keep(v):
    return (v, None)

def back_low(kept, grad):
    return (low(grad),)
low.defvjp(low_keep, low_pass)
low_back.defvjp(back_keep, back_low)

def precise_matrix_product(left, right):
    return jnp.dot(left, right, precision=PRECISE_MODE)

def rms_norm(rows_in, gain):
    factor = lax.rsqrt(lax.optimization_barrier(jnp.mean(rows_in * rows_in, axis=-1, keepdims=True)) + EPS)
    return rows_in * factor * gain

def hedgehog(vectors, maps):
    mixed = jnp.einsum('cthd,hde->cthe', vectors, maps, precision=PRECISE_MODE)
    return jnp.concatenate([jax.nn.softmax(mixed, axis=-1), jax.nn.softmax(-mixed, axis=-1)], axis=-1)

def layout(lengths_row):
    blocks = (lengths_row + STRETCH - 1) // STRETCH
    starts = jnp.cumsum(blocks) - blocks
    total = TOKENS // STRETCH
    stretch_ids = jnp.arange(total, dtype=jnp.int32)
    sequence_owner = lax.optimization_barrier(jnp.sum((starts[None, :] <= stretch_ids[:, None]).astype(jnp.int32), axis=1)) - 1
    slots = jnp.arange(TOKENS, dtype=jnp.int32).reshape(total, STRETCH)
    member = (sequence_owner[:, None] == jnp.arange(NSEQ, dtype=jnp.int32)[None, :]).astype(jnp.int32)
    ends = lax.optimization_barrier(jnp.sum(member * (starts * STRETCH + lengths_row)[None, :], axis=1))
    valid_mask = (slots < ends[:, None]).astype(jnp.float32)
    return (sequence_owner, valid_mask)

def residual_block(input_rows, adapter_width_factor, query_up_factor, keyvalue_up_factor, output_input_factor, query_feature_weight, key_feature_weight, frozen_weight, sequence_owner, valid_mask):
    gain_attn, gain_mlp, query_weight, keyvalue_weight, output_weight, gate_up_weight, down_weight = frozen_weight
    total = sequence_owner.shape[0]
    scale = HEAD_SIZE ** (-0.5)
    normalized_input = low(rms_norm(input_rows, gain_attn))
    middle_rows = jnp.einsum('kv,mvs->kms', normalized_input, adapter_width_factor[:3], precision=PRECISE_MODE)
    query_vectors = precise_matrix_product(normalized_input, query_weight) + ADAPTER_SCALE * precise_matrix_product(middle_rows[:, 0], query_up_factor)
    keyvalue_rows = jnp.einsum('fc,cyq->fyq', normalized_input, keyvalue_weight, precision=PRECISE_MODE) + ADAPTER_SCALE * jnp.einsum('fxw,xwg->fxg', middle_rows[:, 1:3], keyvalue_up_factor, precision=PRECISE_MODE)
    query_vectors = low(low_back(query_vectors)).reshape(total, STRETCH, QUERY_HEADS, HEAD_SIZE)
    keyvalue_rows = low(low_back(keyvalue_rows)).reshape(total, STRETCH, 2, KEYVALUE_HEADS, HEAD_SIZE)
    keys = keyvalue_rows[:, :, 0]
    values = keyvalue_rows[:, :, 1]
    phi_query = hedgehog(query_vectors, query_feature_weight)
    phi_key = hedgehog(keys, key_feature_weight)
    masked = phi_key * valid_mask[:, :, None, None]
    stretch_states = jnp.einsum('ctkf,ctkd->ckfd', masked, values, precision=PRECISE_MODE)
    stretch_norms = lax.optimization_barrier(jnp.sum(masked, axis=1))
    order = jnp.arange(total, dtype=jnp.int32)
    lag = ((order[None, :] <= order[:, None] - 2) & (sequence_owner[None, :] == sequence_owner[:, None])).astype(jnp.float32)
    states = jnp.einsum('cj,jkfd->ckfd', lag, stretch_states, precision=PRECISE_MODE)
    norms = jnp.einsum('cj,jkf->ckf', lag, stretch_norms, precision=PRECISE_MODE)
    group_query = query_vectors.reshape(total, STRETCH, KEYVALUE_HEADS, GQ, HEAD_SIZE)
    group_phi = phi_query.reshape(total, STRETCH, KEYVALUE_HEADS, GQ, 2 * HEAD_SIZE)
    lin_num = jnp.einsum('ctkgf,ckfd->ckgtd', group_phi, states, precision=PRECISE_MODE)
    lin_den = jnp.einsum('ctkgf,ckf->ckgt', group_phi, norms, precision=PRECISE_MODE)
    before = jnp.concatenate([jnp.full((1,), -1, jnp.int32), sequence_owner[:-1]])
    win_keys = jnp.concatenate([jnp.concatenate([jnp.zeros_like(keys[:1]), keys[:-1]]), keys], axis=1)
    win_vals = jnp.concatenate([jnp.concatenate([jnp.zeros_like(values[:1]), values[:-1]]), values], axis=1)
    prev_valid = jnp.concatenate([jnp.zeros_like(valid_mask[:1]), valid_mask[:-1]]) * (before == sequence_owner).astype(jnp.float32)[:, None]
    inner = jnp.arange(STRETCH, dtype=jnp.int32)
    causal = (inner[None, :] <= inner[:, None]).astype(jnp.float32)
    mask = jnp.concatenate([jnp.broadcast_to(prev_valid[:, None, :], (total, STRETCH, STRETCH)), causal[None] * valid_mask[:, None, :]], axis=2)
    scores = low_back(jnp.einsum('ctkgd,cskd->ckgts', group_query, win_keys, precision=PRECISE_MODE) * scale)
    weights = jnp.exp(scores) * mask[:, None, None]
    win_den = lax.optimization_barrier(jnp.sum(weights, axis=-1))
    win_num = low_back(jnp.einsum('ckgts,cskd->ckgtd', low(weights), win_vals, precision=PRECISE_MODE))
    attended = (win_num + lin_num) / (win_den + lin_den)[..., None]
    attention_reduced = low(jnp.transpose(attended, (0, 3, 1, 2, 4)).reshape(TOKENS, QUERY_HEADS * HEAD_SIZE))
    side_branch = precise_matrix_product(attention_reduced, output_weight) + ADAPTER_SCALE * precise_matrix_product(precise_matrix_product(attention_reduced, output_input_factor), adapter_width_factor[3].T)
    resid = input_rows + low_back(side_branch)
    mlp_in = low(rms_norm(resid, gain_mlp))
    gate_up = low_back(jnp.einsum('td,dgf->tgf', mlp_in, gate_up_weight, precision=PRECISE_MODE))
    hidden = low(jax.nn.silu(gate_up[:, 0]) * gate_up[:, 1])
    return resid + low_back(precise_matrix_product(hidden, down_weight))

def reference(tokens, cotangent, lengths, attention_norm_gain, feedforward_norm_gain, query_weight, keyvalue_weight, output_weight, gate_up_weight, down_weight, adapter_width_factor, query_up_factor, keyvalue_up_factor, output_input_factor, query_feature_weight, key_feature_weight):
    frozen_weight = tuple((single_entry.astype(jnp.float32) for single_entry in (attention_norm_gain, feedforward_norm_gain, query_weight, keyvalue_weight, output_weight, gate_up_weight, down_weight)))
    trainable_weight = tuple((single_entry.astype(jnp.float32) for single_entry in (adapter_width_factor, query_up_factor, keyvalue_up_factor, output_input_factor, query_feature_weight, key_feature_weight)))
    outputs = []
    input_grads = []
    totals = tuple((jnp.zeros_like(single_entry) for single_entry in trainable_weight))
    for batch in range(MB):
        sequence_owner, valid_mask = layout(lengths[batch])

        def apply(x_in, lin, lqu, lkvu, loi, fquery, fkey):
            return residual_block(x_in, lin, lqu, lkvu, loi, fquery, fkey, frozen_weight, sequence_owner, valid_mask)
        primal, pullback = jax.vjp(apply, tokens[batch].astype(jnp.float32), trainable_weight[0], trainable_weight[1], trainable_weight[2], trainable_weight[3], trainable_weight[4], trainable_weight[5])
        grads = pullback(cotangent[batch].astype(jnp.float32))
        outputs.append(primal.astype(jnp.bfloat16))
        input_grads.append(grads[0])
        totals = tuple((acc + add for acc, add in zip(totals, grads[1:])))
    return (jnp.stack(outputs), jnp.stack(input_grads), totals[0], totals[1], totals[2], totals[3], totals[4], totals[5])
```

```python
import functools
import math

import jax
import jax.numpy as jnp
from jax import lax
from jax.experimental import pallas as pl
from jax.experimental.pallas import tpu as pltpu
from jax.sharding import PartitionSpec as P

STRETCH = 64
PAIR = 2 * STRETCH
WIN = 3 * STRETCH
EXT = 80
EPS = 1e-05
ADAPTER_SCALE = 2.0
BF = jnp.bfloat16
F32 = jnp.float32
VMEM_LIMIT = 48 * 1024 * 1024


def dotg(left, right, lc, rc):
    return lax.dot_general(left, right, (((lc,), (rc,)), ((), ())), preferred_element_type=F32)


def ring_order(count):
    if count % 8:
        return list(range(count))
    deep, wide = 4, count // 4
    path = [z * wide for z in range(deep)]
    for step, z in enumerate(reversed(range(deep))):
        ys = list(range(1, wide))
        path += [z * wide + y for y in (ys if step % 2 == 0 else ys[::-1])]
    return path


def ring_parts(shard):
    count = lax.axis_size("seq")
    order = ring_order(count)

    def hop(value, step):
        pairs = [(order[i], order[(i + step) % count]) for i in range(count)]
        return lax.ppermute(value, "seq", pairs)

    parts = [(0, 0, shard)]
    ahead = back = shard
    for distance in range(1, (count + 1) // 2):
        ahead, back = hop(ahead, 1), hop(back, -1)
        parts += [(-distance, 0, ahead), (distance, 0, back)]
    half = shard.shape[0] // 2
    parts.append((count // 2, 0, hop(ahead[:half], 1)))
    parts.append((count // 2, half, hop(back[half:], -1)))
    return parts


def ring_gather(shard):
    count = lax.axis_size("seq")
    order = ring_order(count)
    inverse = [0] * count
    for place, index in enumerate(order):
        inverse[index] = place
    me = jnp.asarray(inverse, jnp.int32)[lax.axis_index("seq")]
    table = jnp.asarray(order, jnp.int32)
    rows = shard.shape[0]
    out = jnp.zeros((count * rows,) + shard.shape[1:], shard.dtype)
    for offset, first, part in ring_parts(shard):
        source = table[(me + offset) % count]
        out = lax.dynamic_update_slice_in_dim(out, part, source * rows + first, 0)
    return out


def flip(value, axis, bit):
    count = lax.axis_size(axis)
    return lax.ppermute(value, axis, [(i, i ^ bit) for i in range(count)])


def group_gather(share):
    count = lax.axis_size("grp")
    out = []
    for far in range(0, count, 2):
        mine = share if far == 0 else flip(share, "grp", far)
        out += [mine, flip(mine, "grp", 1)]
    return out


def group_scatter(block):
    count = lax.axis_size("grp")
    total = None
    for far in list(range(2, count, 2)) + [0]:
        there = flip(block(far + 1).astype(BF), "grp", 1)
        both = block(far).astype(F32) + there.astype(F32)
        if far:
            both = flip(both.astype(BF), "grp", far).astype(F32)
        total = both if total is None else total + both
    return total


def shifted(value, axis, steps):
    count = lax.axis_size(axis)
    first, last = max(0, -steps), min(count, count - steps)
    return lax.ppermute(value, axis, [(i, i + steps) for i in range(first, last)])


def small_sums(wide, rest):
    n_seq, n_grp = lax.axis_size("seq"), lax.axis_size("grp")
    seq_index, group_index = lax.axis_index("seq"), lax.axis_index("grp")
    planes = wide.shape[0]
    blocks = wide.reshape(planes, n_seq, n_grp, -1).transpose(2, 1, 0, 3)
    blocks = jnp.take(blocks, jnp.arange(n_grp) ^ group_index, axis=0)
    blocks = jnp.take(blocks, jnp.arange(n_seq) ^ seq_index, axis=1)
    bit = n_grp // 2
    while bit:
        sent = flip(blocks[bit:].astype(BF), "grp", bit)
        blocks = blocks[:bit] + sent.astype(F32)
        bit //= 2
    blocks = blocks[0]
    rest = rest.astype(BF)
    bit = n_seq // 2
    while bit:
        cut = blocks[bit:].astype(BF)
        packed = jnp.concatenate([rest, cut.reshape(-1)])
        sent = flip(packed, "seq", bit)
        rest = (rest.astype(F32) + sent[: rest.shape[0]].astype(F32)).astype(BF)
        blocks = blocks[:bit] + sent[rest.shape[0] :].reshape(cut.shape).astype(F32)
        bit //= 2
    return blocks[0], rest.astype(F32)


def owners(stretch_ids, starts):
    return jnp.sum((starts[None, :] <= stretch_ids[:, None]).astype(jnp.int32), axis=1) - 1


def layout(lengths_row, base, blocks):
    counts = (lengths_row + STRETCH - 1) // STRETCH
    starts = jnp.cumsum(counts) - counts
    ids = base + jnp.arange(-3, blocks + 2, dtype=jnp.int32)
    owner = owners(ids, starts)
    ends = starts * STRETCH + lengths_row
    member = owner[:, None] == jnp.arange(starts.shape[0], dtype=jnp.int32)[None, :]
    end = jnp.sum(jnp.where(member, ends[None, :], 0), axis=1)
    valid = jnp.clip(end - ids * STRETCH, 0, STRETCH)[2:]
    one = (owner[2:] == owner[1:-1]).astype(jnp.int32)
    two = (owner[2:] == owner[:-2]).astype(jnp.int32)
    return jnp.stack([valid, one, two]), starts


def half_mask(shape):
    return (lax.broadcasted_iota(jnp.int32, shape, 1) & (PAIR - 1)) < STRETCH


def states_kernel(tab, kv_ref, wk_ref, phi_ref, ve_ref, st_ref, tail_ref, carry):
    step = pl.program_id(0)
    heads = kv_ref.shape[1] // PAIR

    @pl.when(step == 0)
    def _():
        carry[...] = jnp.zeros_like(carry)

    one_a, one_b = (tab[1, 2 * step + 1 + i].astype(F32) for i in range(2))
    lane = lax.broadcasted_iota(jnp.int32, (1, PAIR), 1)
    low = lane < STRETCH
    inside = lane & (STRETCH - 1)
    valid = inside < jnp.where(low, tab[0, 2 * step + 1], tab[0, 2 * step + 2])
    valid = jnp.where(valid, 1.0, 0.0)
    valid_low = jnp.where(low, valid, 0.0)
    valid_high = valid - valid_low
    wide = lax.broadcasted_iota(jnp.int32, (PAIR, PAIR), 1)
    for k in range(heads):
        kv = kv_ref[:, k * PAIR : (k + 1) * PAIR]
        moved = pltpu.roll(kv.astype(F32), STRETCH, 1)
        ve = jnp.where(
            wide < STRETCH, moved, jnp.where(wide < STRETCH + 2, 1.0, 0.0)
        ).astype(BF)
        ve_ref[:, k * PAIR : (k + 1) * PAIR] = ve
        mixed = dotg(wk_ref[k], kv, 1, 1)
        top = jnp.exp(mixed - jnp.max(mixed, axis=0, keepdims=True))
        bottom = jnp.exp(jnp.min(mixed, axis=0, keepdims=True) - mixed)
        top = top * (1.0 / jnp.sum(top, axis=0, keepdims=True))
        bottom = bottom * (1.0 / jnp.sum(bottom, axis=0, keepdims=True))
        phi = jnp.concatenate([top, bottom], axis=0)
        phi_ref[k * PAIR : (k + 1) * PAIR, :] = (phi * valid).astype(BF)
        first = dotg(ve, (phi * valid_low).astype(BF), 0, 1)[:EXT]
        second = dotg(ve, (phi * valid_high).astype(BF), 0, 1)[:EXT]
        st_ref[0, k, :EXT] = first
        st_ref[0, k, EXT:] = second
        mid = carry[k] * one_a + first
        tail = mid * one_b + second
        carry[k] = tail
        tail_ref[k, 0] = mid.astype(BF)
        tail_ref[k, 1] = tail.astype(BF)


def window_mask(tab, pair):
    lane = lax.broadcasted_iota(jnp.int32, (1, PAIR), 1)
    low = lane < STRETCH
    before = tab[0, 2 * pair] * tab[1, 2 * pair + 1]
    limits = [
        jnp.where(low, before, 0),
        jnp.where(
            low,
            jnp.minimum(lane + 1, tab[0, 2 * pair + 1]),
            tab[0, 2 * pair + 1] * tab[1, 2 * pair + 2],
        ),
        jnp.where(low, 0, jnp.minimum(lane - STRETCH + 1, tab[0, 2 * pair + 2])),
    ]
    row = lax.broadcasted_iota(jnp.int32, (STRETCH, PAIR), 0)
    return jnp.concatenate([jnp.where(row < limit, 1.0, 0.0) for limit in limits], axis=0)


def forward_kernel(
    per, scale, tab, q_ref, kv_ref, ve_ref, wq_ref, st_ref, ent_ref,
    att_ref, w_ref, phi_ref, s_ref, r_ref, carry,
):
    step = pl.program_id(0)
    heads = kv_ref.shape[1] // PAIR

    @pl.when(step == 0)
    def _():
        carry[...] = ent_ref[...]

    one_a, one_b = (tab[1, 2 * step + 1 + i].astype(F32) for i in range(2))
    two_a, two_b = (tab[2, 2 * step + 1 + i].astype(F32) for i in range(2))
    mask = window_mask(tab, step)
    mask = jnp.concatenate([mask] * per, axis=1)
    lanes = per * PAIR
    low = half_mask((EXT, lanes))
    rows = pl.ds(pl.multiple_of(step * PAIR, PAIR), WIN)
    for k in range(heads):
        kv = kv_ref[rows, k * PAIR : (k + 1) * PAIR]
        ve = ve_ref[rows, k * PAIR : (k + 1) * PAIR]
        base = k * per * STRETCH
        stacked = q_ref[base : base + per * STRETCH, :]
        q = jnp.concatenate(
            [stacked[g * STRETCH : (g + 1) * STRETCH] for g in range(per)], axis=1
        )
        q = jnp.concatenate([q, jnp.zeros_like(q)], axis=0)
        scores = dotg(kv, q, 1, 0)
        weights = (jnp.exp2(scores * scale) * mask).astype(BF)
        w_ref[0, k] = weights
        mixed = dotg(wq_ref[k], stacked, 1, 0)
        parts = []
        for g in range(per):
            u = mixed[g * STRETCH : (g + 1) * STRETCH]
            top = jnp.exp(u - jnp.max(u, axis=0, keepdims=True))
            bottom = jnp.exp(jnp.min(u, axis=0, keepdims=True) - u)
            top = top * (1.0 / jnp.sum(top, axis=0, keepdims=True))
            bottom = bottom * (1.0 / jnp.sum(bottom, axis=0, keepdims=True))
            parts.append(jnp.concatenate([top, bottom], axis=0).astype(BF))
        phi = jnp.concatenate(parts, axis=1)
        phi_ref[0, k] = phi
        older, old = carry[k, 0], carry[k, 1]
        states = jnp.concatenate([older * two_a, old * two_b], axis=0).astype(BF)
        s_ref[0, k] = states
        linear = dotg(states, phi, 1, 0)
        total = dotg(ve, weights, 0, 0)[:EXT] + jnp.where(low, linear[:EXT], linear[EXT:])
        inverse = 1.0 / total[STRETCH : STRETCH + 1]
        att = (total[:STRETCH] * inverse).astype(BF)
        for g in range(per):
            att_ref[base + g * STRETCH : base + (g + 1) * STRETCH, :] = att[
                :, g * PAIR : (g + 1) * PAIR
            ]
            r_ref[0, k * per + g : k * per + g + 1, :] = inverse[:, g * PAIR : (g + 1) * PAIR]
        current = old * one_a + st_ref[0, k, :EXT]
        carry[k, 0] = current
        carry[k, 1] = current * one_b + st_ref[0, k, EXT:]


def backward_kernel(
    per, pairs, scale, tab, order, q_ref, kv_ref, ve_ref, wq_ref, d_ref, att_ref, w_ref, phi_ref,
    s_ref, r_ref, dq_ref, dkv_ref, ds_ref, head_ref, map_ref, carry,
):
    step = pl.program_id(0)
    pair = pairs - 1 - step
    heads = kv_ref.shape[1] // PAIR

    @pl.when(step == 0)
    def _():
        carry[...] = jnp.zeros_like(carry)
        dkv_ref[...] = jnp.zeros_like(dkv_ref)
        map_ref[...] = jnp.zeros_like(map_ref)

    one_b = tab[1, 2 * pair + 2].astype(F32)
    one_c = tab[1, 2 * pair + 3].astype(F32)
    lanes = per * PAIR
    low = half_mask((EXT, lanes))
    rows = pl.ds(pl.multiple_of(pair * PAIR, PAIR), WIN)
    for k in range(heads):
        kv = kv_ref[rows, k * PAIR : (k + 1) * PAIR]
        ve = ve_ref[rows, k * PAIR : (k + 1) * PAIR]
        base = k * per * STRETCH

        def side(ref):
            return jnp.concatenate(
                [ref[base + g * STRETCH : base + (g + 1) * STRETCH, :] for g in range(per)], axis=1
            )

        stacked = q_ref[base : base + per * STRETCH, :]
        q = side(q_ref)
        d_att = side(d_ref)
        att = side(att_ref).astype(F32)
        inverse = jnp.concatenate(
            [r_ref[0, k * per + g : k * per + g + 1, :] for g in range(per)], axis=1
        )
        ratio = d_att * inverse
        d_den = -jnp.sum(ratio * att, axis=0, keepdims=True)
        d_high = d_den.astype(BF).astype(F32)
        row = lax.broadcasted_iota(jnp.int32, (EXT - STRETCH, lanes), 0)
        extra = jnp.where(row == 0, d_high, jnp.where(row == 1, d_den - d_high, 0.0))
        ratio_ext = jnp.concatenate([ratio, extra], axis=0)
        ratio_low = ratio_ext.astype(BF)
        weights = w_ref[0, k]
        padded = jnp.concatenate(
            [ratio_low, jnp.zeros((PAIR - EXT, lanes), BF)], axis=0
        )
        d_weights = dotg(ve, padded, 1, 0)
        d_scores = (d_weights * weights.astype(F32)).astype(BF)
        d_query = dotg(kv, d_scores, 0, 0)[:STRETCH] * scale
        zeros = jnp.zeros((STRETCH, lanes), BF)
        q_scaled = (q.astype(F32) * scale).astype(BF)
        d_kv = dotg(d_scores, jnp.concatenate([q_scaled, zeros], axis=0), 1, 1) + dotg(
            weights, jnp.concatenate([zeros, ratio_low[:STRETCH]], axis=0), 1, 1
        )
        dkv_ref[rows, k * PAIR : (k + 1) * PAIR] += d_kv
        phi = phi_ref[0, k]
        both = jnp.concatenate(
            [jnp.where(low, ratio_ext, 0.0), jnp.where(low, 0.0, ratio_ext)], axis=0
        ).astype(BF)
        d_phi = dotg(s_ref[0, k], both, 0, 0)
        d_state = dotg(both, phi, 1, 1)
        ds_ref[0, k] = d_state
        top, bottom = phi[:STRETCH].astype(F32), phi[STRETCH:].astype(F32)
        a, b = d_phi[:STRETCH], d_phi[STRETCH:]
        d_mixed = top * (a - jnp.sum(top * a, axis=0, keepdims=True)) - bottom * (
            b - jnp.sum(bottom * b, axis=0, keepdims=True)
        )
        d_mixed = d_mixed.astype(BF)
        d_mixed = jnp.concatenate(
            [d_mixed[:, g * PAIR : (g + 1) * PAIR] for g in range(per)], axis=0
        )
        d_stacked = jnp.concatenate(
            [d_query[:, g * PAIR : (g + 1) * PAIR] for g in range(per)], axis=0
        ) + dotg(wq_ref[k], d_mixed, 0, 0)
        dq_ref[base : base + per * STRETCH, :] = d_stacked.astype(BF)
        map_ref[k] += dotg(stacked, d_mixed, 1, 1)
        rest = d_state[EXT:] + one_c * carry[k]
        head = d_state[:EXT] + one_b * rest
        carry[k] = head
        head_ref[k, 0] = rest.astype(BF)
        head_ref[k, 1] = head.astype(BF)


def keys_kernel(
    pairs, tab, kv_ref, ve_ref, wk_ref, phi_ref, dkv_ref, back_ref, ds_ref, ent_ref,
    out_ref, map_ref, carry,
):
    step = pl.program_id(0)
    pair = pairs - 1 - step
    heads = kv_ref.shape[1] // PAIR

    @pl.when(step == 0)
    def _():
        carry[...] = ent_ref[...]
        map_ref[...] = jnp.zeros_like(map_ref)

    one_b = tab[1, 2 * pair + 2].astype(F32)
    one_c = tab[1, 2 * pair + 3].astype(F32)
    two_c = tab[2, 2 * pair + 3].astype(F32)
    two_d = tab[2, 2 * pair + 4].astype(F32)
    row = lax.broadcasted_iota(jnp.int32, (PAIR, PAIR), 0)
    lane = lax.broadcasted_iota(jnp.int32, (PAIR, PAIR), 1)
    last = jnp.where(step == 0, 1.0, 0.0)
    rows = pl.ds(pl.multiple_of(pair * PAIR + STRETCH, STRETCH), PAIR)
    for k in range(heads):
        kv = kv_ref[rows, k * PAIR : (k + 1) * PAIR]
        ve = ve_ref[rows, k * PAIR : (k + 1) * PAIR].astype(F32)
        next_one, next_two = carry[k, 0], carry[k, 1]
        pad = jnp.zeros((PAIR - EXT, PAIR), F32)
        grads = jnp.concatenate(
            [next_one * two_c, pad, next_two * two_d, pad], axis=0
        ).astype(BF)
        both = jnp.concatenate(
            [jnp.where(row < STRETCH, ve, 0.0), jnp.where(row < STRETCH, 0.0, ve)], axis=1
        ).astype(BF)
        d_phi = dotg(grads, both, 0, 1)
        phi = phi_ref[k * PAIR : (k + 1) * PAIR, :]
        d_both = dotg(phi, grads, 0, 1)
        d_value = jnp.where(row < STRETCH, d_both[:, :PAIR], d_both[:, PAIR:])
        d_value = jnp.where(lane < STRETCH, 0.0, pltpu.roll(d_value, STRETCH, 1))
        top, bottom = phi[:STRETCH].astype(F32), phi[STRETCH:].astype(F32)
        a, b = d_phi[:STRETCH], d_phi[STRETCH:]
        d_mixed = top * (a - jnp.sum(top * a, axis=0, keepdims=True)) - bottom * (
            b - jnp.sum(bottom * b, axis=0, keepdims=True)
        )
        d_mixed = d_mixed.astype(BF)
        d_key = dotg(d_mixed, wk_ref[k], 0, 0)
        map_ref[k] += dotg(kv, d_mixed, 0, 1)
        total = dkv_ref[rows, k * PAIR : (k + 1) * PAIR] + d_value + d_key
        returned = back_ref[:, k * PAIR : (k + 1) * PAIR].astype(F32) * last
        total = total + jnp.concatenate([jnp.zeros_like(returned), returned], axis=0)
        out_ref[k * PAIR : (k + 1) * PAIR, :] = jnp.transpose(total).astype(BF)
        state = ds_ref[0, k]
        rest = state[EXT:] + one_c * next_one
        carry[k, 1] = rest
        carry[k, 0] = state[:EXT] + one_b * rest


def whole(shape):
    return pl.BlockSpec(shape, lambda i, *_: (0,) * len(shape))


def sds(shape, kind):
    return jax.ShapeDtypeStruct(shape, kind)


def params():
    return pltpu.CompilerParams(
        dimension_semantics=("arbitrary",), vmem_limit_bytes=VMEM_LIMIT
    )


def run_states(table, kv, maps):
    rows, width = kv.shape
    heads, pairs = width // PAIR, rows // PAIR
    return pl.pallas_call(
        states_kernel,
        grid_spec=pltpu.PrefetchScalarGridSpec(
            num_scalar_prefetch=1,
            grid=(pairs,),
            in_specs=[pl.BlockSpec((PAIR, width), lambda i, *_: (i, 0)), whole(maps.shape)],
            out_specs=[
                pl.BlockSpec((width, PAIR), lambda i, *_: (0, i)),
                pl.BlockSpec((PAIR, width), lambda i, *_: (i, 0)),
                pl.BlockSpec((1, heads, 2 * EXT, PAIR), lambda i, *_: (i, 0, 0, 0)),
                whole((heads, 2, EXT, PAIR)),
            ],
            scratch_shapes=[pltpu.VMEM((heads, EXT, PAIR), F32)],
        ),
        out_shape=[
            sds((width, rows), BF),
            sds((rows, width), BF),
            sds((pairs, heads, 2 * EXT, PAIR), F32),
            sds((heads, 2, EXT, PAIR), BF),
        ],
        compiler_params=params(),
        name="states",
    )(table, kv, maps)


def run_forward(table, q, kv, ve, maps, states, entering):
    q_width, rows = q.shape
    width = kv.shape[1]
    heads, pairs = width // PAIR, rows // PAIR
    per = q_width // STRETCH // heads
    scale = STRETCH ** (-0.5) * math.log2(math.e)
    step = lambda *shape: pl.BlockSpec((1,) + shape, lambda i, *_: (i,) + (0,) * len(shape))
    return pl.pallas_call(
        functools.partial(forward_kernel, per, scale),
        grid_spec=pltpu.PrefetchScalarGridSpec(
            num_scalar_prefetch=1,
            grid=(pairs,),
            in_specs=[
                pl.BlockSpec((q_width, PAIR), lambda i, *_: (0, i)),
                whole(kv.shape),
                whole(ve.shape),
                whole(maps.shape),
                step(heads, 2 * EXT, PAIR),
                whole(entering.shape),
            ],
            out_specs=[
                pl.BlockSpec((q_width, PAIR), lambda i, *_: (0, i)),
                step(heads, WIN, per * PAIR),
                step(heads, PAIR, per * PAIR),
                step(heads, 2 * EXT, PAIR),
                step(heads * per, PAIR),
            ],
            scratch_shapes=[pltpu.VMEM((heads, 2, EXT, PAIR), F32)],
        ),
        out_shape=[
            sds((q_width, rows), BF),
            sds((pairs, heads, WIN, per * PAIR), BF),
            sds((pairs, heads, PAIR, per * PAIR), BF),
            sds((pairs, heads, 2 * EXT, PAIR), BF),
            sds((pairs, heads * per, PAIR), F32),
        ],
        compiler_params=params(),
        name="attention_forward",
    )(table, q, kv, ve, maps, states, entering)


def run_backward(table, order, q, kv, ve, maps, d_att, att, weights, phi, states, inverse):
    q_width, rows = q.shape
    width = kv.shape[1]
    heads, pairs = width // PAIR, rows // PAIR
    per = q_width // STRETCH // heads
    rev = lambda i: pairs - 1 - i
    step = lambda *shape: pl.BlockSpec((1,) + shape, lambda i, *_: (rev(i),) + (0,) * len(shape))
    column = pl.BlockSpec((q_width, PAIR), lambda i, *_: (0, rev(i)))
    return pl.pallas_call(
        functools.partial(backward_kernel, per, pairs, STRETCH ** (-0.5)),
        grid_spec=pltpu.PrefetchScalarGridSpec(
            num_scalar_prefetch=2,
            grid=(pairs,),
            in_specs=[
                column,
                whole(kv.shape),
                whole(ve.shape),
                whole(maps.shape),
                pl.BlockSpec((q_width, PAIR), lambda i, tab, order: (0, order[rev(i)])),
                column,
                step(heads, WIN, per * PAIR),
                step(heads, PAIR, per * PAIR),
                step(heads, 2 * EXT, PAIR),
                step(heads * per, PAIR),
            ],
            out_specs=[
                column,
                whole(kv.shape),
                step(heads, 2 * EXT, PAIR),
                whole((heads, 2, EXT, PAIR)),
                whole(maps.shape),
            ],
            scratch_shapes=[pltpu.VMEM((heads, EXT, PAIR), F32)],
        ),
        out_shape=[
            sds((q_width, rows), BF),
            sds(kv.shape, F32),
            sds((pairs, heads, 2 * EXT, PAIR), F32),
            sds((heads, 2, EXT, PAIR), BF),
            sds(maps.shape, F32),
        ],
        compiler_params=params(),
        name="attention_backward",
    )(table, order, q, kv, ve, maps, d_att, att, weights, phi, states, inverse)


def run_keys(table, kv, ve, maps, phi, d_kv, returned, d_states, entering):
    width, rows = phi.shape
    heads, pairs = width // PAIR, rows // PAIR
    rev = lambda i: pairs - 1 - i
    return pl.pallas_call(
        functools.partial(keys_kernel, pairs),
        grid_spec=pltpu.PrefetchScalarGridSpec(
            num_scalar_prefetch=1,
            grid=(pairs,),
            in_specs=[
                whole(kv.shape),
                whole(ve.shape),
                whole(maps.shape),
                pl.BlockSpec((width, PAIR), lambda i, *_: (0, rev(i))),
                whole(d_kv.shape),
                whole(returned.shape),
                pl.BlockSpec((1, heads, 2 * EXT, PAIR), lambda i, *_: (rev(i), 0, 0, 0)),
                whole(entering.shape),
            ],
            out_specs=[
                pl.BlockSpec((width, PAIR), lambda i, *_: (0, rev(i))),
                whole((heads, PAIR, STRETCH)),
            ],
            scratch_shapes=[pltpu.VMEM((heads, 2, EXT, PAIR), F32)],
        ),
        out_shape=[sds((width, rows), BF), sds((heads, PAIR, STRETCH), F32)],
        compiler_params=params(),
        name="attention_keys",
    )(table, kv, ve, maps, phi, d_kv, returned, d_states, entering)


def exchange(ends, starts, base, blocks, sign):
    count = lax.axis_size("seq")
    edge = base - 1 if sign > 0 else base + blocks
    near = shifted(ends, "seq", sign)
    outer = near[:, 1].astype(F32)
    inner = near[:, 0].astype(F32)
    full = ends[:, 1]
    ids = jnp.stack(
        [edge, edge - sign] + [edge - sign * (r - 1) * blocks for r in range(2, count)]
    )
    owner = owners(ids, starts)
    for r in range(2, count):
        far = shifted(full, "seq", sign * r).astype(F32)
        outer = outer + jnp.where(owner[r] == owner[0], far, 0.0)
        inner = inner + jnp.where(owner[r] == owner[1], far, 0.0)
    return inner, outer


def local(
    tokens,
    cotangent,
    lengths,
    attention_norm_gain,
    feedforward_norm_gain,
    query_weight,
    keyvalue_weight,
    output_weight,
    gate_up_weight,
    down_weight,
    adapter_width_factor,
    query_up_factor,
    keyvalue_up_factor,
    output_input_factor,
    query_feature_weight,
    key_feature_weight,
):
    batches, rows, model = tokens.shape
    n_seq, n_grp = lax.axis_size("seq"), lax.axis_size("grp")
    group_index, seq_index = lax.axis_index("grp"), lax.axis_index("seq")
    share = rows // n_grp
    blocks, pairs = rows // STRETCH, rows // PAIR
    rank = adapter_width_factor.shape[2]
    depth = query_weight.shape[0]
    q_width = query_weight.shape[1]
    kv_heads = key_feature_weight.shape[0]
    kv_width = kv_heads * PAIR
    per = query_feature_weight.shape[0] // kv_heads
    hidden_width = down_weight.shape[0]
    gain_attn = attention_norm_gain.astype(F32)
    gain_mlp = feedforward_norm_gain.astype(F32)
    base = seq_index * blocks
    width = q_width + kv_width

    kv_shard = (
        keyvalue_weight.reshape(depth, 2, kv_heads, STRETCH)
        .transpose(0, 2, 1, 3)
        .reshape(depth, kv_width)
    )
    adapter_shard = adapter_width_factor.transpose(1, 0, 2).reshape(depth, 4 * rank)
    in_weight = ring_gather(jnp.concatenate([query_weight, kv_shard, adapter_shard], axis=1))
    out_shard, gate_shard, down_shard, in_weight = lax.optimization_barrier(
        (output_weight.T, gate_up_weight.reshape(depth, -1), down_weight.T, in_weight)
    )
    out_weight = ring_gather(out_shard)
    out_weight, gate_shard, down_shard = lax.optimization_barrier(
        (out_weight, gate_shard, down_shard)
    )
    gate_weight = ring_gather(gate_shard)
    down_merged = ring_gather(down_shard)
    adapter_merged = in_weight[:, width:]
    out_factor = adapter_merged[:, 3 * rank :]

    key_up = keyvalue_up_factor.reshape(2, rank, kv_heads, 1, STRETCH)
    kv_up = (
        jnp.zeros((2, rank, kv_heads, 2, STRETCH), BF)
        .at[0, :, :, 0].set(key_up[0, :, :, 0])
        .at[1, :, :, 1].set(key_up[1, :, :, 0])
        .reshape(2 * rank, kv_width)
    )
    maps_t = query_feature_weight.transpose(0, 2, 1).reshape(kv_heads, per, STRETCH, STRETCH)
    query_maps = jnp.zeros((kv_heads, per, STRETCH, per, STRETCH), BF)
    for g in range(per):
        query_maps = query_maps.at[:, g, :, g, :].set(maps_t[:, g])
    query_maps = query_maps.reshape(kv_heads, per * STRETCH, per * STRETCH)
    key_maps = jnp.concatenate(
        [key_feature_weight.transpose(0, 2, 1), jnp.zeros((kv_heads, STRETCH, STRETCH), BF)], axis=2
    )

    def rel_rows(array, r):
        return lax.dynamic_slice_in_dim(array, (group_index ^ r) * share, share, 0)

    def rel_lanes(array, r):
        return lax.dynamic_slice_in_dim(array, (group_index ^ r) * share, share, 1)

    saved = []
    for batch in range(batches):
        x = tokens[batch].astype(F32)
        factor = lax.rsqrt(jnp.mean(x * x, axis=-1, keepdims=True) + EPS)
        normed = (x * factor * gain_attn).astype(BF)
        side = dotg(normed, in_weight[:, q_width:], 1, 0)
        mids = side[:, kv_width:].astype(BF)
        query = dotg(in_weight[:, :q_width], normed, 0, 1) + ADAPTER_SCALE * dotg(
            query_up_factor, mids[:, :rank], 0, 1
        )
        query = query.astype(BF)
        kv = side[:, :kv_width] + ADAPTER_SCALE * dotg(mids[:, rank : 3 * rank], kv_up, 1, 0)
        kv = kv.astype(BF)
        table, starts = layout(lengths[batch], base, blocks)
        phi_key, ve, states, ends = run_states(table, kv, key_maps)
        halo = shifted(
            jnp.concatenate([kv[rows - STRETCH :], ve[rows - STRETCH :]], axis=1), "seq", 1
        )
        kv = jnp.concatenate([halo[:, :kv_width], kv])
        ve = jnp.concatenate([halo[:, kv_width:], ve])
        entering = jnp.stack(exchange(ends, starts, base, blocks, 1), axis=1)
        saved.append([normed, mids, query, kv, ve, table, starts, phi_key, states, entering])

    attended = []
    for batch in range(batches):
        normed, mids, query, kv, ve, table, starts, phi_key, states, entering = saved[batch]
        att, weights, phi, sums, inverse = run_forward(
            table, query, kv, ve, query_maps, states, entering
        )
        out_mid = dotg(output_input_factor, att, 0, 0)
        att_ext = jnp.concatenate([att, (ADAPTER_SCALE * out_mid).astype(BF)], axis=0)
        out_ext = jnp.concatenate([out_weight, out_factor], axis=1)
        branch = group_scatter(
            lambda r: dotg(rel_lanes(att_ext, r), out_ext, 0, 1).astype(BF)
        )
        resid = rel_rows(tokens[batch], 0).astype(F32) + branch
        mlp_factor = lax.rsqrt(jnp.mean(resid * resid, axis=-1, keepdims=True) + EPS)
        mlp_in = group_gather((resid * mlp_factor * gain_mlp).astype(BF))
        attended.append([att, weights, phi, sums, inverse, out_mid, resid, mlp_factor, mlp_in])

    block_rows, d_resids, d_branches = [], [], []
    for batch in range(batches):
        resid, mlp_factor, mlp_in = attended[batch][6:]
        mlp_in = jnp.concatenate(mlp_in)
        upstream = jnp.concatenate([rel_rows(cotangent[batch], r) for r in range(n_grp)])
        gate_up = dotg(mlp_in, gate_weight, 1, 0)
        gate, up = gate_up[:, :hidden_width], gate_up[:, hidden_width:]
        sig = 1.0 / (1.0 + jnp.exp(-gate))
        hidden = (gate * sig * up).astype(BF)
        d_hidden = dotg(upstream, down_merged, 1, 0)
        d_gate = d_hidden * up * sig * (1.0 + gate * (1.0 - sig))
        d_up = d_hidden * gate * sig
        d_gate_up = jnp.concatenate([d_gate.astype(BF), d_up.astype(BF)], axis=1)
        d_in = dotg(d_gate_up, gate_weight, 1, 1).astype(BF)
        d_in = group_scatter(lambda r: d_in[r * share : (r + 1) * share])
        mlp_out = dotg(hidden, down_merged, 1, 1).astype(BF)
        mlp_out = group_scatter(lambda r: mlp_out[r * share : (r + 1) * share])
        block_rows.append((resid + mlp_out).astype(BF))
        e = gain_mlp * d_in
        d_resid = (
            upstream[:share].astype(F32)
            + mlp_factor * e
            - resid * mlp_factor**3 * jnp.mean(resid * e, axis=-1, keepdims=True)
        )
        d_resids.append(d_resid)
        d_branches.append(group_gather(d_resid.astype(BF)))

    order_index = jnp.arange(pairs, dtype=jnp.int32)
    per_share = share // PAIR
    order = ((order_index // per_share) ^ group_index) * per_share + order_index % per_share
    gone = []
    for batch in range(batches):
        normed, mids, query, kv, ve, table, starts, phi_key, states, entering = saved[batch]
        att, weights, phi, sums, inverse, out_mid = attended[batch][:6]
        d_branch = jnp.concatenate(d_branches[batch])
        back_out = ADAPTER_SCALE * dotg(out_factor, d_branch, 0, 1)
        d_att = dotg(out_weight, d_branch, 0, 1) + dotg(
            output_input_factor, back_out.astype(BF), 1, 0
        )
        dq, d_kv, d_states, heads_sum, map_grad = run_backward(
            table, order, query, kv, ve, query_maps, d_att, att, weights, phi, sums, inverse
        )
        returned = shifted(d_kv[:STRETCH].astype(BF), "seq", -1)
        leaving = exchange(heads_sum, starts, base, blocks, -1)
        leaving = jnp.stack([leaving[1], leaving[0]], axis=1)
        gone.append([dq, d_kv, d_states, map_grad, returned, leaving, d_branch, back_out])

    input_grads = []
    wide = jnp.zeros((4 * rank, model), F32)
    up_grad = jnp.zeros((3 * rank, width), F32)
    out_in_grad = jnp.zeros((q_width, rank), F32)
    query_map_grad = jnp.zeros(query_maps.shape, F32)
    key_map_grad = jnp.zeros((kv_heads, STRETCH, STRETCH), F32)
    for batch in range(batches):
        normed, mids, query, kv, ve, table, starts, phi_key, states, entering = saved[batch]
        att, _, _, _, _, out_mid, resid, mlp_factor, _ = attended[batch]
        dq, d_kv, d_states, map_grad, returned, leaving, d_branch, back_out = gone[batch]
        d_kv_low, key_grad = run_keys(
            table, kv, ve, key_maps, phi_key, d_kv, returned, d_states, leaving
        )
        back_in = jnp.concatenate(
            [dotg(query_up_factor, dq, 1, 0), dotg(kv_up, d_kv_low, 1, 0)], axis=0
        )
        back_in = (ADAPTER_SCALE * back_in).astype(BF)
        stacked = jnp.concatenate([dq, d_kv_low, back_in], axis=0)
        d_normed = group_scatter(
            lambda r: dotg(
                rel_lanes(stacked, r), in_weight[:, : width + 3 * rank], 0, 1
            ).astype(BF)
        )
        x = rel_rows(tokens[batch], 0).astype(F32)
        factor = lax.rsqrt(jnp.mean(x * x, axis=-1, keepdims=True) + EPS)
        e = gain_attn * d_normed
        input_grads.append(
            d_resids[batch]
            + factor * e
            - x * factor**3 * jnp.mean(x * e, axis=-1, keepdims=True)
        )
        order_rel = [rel_lanes(out_mid, r) for r in range(n_grp)]
        out_mid_rel = jnp.concatenate(order_rel, axis=1).astype(BF)
        att_rel = jnp.concatenate([rel_lanes(att, r) for r in range(n_grp)], axis=1)
        wide = wide + jnp.concatenate(
            [dotg(back_in, normed, 1, 0), ADAPTER_SCALE * dotg(out_mid_rel, d_branch, 1, 0)]
        )
        up_grad = up_grad + ADAPTER_SCALE * dotg(
            mids[:, : 3 * rank], jnp.concatenate([dq, d_kv_low]), 0, 1
        )
        out_in_grad = out_in_grad + dotg(att_rel, back_out.astype(BF), 1, 1)
        query_map_grad = query_map_grad + map_grad
        key_map_grad = key_map_grad + key_grad[:, :STRETCH]

    kv_grad = up_grad[rank:, q_width:].reshape(2, rank, kv_heads, 2, STRETCH)
    kv_grad = jnp.stack([kv_grad[0, :, :, 0], kv_grad[1, :, :, 1]])
    map_blocks = query_map_grad.reshape(kv_heads, per, STRETCH, per, STRETCH)
    query_map_grad = jnp.stack([map_blocks[:, g, :, g] for g in range(per)], axis=1)
    pieces = [
        (up_grad[:rank, :q_width], query_up_factor.shape),
        (kv_grad, keyvalue_up_factor.shape),
        (out_in_grad, output_input_factor.shape),
        (query_map_grad, query_feature_weight.shape),
        (key_map_grad, key_feature_weight.shape),
    ]
    wide_share, rest = small_sums(
        wide, jnp.concatenate([piece.reshape(-1) for piece, _ in pieces])
    )
    wide_share = wide_share.reshape(4, rank, -1).transpose(0, 2, 1)
    outs, first = [], 0
    for piece, shape in pieces:
        outs.append(rest[first : first + piece.size].reshape(shape))
        first += piece.size
    return (jnp.stack(block_rows), jnp.stack(input_grads), wide_share, *outs)


def solution(mesh):
    return jax.shard_map(
        local,
        mesh=mesh,
        in_specs=(
            P(None, "seq", None),
            P(None, "seq", None),
            P(),
            P(),
            P(),
            P("seq", "grp"),
            P("seq", None, "grp"),
            P("grp", "seq"),
            P("seq", None, "grp"),
            P("grp", "seq"),
            P(None, "seq", None),
            P(None, "grp"),
            P(None, None, "grp"),
            P("grp", None),
            P("grp", None, None),
            P("grp", None, None),
        ),
        out_specs=(
            P(None, ("seq", "grp"), None),
            P(None, ("seq", "grp"), None),
            P(None, ("seq", "grp"), None),
            P(None, "grp"),
            P(None, None, "grp"),
            P("grp", None),
            P("grp", None, None),
            P("grp", None, None),
        ),
        check_vma=False,
    )
```

```python
import functools
import math

import jax
import jax.numpy as jnp
from jax import lax
from jax.experimental import pallas as pl
from jax.experimental.pallas import tpu as pltpu
from jax.sharding import PartitionSpec as P

STRETCH = 64
PAIR = 2 * STRETCH
WIN = 3 * STRETCH
EXT = 80
EPS = 1e-05
ADAPTER_SCALE = 2.0
BF = jnp.bfloat16
F32 = jnp.float32
VMEM_LIMIT = 58 * 1024 * 1024
CHUNK = 256
ROW_TILE = 512


def dotg(left, right, lc, rc):
    return lax.dot_general(left, right, (((lc,), (rc,)), ((), ())), preferred_element_type=F32)


def ring_order(count):
    if count % 8:
        return list(range(count))
    deep, wide = 4, count // 4
    path = [z * wide for z in range(deep)]
    for step, z in enumerate(reversed(range(deep))):
        ys = list(range(1, wide))
        path += [z * wide + y for y in (ys if step % 2 == 0 else ys[::-1])]
    return path


def ring_offsets(count):
    out = [0]
    for distance in range(1, (count + 1) // 2):
        out += [-distance, distance]
    return out + [count // 2]


def ring_sources(count):
    order = ring_order(count)
    return [[order[(order.index(s) + o) % count] for o in ring_offsets(count)] for s in range(count)]


def ring_cut(rows):
    return (rows // 2 + 15) // 16 * 16


def ring_layout(count, rows):
    cut = ring_cut(rows)
    return [(q, 0, rows) for q in range(count - 1)] + [
        (count - 1, 0, cut), (count - 1, cut, rows - cut),
    ]


def pieces_of(width):
    quarter = width // 4
    return [(0, quarter), (quarter, quarter), (2 * quarter, 2 * quarter)]


class Ring:
    def __init__(self, shard):
        self.count = lax.axis_size("seq")
        self.order = ring_order(self.count)
        self.parts = [shard]
        self.ahead = self.back = shard
        self.done = 0

    def move(self, value, step):
        pairs = [(self.order[i], self.order[(i + step) % self.count]) for i in range(self.count)]
        return lax.ppermute(value, "seq", pairs)

    def hop(self, *after):
        self.ahead, self.back, *_ = lax.optimization_barrier((self.ahead, self.back, *after))
        self.done += 1
        if self.done < (self.count + 1) // 2:
            self.ahead, self.back = self.move(self.ahead, 1), self.move(self.back, -1)
            self.parts += [self.ahead, self.back]
        else:
            cut = ring_cut(self.ahead.shape[0])
            self.parts += [self.move(self.ahead[:cut], 1), self.move(self.back[cut:], -1)]

    def hops(self):
        return (self.count + 1) // 2

    def tie(self, *values):
        self.ahead, self.back, *values = lax.optimization_barrier((self.ahead, self.back, *values))
        return values

    def finish(self):
        while self.done < self.hops():
            self.hop()
        return self


def after(value, *others):
    return lax.optimization_barrier((value, *others))[0]


def flip(value, axis, bit):
    count = lax.axis_size(axis)
    return lax.ppermute(value, axis, [(i, i ^ bit) for i in range(count)])


def shifted(value, axis, steps):
    count = lax.axis_size(axis)
    first, last = max(0, -steps), min(count, count - steps)
    return lax.ppermute(value, axis, [(i, i + steps) for i in range(first, last)])


def group_gather(share):
    count = lax.axis_size("grp")
    out = []
    for far in range(0, count, 2):
        mine = share if far == 0 else flip(share, "grp", far)
        out += [mine, flip(mine, "grp", 1)]
    return out


def far_gather(share):
    return [share] + [flip(share, "grp", far) for far in range(2, lax.axis_size("grp"), 2)]


def near_gather(fars):
    out = []
    for far in fars:
        out += [far, flip(far, "grp", 1)]
    return out


def group_exchange(blocks):
    return [blocks[0]] + [flip(blocks[r], "grp", r) for r in range(1, len(blocks))]


def scatter_start(blocks):
    count = len(blocks)
    fars = []
    for far in range(2, count, 2):
        there = flip(blocks[far + 1], "grp", 1)
        fars.append((blocks[far].astype(F32) + there.astype(F32)).astype(BF))
    return fars, [blocks[0], flip(blocks[1], "grp", 1)]


def scatter_end(fars, nears):
    return nears + [flip(far, "grp", 2 * (i + 1)) for i, far in enumerate(fars)]


def exchange(ends, halo, sign):
    count = lax.axis_size("seq")
    wide = max(1, count // 4)
    here = [ends] + [flip(ends, "seq", j) for j in range(1, wide)]
    near = jnp.stack(here)
    out = [near]
    for r in range(1, count // wide):
        out.append(shifted(near if r == 1 else near[:, :, :, 1:], "seq", sign * r * wide))
    return out, shifted(halo, "seq", sign)


class Slots:
    def __init__(self, lens, batch):
        self.starts, self.ends, at = [], [], 0
        for i in range(lens.shape[1]):
            length = lens[batch, i]
            self.starts.append(at)
            self.ends.append(at * STRETCH + length)
            at = at + ((length + STRETCH - 1) >> 6)

    def owner(self, c):
        total = -1
        for start in self.starts:
            total = total + jnp.where(start <= c, 1, 0)
        return total

    def valid(self, c):
        end = 0
        for start, stop in zip(self.starts, self.ends):
            end = jnp.where(start <= c, stop, end)
        return jnp.clip(end - c * STRETCH, 0, STRETCH)

    def same(self, a, b):
        return jnp.where(self.owner(a) == self.owner(b), 1, 0)

    def weight(self, a, b):
        return self.same(a, b).astype(F32)


def entering(slots, info, arrays, blocks, wide, count, sign, place, near_k):
    seq = info[2]
    base = info[0]
    z, y = seq // wide, seq % wide
    edge = base - 1 if sign > 0 else base + blocks
    inner = outer = jnp.zeros((EXT, PAIR), F32)
    for r in range(count // wide):
        for j in range(wide):
            if r == 0 and j == 0:
                continue
            source = (z - sign * r) * wide + (y ^ j)
            ahead = (seq - source) * sign > 0
            end = source * blocks + (blocks - 1 if sign > 0 else 0)
            direct = (seq - source) * sign == 1
            full = arrays[r][j, place, near_k, arrays[r].shape[3] - 1].astype(F32)
            a = jnp.where(ahead & (slots.owner(end) == slots.owner(edge)), 1.0, 0.0)
            outer = outer + a * full
            b = jnp.where(
                ahead & (~direct) & (slots.owner(end) == slots.owner(edge - sign)), 1.0, 0.0
            )
            inner = inner + b * full
            if arrays[r].shape[3] == 2:
                part = arrays[r][j, place, near_k, 0].astype(F32)
                inner = inner + jnp.where(direct, 1.0, 0.0) * part
    return inner, outer


def half_mask(shape):
    return (lax.broadcasted_iota(jnp.int32, shape, 1) & (PAIR - 1)) < STRETCH


def feature_softmax(u):
    top = jnp.exp(u - jnp.max(u, axis=0, keepdims=True))
    bottom = jnp.exp(jnp.min(u, axis=0, keepdims=True) - u)
    top = top * (1.0 / jnp.sum(top, axis=0, keepdims=True))
    bottom = bottom * (1.0 / jnp.sum(bottom, axis=0, keepdims=True))
    return jnp.concatenate([top, bottom], axis=0)


def feature_back(phi, d_phi):
    top, bottom = phi[:STRETCH].astype(F32), phi[STRETCH:].astype(F32)
    a, b = d_phi[:STRETCH], d_phi[STRETCH:]
    return top * (a - jnp.sum(top * a, axis=0, keepdims=True)) - bottom * (
        b - jnp.sum(bottom * b, axis=0, keepdims=True)
    )


def assemble_kernel(parts_of, width, splits, info, *refs):
    ins, outs = refs[: len(parts_of)], refs[len(parts_of) :]
    for (q, first, rows), ref in zip(parts_of, ins):
        column = pl.ds(pl.multiple_of(info[3 + q] * width, width), width)
        at = 0
        for out, size in zip(outs, splits):
            low, high = max(at, first), min(at + size, first + rows)
            if low < high:
                out[low - at : high - at, column] = ref[low - first : high - first, :]
            at += size


def project_kernel(
    batch, q_width, info, lens, normed_ref, w_ref, up_ref, kv_up_ref, wk_ref,
    q_ref, kv_ref, ve_ref, mid_ref, phi_ref, st_ref, ends_ref, halo_ref, carry,
):
    step = pl.program_id(0)
    rows = normed_ref.shape[0]
    width = kv_ref.shape[1]
    heads = width // PAIR

    @pl.when(step == 0)
    def _():
        carry[...] = jnp.zeros_like(carry)

    normed = normed_ref[...]
    mixed = dotg(w_ref[: q_width + 32], normed, 1, 1)
    mids = mixed[q_width:].astype(BF)
    mid_ref[...] = mids
    query = mixed[:q_width] + ADAPTER_SCALE * dotg(up_ref[...], mids, 1, 0)
    q_ref[...] = query.astype(BF)
    kv_all = dotg(normed, w_ref[q_width + 32 :], 1, 1) + ADAPTER_SCALE * dotg(
        mids, kv_up_ref[...], 0, 0
    )
    kv_all = kv_all.astype(BF)
    kv_ref[...] = kv_all
    halo_ref[:, :width] = kv_all[rows - STRETCH :]

    slots = Slots(lens, batch)
    base = info[0]
    lane = lax.broadcasted_iota(jnp.int32, (1, PAIR), 1)
    low = lane < STRETCH
    inside = lane & (STRETCH - 1)
    wide = lax.broadcasted_iota(jnp.int32, (PAIR, PAIR), 1)
    for sub in range(rows // PAIR):
        block = base + 2 * (step * (rows // PAIR) + sub)
        one_a, one_b = slots.weight(block - 1, block), slots.weight(block, block + 1)
        valid = inside < jnp.where(low, slots.valid(block), slots.valid(block + 1))
        valid = jnp.where(valid, 1.0, 0.0)
        valid_low = jnp.where(low, valid, 0.0)
        valid_high = valid - valid_low
        at = sub * PAIR
        for k in range(heads):
            kv = kv_all[at : at + PAIR, k * PAIR : (k + 1) * PAIR]
            moved = pltpu.roll(kv.astype(F32), STRETCH, 1)
            ve = jnp.where(
                wide < STRETCH, moved, jnp.where(wide < STRETCH + 2, 1.0, 0.0)
            ).astype(BF)
            ve_ref[at : at + PAIR, k * PAIR : (k + 1) * PAIR] = ve
            if sub == rows // PAIR - 1:
                halo_ref[:, width + k * PAIR : width + (k + 1) * PAIR] = ve[STRETCH:]
            phi = feature_softmax(dotg(wk_ref[k], kv, 1, 1))
            phi_ref[k * PAIR : (k + 1) * PAIR, at : at + PAIR] = (phi * valid).astype(BF)
            first = dotg(ve, (phi * valid_low).astype(BF), 0, 1)[:EXT]
            second = dotg(ve, (phi * valid_high).astype(BF), 0, 1)[:EXT]
            st_ref[sub, k, :EXT] = first
            st_ref[sub, k, EXT:] = second
            mid = carry[k] * one_a + first
            tail = mid * one_b + second
            carry[k] = tail
            ends_ref[k, 0] = mid.astype(BF)
            ends_ref[k, 1] = tail.astype(BF)


def window_mask(slots, block):
    lane = lax.broadcasted_iota(jnp.int32, (1, PAIR), 1)
    low = lane < STRETCH
    before = slots.valid(block - 1) * slots.same(block - 1, block)
    own = slots.valid(block)
    limits = [
        jnp.where(low, before, 0),
        jnp.where(low, jnp.minimum(lane + 1, own), own * slots.same(block, block + 1)),
        jnp.where(low, 0, jnp.minimum(lane - STRETCH + 1, slots.valid(block + 1))),
    ]
    row = lax.broadcasted_iota(jnp.int32, (STRETCH, PAIR), 0)
    return jnp.concatenate([jnp.where(row < limit, 1.0, 0.0) for limit in limits], axis=0)


def fill_window(batch, kv_ref, ve_ref, halo_ref, kv_all, ve_all):
    width = kv_ref.shape[1]
    kv_all[:STRETCH] = halo_ref[batch, :, :width]
    ve_all[:STRETCH] = halo_ref[batch, :, width:]
    kv_all[STRETCH:] = kv_ref[...]
    ve_all[STRETCH:] = ve_ref[...]


def forward_kernel(
    batch, per, blocks, wide, count, n_far, scale, info, lens, q_ref, kv_ref, ve_ref, halo_ref,
    wq_ref, oin_ref, st_ref, *refs,
):
    fars = refs[:n_far]
    att_ref, w_ref, phi_ref, s_ref, r_ref, carry, kv_all, ve_all = refs[n_far:]
    step = pl.program_id(0)
    heads = kv_ref.shape[1] // PAIR
    slots = Slots(lens, batch)
    block = info[0] + 2 * step

    @pl.when(step == 0)
    def _():
        fill_window(batch, kv_ref, ve_ref, halo_ref, kv_all, ve_all)
        for k in range(heads):
            inner, outer = entering(slots, info, fars, blocks, wide, count, 1, batch, k)
            carry[k, 0] = inner
            carry[k, 1] = outer

    one_a, one_b = slots.weight(block - 1, block), slots.weight(block, block + 1)
    two_a, two_b = slots.weight(block - 2, block), slots.weight(block - 1, block + 1)
    mask = window_mask(slots, block)
    mask = jnp.concatenate([mask] * per, axis=1)
    lanes = per * PAIR
    low = half_mask((EXT, lanes))
    rows = pl.ds(pl.multiple_of(step * PAIR, PAIR), WIN)
    out_mid = jnp.zeros((16, PAIR), F32)
    for k in range(heads):
        kv = kv_all[rows, k * PAIR : (k + 1) * PAIR]
        ve = ve_all[rows, k * PAIR : (k + 1) * PAIR]
        base = k * per * STRETCH
        stacked = q_ref[base : base + per * STRETCH, :]
        q = jnp.concatenate(
            [stacked[g * STRETCH : (g + 1) * STRETCH] for g in range(per)], axis=1
        )
        q = jnp.concatenate([q, jnp.zeros_like(q)], axis=0)
        scores = dotg(kv, q, 1, 0)
        weights = (jnp.exp2(scores * scale) * mask).astype(BF)
        w_ref[0, k] = weights
        mixed = dotg(wq_ref[k], stacked, 1, 0)
        phi = jnp.concatenate(
            [
                feature_softmax(mixed[g * STRETCH : (g + 1) * STRETCH]).astype(BF)
                for g in range(per)
            ],
            axis=1,
        )
        phi_ref[0, k] = phi
        older, old = carry[k, 0], carry[k, 1]
        states = jnp.concatenate([older * two_a, old * two_b], axis=0).astype(BF)
        s_ref[0, k] = states
        linear = dotg(states, phi, 1, 0)
        total = dotg(ve, weights, 0, 0)[:EXT] + jnp.where(low, linear[:EXT], linear[EXT:])
        inverse = 1.0 / total[STRETCH : STRETCH + 1]
        att = (total[:STRETCH] * inverse).astype(BF)
        att = jnp.concatenate([att[:, g * PAIR : (g + 1) * PAIR] for g in range(per)], axis=0)
        att_ref[0, base : base + per * STRETCH, :] = att
        out_mid = out_mid + dotg(oin_ref[base : base + per * STRETCH, :], att, 0, 0)
        for g in range(per):
            r_ref[0, k * per + g : k * per + g + 1, :] = inverse[:, g * PAIR : (g + 1) * PAIR]
        current = old * one_a + st_ref[0, k, :EXT]
        carry[k, 0] = current
        carry[k, 1] = current * one_b + st_ref[0, k, EXT:]
    att_ref[0, heads * per * STRETCH :, :] = (ADAPTER_SCALE * out_mid).astype(BF)


def residual_kernel(n_grp, info, x_ref, gain_ref, *refs):
    atts, weights = refs[:n_grp], refs[n_grp : 2 * n_grp]
    resid_ref, low_ref, mid_ref, buffer, sems = refs[2 * n_grp :]
    copies = [
        pltpu.make_async_copy(weights[r], buffer.at[r], sems.at[r]) for r in range(n_grp)
    ]
    for copy in copies:
        copy.start()
    q_width = buffer.shape[1] - 16
    resid_ref[...] = x_ref[0].astype(F32)
    mid = jnp.zeros(mid_ref.shape, F32)
    for r in range(n_grp):
        copies[r].wait()
        att = atts[r][0] if len(atts[r].shape) == 3 else atts[r][...]
        mid = mid + att[q_width:].astype(F32)
        resid_ref[...] += dotg(att, buffer[r], 0, 0)
    mid_ref[...] = mid.astype(BF)
    resid = resid_ref[...]
    factor = lax.rsqrt(jnp.mean(resid * resid, axis=1, keepdims=True) + EPS)
    low_ref[...] = (resid * factor * gain_ref[...]).astype(BF)


def branch_kernel(n_grp, n_sum, info, dy_ref, resid_ref, gain_ref, mid_ref, *refs):
    summands, refs = refs[:n_sum], refs[n_sum:]
    weights, refs = refs[:n_grp], refs[n_grp:]
    d_resid_ref, wide_ref, refs = refs[0], refs[1], refs[2:]
    outs, (buffer, sems) = refs[:n_grp], refs[n_grp:]
    copies = [
        pltpu.make_async_copy(weights[r], buffer.at[r], sems.at[r]) for r in range(n_grp)
    ]
    for copy in copies:
        copy.start()
    d_in = summands[0][...].astype(F32)
    for summand in summands[1:]:
        d_in = d_in + summand[...].astype(F32)
    resid = resid_ref[...]
    factor = lax.rsqrt(jnp.mean(resid * resid, axis=1, keepdims=True) + EPS)
    e = gain_ref[...] * d_in
    slope = factor * factor * factor * jnp.mean(resid * e, axis=1, keepdims=True)
    d_resid = dy_ref[0].astype(F32) + factor * e - resid * slope
    d_resid_ref[...] = d_resid
    low = d_resid.astype(BF)
    wide_ref[...] = dotg(mid_ref[...], low, 1, 0)
    for r in range(n_grp):
        copies[r].wait()
        outs[r][...] = dotg(buffer[r], low, 1, 1).astype(BF)


def tokens_kernel(n_grp, info, x_ref, gain_ref, d_resid_ref, *refs):
    dqs, rests, weights = refs[:n_grp], refs[n_grp : 2 * n_grp], refs[2 * n_grp : 3 * n_grp]
    out_ref, buffer, total, sems = refs[3 * n_grp :][-4:]
    copies = [
        pltpu.make_async_copy(weights[r], buffer.at[r], sems.at[r]) for r in range(n_grp)
    ]
    for copy in copies:
        copy.start()
    for r in range(n_grp):
        copies[r].wait()
        d_q = dqs[r][0] if len(dqs[r].shape) == 3 else dqs[r][...]
        rest = rests[r][0] if len(rests[r].shape) == 3 else rests[r][...]
        part = dotg(jnp.concatenate([d_q, rest], axis=0), buffer[r], 0, 0)
        if r:
            total[...] += part
        else:
            total[...] = part
    x = x_ref[0].astype(F32)
    factor = lax.rsqrt(jnp.mean(x * x, axis=1, keepdims=True) + EPS)
    e = gain_ref[...] * total[...]
    slope = factor * factor * factor * jnp.mean(x * e, axis=1, keepdims=True)
    out_ref[0] = d_resid_ref[...] + factor * e - x * slope


def mlp_kernel(
    batch, n_grp, layout, sizes, first_half, info, *refs,
):
    n_parts = len(layout)
    xs, refs = refs[:n_grp], refs[n_grp:]
    dy_hbm, refs = refs[0], refs[1:]
    part_sets = []
    for _ in sizes:
        part_sets.append(refs[:n_parts])
        refs = refs[n_parts:]
    n_prev = 0 if first_half else 2
    prevs, refs = refs[:n_prev], refs[n_prev:]
    n_out = 2 if first_half else 2 * n_grp
    outs, refs = refs[:n_out], refs[n_out:]
    x, dy, w, acc_out, acc_in, sem, wsem = refs[:7]
    j, n = pl.program_id(0), pl.num_programs(0)
    slot = j % 2
    share = xs[0].shape[0]
    rows_all = x.shape[0]
    depth = layout[0][2]

    def loads(jj, s, which):
        copies = []
        first_step = sum(sizes[:which]) // CHUNK
        for (q, first, rows), part in zip(layout, part_sets[which]):
            to = pl.ds(pl.multiple_of(info[3 + q] * depth + first, 16), rows)
            for kind in range(3):
                column = pl.multiple_of(kind * sizes[which] + (jj - first_step) * CHUNK, CHUNK)
                copies.append(
                    pltpu.make_async_copy(
                        part.at[:, pl.ds(column, CHUNK)],
                        w.at[s, to, pl.ds(kind * CHUNK, CHUNK)],
                        wsem.at[s],
                    )
                )
        return copies

    def start_loads(jj, s):
        for which in range(len(sizes)):
            low, high = sum(sizes[:which]) // CHUNK, sum(sizes[: which + 1]) // CHUNK

            @pl.when((jj >= low) & (jj < high))
            def _(which=which):
                for copy in loads(jj, s, which):
                    copy.start()

    def inputs():
        copies = []
        for r in range(n_grp):
            rows = pl.ds(r * share, share)
            copies.append(pltpu.make_async_copy(xs[r], x.at[rows], sem.at[0]))
            there = pl.ds(pl.multiple_of((info[1] ^ r) * share, share), share)
            copies.append(pltpu.make_async_copy(dy_hbm.at[batch, there], dy.at[rows], sem.at[0]))
        return copies

    def earlier():
        return [
            pltpu.make_async_copy(prev, refs[7 + i], sem.at[1]) for i, prev in enumerate(prevs)
        ]

    @pl.when(j == 0)
    def _():
        for copy in inputs() + earlier():
            copy.start()
        start_loads(j, 0)
        for copy in inputs():
            copy.wait()

    @pl.when(j + 1 < n)
    def _():
        start_loads(j + 1, 1 - slot)

    for copy in loads(0, slot, 0):
        copy.wait()
    gate_up_w = w.at[slot, :, pl.ds(0, 2 * CHUNK)]
    down_w = w.at[slot, :, pl.ds(2 * CHUNK, CHUNK)]

    def body(i, start):
        rows = pl.ds(pl.multiple_of(i * ROW_TILE, ROW_TILE), ROW_TILE)
        gate_up = dotg(x[rows, :], gate_up_w[...], 1, 0)
        d_hidden = dotg(dy[rows, :], down_w[...], 1, 0)
        gate, up = gate_up[:, :CHUNK], gate_up[:, CHUNK:]
        sig = 1.0 / (1.0 + jnp.exp(-gate))
        act = gate * sig
        hidden = (act * up).astype(BF)
        d_gate = (d_hidden * up * (sig + act * (1.0 - sig))).astype(BF)
        d_up = (d_hidden * act).astype(BF)
        out = dotg(hidden, down_w[...], 1, 1)
        d_in = dotg(jnp.concatenate([d_gate, d_up], axis=1), gate_up_w[...], 1, 1)
        if start:
            acc_out[rows, :] = out
            acc_in[rows, :] = d_in
        else:
            acc_out[rows, :] += out
            acc_in[rows, :] += d_in
        return 0

    tiles = rows_all // ROW_TILE

    @pl.when(j == 0)
    def _():
        lax.fori_loop(0, tiles, lambda i, c: body(i, True), 0)

    @pl.when(j > 0)
    def _():
        lax.fori_loop(0, tiles, lambda i, c: body(i, False), 0)

    @pl.when(j == n - 1)
    def _():
        if first_half:
            x[...] = acc_in[...].astype(BF)
            dy[...] = acc_out[...].astype(BF)
            copies = [
                pltpu.make_async_copy(x, outs[0], sem.at[0]),
                pltpu.make_async_copy(dy, outs[1], sem.at[0]),
            ]
        else:
            for copy in earlier():
                copy.wait()
            x[...] = (acc_in[...] + refs[7][...].astype(F32)).astype(BF)
            dy[...] = (acc_out[...] + refs[8][...].astype(F32)).astype(BF)
            copies = []
            for r in range(n_grp):
                rows = pl.ds(r * share, share)
                copies.append(pltpu.make_async_copy(x.at[rows], outs[r], sem.at[0]))
                copies.append(pltpu.make_async_copy(dy.at[rows], outs[n_grp + r], sem.at[0]))
        for copy in copies:
            copy.start()
        for copy in copies:
            copy.wait()


def backward_kernel(
    batch, per, pairs, n_grp, has_prev, scale, info, lens, q_ref, kv_ref, ve_ref, halo_ref, wq_ref,
    oin_ref, att_ref, w_ref, phi_ref, s_ref, r_ref, *refs,
):
    blocks_in, refs = refs[:n_grp], refs[n_grp:]
    prevs, refs = (refs[:1], refs[1:]) if has_prev else (None, refs)
    (
        dq_ref, dkv_ref, ds_ref, ends_ref, back_ref, map_ref, carry, kv_all, ve_all, d_outs, sem,
    ) = refs
    step = pl.program_id(0)
    pair = pairs - 1 - step
    heads = kv_ref.shape[1] // PAIR
    slots = Slots(lens, batch)
    block = info[0] + 2 * pair
    q_width = q_ref.shape[0]
    per_block = blocks_in[0].shape[1] // PAIR

    @pl.when(step == 0)
    def _():
        copies = []
        for r in range(n_grp):
            for i in range(per_block):
                copies.append(
                    pltpu.make_async_copy(
                        blocks_in[r].at[:, pl.ds(i * PAIR, PAIR)],
                        d_outs.at[(info[1] ^ r) * per_block + i],
                        sem,
                    )
                )
        for copy in copies:
            copy.start()
        fill_window(batch, kv_ref, ve_ref, halo_ref, kv_all, ve_all)
        carry[...] = jnp.zeros_like(carry)
        dkv_ref[...] = jnp.zeros_like(dkv_ref)
        map_ref[...] = prevs[0][...] if has_prev else jnp.zeros_like(map_ref)
        for copy in copies:
            copy.wait()
    one_b = slots.weight(block, block + 1)
    one_c = slots.weight(block + 1, block + 2)
    lanes = per * PAIR
    low = half_mask((EXT, lanes))
    rows = pl.ds(pl.multiple_of(pair * PAIR, PAIR), WIN)
    d_out = d_outs[pair]
    back_out = ADAPTER_SCALE * d_out[q_width:]
    d_att_all = d_out[:q_width].astype(F32) + dotg(oin_ref[...], back_out, 1, 0)
    for k in range(heads):
        kv = kv_all[rows, k * PAIR : (k + 1) * PAIR]
        ve = ve_all[rows, k * PAIR : (k + 1) * PAIR]
        base = k * per * STRETCH

        def side(value):
            return jnp.concatenate(
                [value[g * STRETCH : (g + 1) * STRETCH] for g in range(per)], axis=1
            )

        stacked = q_ref[base : base + per * STRETCH, :]
        q = side(stacked)
        d_att = side(d_att_all[base : base + per * STRETCH])
        att = side(att_ref[0, base : base + per * STRETCH, :]).astype(F32)
        inverse = jnp.concatenate(
            [r_ref[0, k * per + g : k * per + g + 1, :] for g in range(per)], axis=1
        )
        ratio = d_att * inverse
        d_den = -jnp.sum(ratio * att, axis=0, keepdims=True)
        d_high = d_den.astype(BF).astype(F32)
        row = lax.broadcasted_iota(jnp.int32, (EXT - STRETCH, lanes), 0)
        extra = jnp.where(row == 0, d_high, jnp.where(row == 1, d_den - d_high, 0.0))
        ratio_ext = jnp.concatenate([ratio, extra], axis=0)
        ratio_low = ratio_ext.astype(BF)
        weights = w_ref[0, k]
        padded = jnp.concatenate([ratio_low, jnp.zeros((PAIR - EXT, lanes), BF)], axis=0)
        d_weights = dotg(ve, padded, 1, 0)
        d_scores = (d_weights * weights.astype(F32)).astype(BF)
        d_query = dotg(kv, d_scores, 0, 0)[:STRETCH] * scale
        zeros = jnp.zeros((STRETCH, lanes), BF)
        q_scaled = (q.astype(F32) * scale).astype(BF)
        d_kv = dotg(d_scores, jnp.concatenate([q_scaled, zeros], axis=0), 1, 1) + dotg(
            weights, jnp.concatenate([zeros, ratio_low[:STRETCH]], axis=0), 1, 1
        )
        dkv_ref[rows, k * PAIR : (k + 1) * PAIR] += d_kv
        phi = phi_ref[0, k]
        both = jnp.concatenate(
            [jnp.where(low, ratio_ext, 0.0), jnp.where(low, 0.0, ratio_ext)], axis=0
        ).astype(BF)
        d_phi = dotg(s_ref[0, k], both, 0, 0)
        d_state = dotg(both, phi, 1, 1)
        ds_ref[0, k] = d_state
        d_mixed = feature_back(phi, d_phi).astype(BF)
        d_mixed = jnp.concatenate(
            [d_mixed[:, g * PAIR : (g + 1) * PAIR] for g in range(per)], axis=0
        )
        d_stacked = jnp.concatenate(
            [d_query[:, g * PAIR : (g + 1) * PAIR] for g in range(per)], axis=0
        ) + dotg(wq_ref[k], d_mixed, 0, 0)
        dq_ref[0, base : base + per * STRETCH, :] = d_stacked.astype(BF)
        map_ref[k] += dotg(stacked, d_mixed, 1, 1)
        rest = d_state[EXT:] + one_c * carry[k]
        head = d_state[:EXT] + one_b * rest
        carry[k] = head
        ends_ref[k, 0] = rest.astype(BF)
        ends_ref[k, 1] = head.astype(BF)

    @pl.when(step == pairs - 1)
    def _():
        back_ref[...] = dkv_ref[:STRETCH, :].astype(BF)


def keys_kernel(
    batch, pairs, blocks, wide_y, count, n_far, has_prev, info, lens, kv_ref, ve_ref, wk_ref,
    phi_ref, dkv_ref, back_ref, ds_ref, dq_ref, q_up_ref, kv_up_ref, *refs,
):
    fars, refs = refs[:n_far], refs[n_far:]
    prevs, refs = (refs[:1], refs[1:]) if has_prev else (None, refs)
    out_ref, map_ref, carry = refs
    step = pl.program_id(0)
    pair = pairs - 1 - step
    heads = kv_ref.shape[1] // PAIR
    slots = Slots(lens, batch)
    block = info[0] + 2 * pair

    @pl.when(step == 0)
    def _():
        for k in range(heads):
            inner, outer = entering(slots, info, fars, blocks, wide_y, count, -1, 0, k)
            carry[k, 0] = outer
            carry[k, 1] = inner
        map_ref[...] = prevs[0][...] if has_prev else jnp.zeros_like(map_ref)

    one_b = slots.weight(block, block + 1)
    one_c = slots.weight(block + 1, block + 2)
    two_c = slots.weight(block, block + 2)
    two_d = slots.weight(block + 1, block + 3)
    row = lax.broadcasted_iota(jnp.int32, (PAIR, PAIR), 0)
    lane = lax.broadcasted_iota(jnp.int32, (PAIR, PAIR), 1)
    last = jnp.where(step == 0, 1.0, 0.0)
    rows = pl.ds(pl.multiple_of(pair * PAIR + STRETCH, STRETCH), PAIR)
    d_kvs = []
    for k in range(heads):
        kv = kv_ref[:, k * PAIR : (k + 1) * PAIR]
        ve = ve_ref[:, k * PAIR : (k + 1) * PAIR].astype(F32)
        next_one, next_two = carry[k, 0], carry[k, 1]
        pad = jnp.zeros((PAIR - EXT, PAIR), F32)
        grads = jnp.concatenate([next_one * two_c, pad, next_two * two_d, pad], axis=0).astype(BF)
        both = jnp.concatenate(
            [jnp.where(row < STRETCH, ve, 0.0), jnp.where(row < STRETCH, 0.0, ve)], axis=1
        ).astype(BF)
        d_phi = dotg(grads, both, 0, 1)
        phi = phi_ref[k * PAIR : (k + 1) * PAIR, :]
        d_both = dotg(phi, grads, 0, 1)
        d_value = jnp.where(row < STRETCH, d_both[:, :PAIR], d_both[:, PAIR:])
        d_value = jnp.where(lane < STRETCH, 0.0, pltpu.roll(d_value, STRETCH, 1))
        d_mixed = feature_back(phi, d_phi).astype(BF)
        d_key = dotg(d_mixed, wk_ref[k], 0, 0)
        map_ref[k] += dotg(kv, d_mixed, 0, 1)
        total = dkv_ref[rows, k * PAIR : (k + 1) * PAIR] + d_value + d_key
        returned = back_ref[:, k * PAIR : (k + 1) * PAIR].astype(F32) * last
        total = total + jnp.concatenate([jnp.zeros_like(returned), returned], axis=0)
        d_kvs.append(jnp.transpose(total).astype(BF))
        state = ds_ref[0, k]
        rest = state[EXT:] + one_c * next_one
        carry[k, 1] = rest
        carry[k, 0] = state[:EXT] + one_b * rest
    d_kv = jnp.concatenate(d_kvs, axis=0)
    back_in = dotg(q_up_ref[...], dq_ref[0], 1, 0) + dotg(kv_up_ref[...], d_kv, 1, 0)
    out_ref[0, :32, :] = (ADAPTER_SCALE * back_in).astype(BF)
    out_ref[0, 32:, :] = d_kv


def adapter_kernel(
    n_grp, has_prev, info, dq_ref, rest_ref, mid_ref, normed_ref, att_ref, *refs
):
    blocks_in, refs = refs[:n_grp], refs[n_grp:]
    prevs, refs = (refs[:3], refs[3:]) if has_prev else (None, refs)
    up_ref, oin_ref, wide_ref = refs
    share = blocks_in[0].shape[1]
    q_width = dq_ref.shape[1]
    for r in range(n_grp):
        there = pl.ds(pl.multiple_of((info[1] ^ r) * share, share), share)
        mids = mid_ref[:, there]
        rest = rest_ref[r]
        both = jnp.concatenate([dq_ref[r], rest], axis=0)
        up = dotg(mids, both, 1, 1)
        oin = dotg(ADAPTER_SCALE * blocks_in[r][q_width:], att_ref[r, :q_width, :], 1, 1)
        wide = dotg(rest[:32], normed_ref[there, :], 1, 0)
        if r or has_prev:
            up_ref[...] = up + (up_ref[...] if r else prevs[0][...])
            oin_ref[...] = oin + (oin_ref[...] if r else prevs[1][...])
            wide_ref[...] = wide + (wide_ref[...] if r else prevs[2][...])
        else:
            up_ref[...] = up
            oin_ref[...] = oin
            wide_ref[...] = wide


def whole(shape):
    return pl.BlockSpec(shape, lambda i, *_: (0,) * len(shape))


def anywhere():
    return pl.BlockSpec(memory_space=pl.ANY)


def sds(shape, kind):
    return jax.ShapeDtypeStruct(shape, kind)


def call(
    kernel, name, grid, scalars, ins, in_specs, out_specs, out_shape, scratch=(), alias=None
):
    return pl.pallas_call(
        kernel,
        grid_spec=pltpu.PrefetchScalarGridSpec(
            num_scalar_prefetch=len(scalars),
            grid=(grid,),
            in_specs=in_specs,
            out_specs=out_specs,
            scratch_shapes=list(scratch),
        ),
        out_shape=out_shape,
        input_output_aliases=alias or {},
        cost_estimate=pl.CostEstimate(flops=0, transcendentals=0, bytes_accessed=1024),
        compiler_params=pltpu.CompilerParams(
            dimension_semantics=("arbitrary",), vmem_limit_bytes=VMEM_LIMIT
        ),
        name=name,
    )(*scalars, *ins)


def run_assemble(info, ring, splits):
    shape = ring.parts[0].shape
    parts_of = ring_layout(ring.count, shape[0])
    outs = [(size, shape[1] * ring.count) for size in splits]
    return call(
        functools.partial(assemble_kernel, parts_of, shape[1], splits), "assemble", 1, [info],
        ring.parts, [whole(part.shape) for part in ring.parts], [whole(out) for out in outs],
        [sds(out, BF) for out in outs],
    )


def run_project(info, lens, batch, normed, weight, q_up, kv_up, maps):
    rows, model = normed.shape
    heads = maps.shape[0]
    width = heads * PAIR
    q_width = weight.shape[0] - 32 - width
    tile = 2 * PAIR
    pairs = rows // PAIR
    return call(
        functools.partial(project_kernel, batch, q_width),
        "project_states", rows // tile, [info, lens],
        [normed, weight, q_up, kv_up, maps],
        [
            pl.BlockSpec((tile, model), lambda i, *_: (i, 0)),
            whole(weight.shape), whole(q_up.shape), whole(kv_up.shape), whole(maps.shape),
        ],
        [
            pl.BlockSpec((q_width, tile), lambda i, *_: (0, i)),
            pl.BlockSpec((tile, width), lambda i, *_: (i, 0)),
            pl.BlockSpec((tile, width), lambda i, *_: (i, 0)),
            pl.BlockSpec((32, tile), lambda i, *_: (0, i)),
            pl.BlockSpec((width, tile), lambda i, *_: (0, i)),
            pl.BlockSpec((2, heads, 2 * EXT, PAIR), lambda i, *_: (i, 0, 0, 0)),
            whole((heads, 2, EXT, PAIR)),
            whole((STRETCH, 2 * width)),
        ],
        [
            sds((q_width, rows), BF),
            sds((rows, width), BF),
            sds((rows, width), BF),
            sds((32, rows), BF),
            sds((width, rows), BF),
            sds((pairs, heads, 2 * EXT, PAIR), F32),
            sds((heads, 2, EXT, PAIR), BF),
            sds((STRETCH, 2 * width), BF),
        ],
        [pltpu.VMEM((heads, EXT, PAIR), F32)],
    )


def run_forward(info, lens, batch, q, kv, ve, halo, maps, o_in, states, fars):
    q_width, rows = q.shape
    width = kv.shape[1]
    heads, pairs = width // PAIR, rows // PAIR
    per = q_width // STRETCH // heads
    count = lax.axis_size("seq")
    wide = max(1, count // 4)
    scale = STRETCH ** (-0.5) * math.log2(math.e)
    step = lambda *shape: pl.BlockSpec((1,) + shape, lambda i, *_: (i,) + (0,) * len(shape))
    column = lambda n: pl.BlockSpec((n, PAIR), lambda i, *_: (0, i))
    share = rows // lax.axis_size("grp")
    return call(
        functools.partial(
            forward_kernel, batch, per, rows // STRETCH, wide, count, len(fars), scale
        ),
        "attention_forward", pairs, [info, lens],
        [q, kv, ve, halo, maps, o_in, states, *fars],
        [
            column(q_width), whole(kv.shape), whole(ve.shape), whole(halo.shape),
            whole(maps.shape), whole(o_in.shape), step(heads, 2 * EXT, PAIR),
            *[whole(far.shape) for far in fars],
        ],
        [
            block_spec(q_width + 16, share, lambda i: i), step(heads, WIN, per * PAIR),
            step(heads, PAIR, per * PAIR), step(heads, 2 * EXT, PAIR), step(heads * per, PAIR),
        ],
        [
            sds((rows // share, q_width + 16, share), BF),
            sds((pairs, heads, WIN, per * PAIR), BF),
            sds((pairs, heads, PAIR, per * PAIR), BF),
            sds((pairs, heads, 2 * EXT, PAIR), BF),
            sds((pairs, heads * per, PAIR), F32),
        ],
        [
            pltpu.VMEM((heads, 2, EXT, PAIR), F32),
            pltpu.VMEM((rows + STRETCH, width), BF),
            pltpu.VMEM((rows + STRETCH, width), BF),
        ],
    )


def block_spec(height, share, pair_of):
    per_block = share // PAIR
    return pl.BlockSpec(
        (1, height, PAIR),
        lambda i, info, *_: ((pair_of(i) // per_block) ^ info[1], 0, pair_of(i) % per_block),
    )


def own_spec(batch, share, model):
    return pl.BlockSpec((1, share, model), lambda i, info: (batch, info[1], 0))


def front(array):
    if len(array.shape) == 2:
        return whole(array.shape)
    return pl.BlockSpec((1,) + array.shape[1:], lambda i, *_: (0, 0, 0))


def run_residual(info, batch, tokens, gain, atts, weights):
    n_grp = len(atts)
    model = tokens.shape[2]
    share = atts[0].shape[-1]
    return call(
        functools.partial(residual_kernel, n_grp), "residual", 1, [info],
        [tokens, gain, *atts, *weights],
        [own_spec(batch, share, model), whole(gain.shape), *[front(att) for att in atts]]
        + [anywhere()] * n_grp,
        [whole((share, model)), whole((share, model)), whole((16, share))],
        [sds((share, model), F32), sds((share, model), BF), sds((16, share), BF)],
        [
            pltpu.VMEM((n_grp,) + weights[0].shape, BF),
            pltpu.SemaphoreType.DMA((n_grp,)),
        ],
    )


def run_branch(info, batch, cotangent, resid, gain, mid, summands, weights):
    n_grp = len(weights)
    share, model = resid.shape
    out = (weights[0].shape[0], share)
    return call(
        functools.partial(branch_kernel, n_grp, len(summands)), "branch_gradient", 1, [info],
        [cotangent, resid, gain, mid, *summands, *weights],
        [
            own_spec(batch, share, model), whole(resid.shape), whole(gain.shape),
            whole(mid.shape), *[whole(resid.shape) for _ in summands],
        ]
        + [anywhere()] * n_grp,
        [whole((share, model)), whole((16, model))] + [whole(out)] * n_grp,
        [sds((share, model), F32), sds((16, model), F32)] + [sds(out, BF)] * n_grp,
        [
            pltpu.VMEM((n_grp,) + weights[0].shape, BF),
            pltpu.SemaphoreType.DMA((n_grp,)),
        ],
    )


def run_tokens(info, batch, tokens, gain, d_resid, dqs, rests, weights, prev):
    n_grp = len(weights)
    batches, _, model = tokens.shape
    share = d_resid.shape[0]
    ins = [tokens, gain, d_resid, *dqs, *rests, *weights]
    specs = [
        own_spec(batch, share, model), whole(gain.shape), whole(d_resid.shape),
        *[front(a) for a in [*dqs, *rests]],
    ] + [anywhere()] * n_grp
    alias = {}
    if prev is not None:
        alias = {len(ins) + 1: 0}
        ins.append(prev)
        specs.append(anywhere())
    return call(
        functools.partial(tokens_kernel, n_grp), "token_gradient", 1, [info], ins, specs,
        pl.BlockSpec((1, share, model), lambda i, *_: (batch, 0, 0)),
        sds((batches, share, model), F32),
        [
            pltpu.VMEM((n_grp,) + weights[0].shape, BF),
            pltpu.VMEM((share, model), F32),
            pltpu.SemaphoreType.DMA((n_grp,)),
        ],
        alias,
    )


def run_mlp(info, batch, xs, cotangent, rings, prevs, sizes):
    n_grp = len(xs)
    share, model = xs[0].shape
    rows = share * n_grp
    depth = rings[0].parts[0].shape[0]
    layout = ring_layout(rings[0].count, depth)
    first = prevs is None
    prevs = [] if first else list(prevs)
    ins = [*xs, cotangent, *[part for ring in rings for part in ring.parts], *prevs]
    if first:
        out_shape = [sds((rows, model), BF)] * 2
    else:
        out_shape = [sds((share, model), BF)] * (2 * n_grp)
    scratch = [
        pltpu.VMEM((rows, model), BF),
        pltpu.VMEM((rows, model), BF),
        pltpu.VMEM((2, model, 3 * CHUNK), BF),
        pltpu.VMEM((rows, model), F32),
        pltpu.VMEM((rows, model), F32),
        pltpu.SemaphoreType.DMA((2,)),
        pltpu.SemaphoreType.DMA((2,)),
    ] + [pltpu.VMEM((rows, model), BF) for _ in prevs]
    return call(
        functools.partial(mlp_kernel, batch, n_grp, layout, sizes, first),
        "feed_forward", sum(sizes) // CHUNK, [info], ins, [anywhere()] * len(ins),
        [anywhere()] * len(out_shape), out_shape, scratch,
    )


def run_backward(
    info, lens, batch, q, kv, ve, halo, maps, o_in, att, weights, phi, states, inverse, d_outs, prevs,
):
    q_width, rows = q.shape
    width = kv.shape[1]
    heads, pairs = width // PAIR, rows // PAIR
    per = q_width // STRETCH // heads
    share = rows // len(d_outs)
    rev = lambda i: pairs - 1 - i
    step = lambda *shape: pl.BlockSpec((1,) + shape, lambda i, *_: (rev(i),) + (0,) * len(shape))
    column = lambda n: pl.BlockSpec((n, PAIR), lambda i, *_: (0, rev(i)))
    prevs = list(prevs or [])
    sums = [sds(maps.shape, F32)]
    return call(
        functools.partial(
            backward_kernel, batch, per, pairs, len(d_outs), bool(prevs), STRETCH ** (-0.5)
        ),
        "attention_backward", pairs, [info, lens],
        [q, kv, ve, halo, maps, o_in, att, weights, phi, states, inverse, *d_outs, *prevs],
        [
            column(q_width), whole(kv.shape), whole(ve.shape), whole(halo.shape),
            whole(maps.shape), whole(o_in.shape), block_spec(q_width + 16, share, rev),
            step(heads, WIN, per * PAIR), step(heads, PAIR, per * PAIR),
            step(heads, 2 * EXT, PAIR), step(heads * per, PAIR),
            *[anywhere() for _ in d_outs], *[whole(prev.shape) for prev in prevs],
        ],
        [
            block_spec(q_width, share, rev), whole((rows + STRETCH, width)), step(heads, 2 * EXT, PAIR),
            whole((heads, 2, EXT, PAIR)), whole((STRETCH, width)),
            *[whole(item.shape) for item in sums],
        ],
        [
            sds((rows // share, q_width, share), BF),
            sds((rows + STRETCH, width), F32),
            sds((pairs, heads, 2 * EXT, PAIR), F32),
            sds((heads, 2, EXT, PAIR), BF),
            sds((STRETCH, width), BF),
            *sums,
        ],
        [
            pltpu.VMEM((heads, EXT, PAIR), F32),
            pltpu.VMEM((rows + STRETCH, width), BF),
            pltpu.VMEM((rows + STRETCH, width), BF),
            pltpu.VMEM((pairs, q_width + 16, PAIR), BF),
            pltpu.SemaphoreType.DMA,
        ],
    )


def run_keys(
    info, lens, batch, kv, ve, maps, phi, d_kv, returned, d_states, d_q, q_up, kv_up, fars, prevs,
):
    width, rows = phi.shape
    heads, pairs = width // PAIR, rows // PAIR
    n_grp, q_width, share = d_q.shape
    count = lax.axis_size("seq")
    wide = max(1, count // 4)
    rev = lambda i: pairs - 1 - i
    column = lambda n: pl.BlockSpec((n, PAIR), lambda i, *_: (0, rev(i)))
    lines = lambda n: pl.BlockSpec((PAIR, n), lambda i, *_: (rev(i), 0))
    prevs = list(prevs or [])
    sums = [sds((heads, PAIR, STRETCH), F32)]
    return call(
        functools.partial(
            keys_kernel, batch, pairs, rows // STRETCH, wide, count, len(fars), bool(prevs)
        ),
        "attention_keys", pairs, [info, lens],
        [
            kv, ve, maps, phi, d_kv, returned, d_states, d_q, q_up, kv_up, *fars, *prevs,
        ],
        [
            lines(width), lines(width), whole(maps.shape), column(width), whole(d_kv.shape),
            whole(returned.shape),
            pl.BlockSpec((1, heads, 2 * EXT, PAIR), lambda i, *_: (rev(i), 0, 0, 0)),
            block_spec(q_width, share, rev), whole(q_up.shape), whole(kv_up.shape),
            *[whole(far.shape) for far in fars], *[whole(prev.shape) for prev in prevs],
        ],
        [block_spec(32 + width, share, rev), *[whole(item.shape) for item in sums]],
        [sds((n_grp, 32 + width, share), BF), *sums],
        [pltpu.VMEM((heads, 2, EXT, PAIR), F32)],
    )


def run_adapters(info, d_q, rest, mids, normed, att, d_outs, prevs):
    model = normed.shape[1]
    prevs = list(prevs or [])
    ins = [d_q, rest, mids, normed, att, *d_outs, *prevs]
    out_shape = [
        sds((32, d_q.shape[1] + rest.shape[1]), F32), sds((16, d_q.shape[1]), F32),
        sds((32, model), F32),
    ]
    return call(
        functools.partial(adapter_kernel, len(d_outs), bool(prevs)),
        "adapter_gradients", 1, [info], ins, [whole(item.shape) for item in ins],
        [whole(item.shape) for item in out_shape], out_shape,
    )


def summed(value, axis):
    value = value.astype(BF)
    bit = 1
    while bit < lax.axis_size(axis):
        value = (value.astype(F32) + flip(value, axis, bit).astype(F32)).astype(BF)
        bit *= 2
    return value


def local(
    tokens,
    cotangent,
    lengths,
    attention_norm_gain,
    feedforward_norm_gain,
    query_weight,
    keyvalue_weight,
    output_weight,
    gate_up_weight,
    down_weight,
    adapter_width_factor,
    query_up_factor,
    keyvalue_up_factor,
    output_input_factor,
    query_feature_weight,
    key_feature_weight,
):
    batches, rows, model = tokens.shape
    n_seq, n_grp = lax.axis_size("seq"), lax.axis_size("grp")
    group_index, seq_index = lax.axis_index("grp"), lax.axis_index("seq")
    share = rows // n_grp
    rank = adapter_width_factor.shape[2]
    depth, q_width = query_weight.shape
    kv_heads = key_feature_weight.shape[0]
    kv_width = kv_heads * PAIR
    per = query_feature_weight.shape[0] // kv_heads
    hidden_width = down_weight.shape[0]
    gain_attn = attention_norm_gain.astype(F32)[None]
    gain_mlp = feedforward_norm_gain.astype(F32)[None]

    sources = lax.dynamic_index_in_dim(
        jnp.asarray(ring_sources(n_seq), jnp.int32), seq_index, 0, False
    )
    info = jnp.concatenate(
        [jnp.stack([seq_index * (rows // STRETCH), group_index, seq_index]).astype(jnp.int32), sources]
    )

    kv_shard = (
        keyvalue_weight.reshape(depth, 2, kv_heads, STRETCH)
        .transpose(2, 1, 3, 0)
        .reshape(kv_width, depth)
    )
    adapters = adapter_width_factor.transpose(0, 2, 1)
    pad = jnp.zeros((rank, depth), BF)
    in_ring = Ring(
        jnp.concatenate(
            [
                query_weight.T, adapters[:3].reshape(3 * rank, depth), pad, kv_shard,
                output_weight, adapters[3], pad,
            ],
            axis=0,
        )
    )
    down_t = down_weight.T
    half_shards = [
        jnp.concatenate(
            [
                gate_up_weight[:, 0, first : first + size],
                gate_up_weight[:, 1, first : first + size],
                down_t[:, first : first + size],
            ],
            axis=1,
        )
        for first, size in pieces_of(hidden_width)
    ]
    ring_a, ring_b, ring_c = rings = [Ring(shard) for shard in half_shards]
    kv_parts = keyvalue_up_factor.reshape(2, rank, kv_heads, STRETCH)
    kv_up = jnp.zeros((2, rank, kv_heads, 2, STRETCH), BF)
    kv_up = kv_up.at[0, :, :, 0].set(kv_parts[0]).at[1, :, :, 1].set(kv_parts[1])
    kv_up = kv_up.reshape(2 * rank, kv_width)
    kv_up = jnp.concatenate(
        [jnp.zeros((rank, kv_width), BF), kv_up, jnp.zeros((rank, kv_width), BF)]
    )
    q_up = jnp.concatenate([query_up_factor, jnp.zeros((3 * rank, q_width), BF)])
    q_up_t = q_up.T
    o_in = jnp.concatenate([output_input_factor, jnp.zeros((q_width, rank), BF)], axis=1)
    maps_t = query_feature_weight.transpose(0, 2, 1).reshape(kv_heads, per, STRETCH, STRETCH)
    query_maps = jnp.zeros((kv_heads, per, STRETCH, per, STRETCH), BF)
    for g in range(per):
        query_maps = query_maps.at[:, g, :, g, :].set(maps_t[:, g])
    query_maps = query_maps.reshape(kv_heads, per * STRETCH, per * STRETCH)
    key_maps = jnp.concatenate(
        [key_feature_weight.transpose(0, 2, 1), jnp.zeros((kv_heads, STRETCH, STRETCH), BF)], axis=2
    )

    normed_rows = []
    for batch in range(batches):
        x = tokens[batch].astype(F32)
        factor = lax.rsqrt(jnp.mean(x * x, axis=-1, keepdims=True) + EPS)
        normed_rows.append((x * factor * gain_attn).astype(BF))
    in_ring.hop()
    in_ring.hop()
    query_maps, key_maps, kv_up, q_up_t, normed_rows[0] = in_ring.tie(
        query_maps, key_maps, kv_up, q_up_t, normed_rows[0]
    )
    in_ring.hop()
    for ring in rings[:2]:
        ring.ahead, ring.back, *_ = lax.optimization_barrier((ring.ahead, ring.back))
    normed_rows[1] = in_ring.tie(normed_rows[1])[0]
    while in_ring.done < in_ring.hops():
        in_ring.hop()
    ring_a.hop(*in_ring.parts[5:7])
    ring_b.hop(*in_ring.parts[5:7])
    weight_in, weight_out = run_assemble(
        info, in_ring, [q_width + 32 + kv_width, q_width + 2 * rank]
    )
    far_out = far_gather(weight_out)

    saved = []
    for batch in range(batches):
        normed = normed_rows[batch]
        q, kv, ve, mids, phi_key, states, ends, halo = run_project(
            info, lengths, batch, normed, weight_in, q_up_t, kv_up, key_maps
        )
        saved.append([q, kv, ve, mids, normed, phi_key, states, ends, halo])
    ends = jnp.stack([item[7] for item in saved])
    halo = jnp.stack([item[8] for item in saved])
    (ends,) = ring_a.tie(ends)
    (ends,) = ring_b.tie(ends)
    fars, halo = exchange(ends, halo, 1)
    for item in saved:
        item[7:] = [fars, halo]
    ring_a.hop(*fars[1:])
    ring_b.hop(*fars[1:])

    attended = []
    for batch in range(batches):
        q, kv, ve, mids, normed, phi_key, states, fars, halo = saved[batch]
        if batch:
            q = after(q, attended[0][0])
        att, weights, phi, sums, inverse = run_forward(
            info, lengths, batch, q, kv, ve, halo, query_maps, o_in, states, fars
        )
        atts = group_exchange([att[r] for r in range(n_grp)])
        attended.append([att, weights, phi, sums, inverse, atts])
    far_out = [far_out[0]] + [after(far, attended[0][0]) for far in far_out[1:]]
    weights_out = near_gather(far_out)
    mlp_ins = []
    for batch in range(batches):
        att, weights, phi, sums, inverse, atts = attended[batch]
        if batch:
            atts[-1] = after(atts[-1], mlp_ins[0][0])
        resid, mlp_in, mid = run_residual(
            info, batch, tokens, gain_mlp, [att, *atts[1:]], weights_out
        )
        if batch == 0:
            (mlp_in,) = ring_a.tie(mlp_in)
            (mlp_in,) = ring_b.tie(mlp_in)
            ring_a.hop(mlp_in)
            ring_b.hop(mlp_in)
        attended[batch][5:] = [resid, mid]
        mlp_ins.append(group_gather(mlp_in))
    ring_a.hop(mlp_ins[1][0])
    ring_b.hop(mlp_ins[1][0])
    ring_c.hop(mlp_ins[1][0], *ring_a.parts[-2:], *ring_b.parts[-2:])

    sizes = [size for _, size in pieces_of(hidden_width)]
    partial = [None] * batches
    ring_a.finish()
    ring_b.finish()
    partial[0] = list(
        run_mlp(info, 0, mlp_ins[0], cotangent, [ring_a, ring_b], None, sizes[:2])
    )
    partial[0][0], mlp_ins[1][0] = ring_c.tie(partial[0][0], mlp_ins[1][0])
    ring_c.hop()
    far_in = far_gather(after(weight_in, partial[0][0]))
    partial[1] = list(
        run_mlp(info, 1, mlp_ins[1], cotangent, [ring_a, ring_b], None, sizes[:2])
    )
    (partial[1][0],) = ring_c.tie(partial[1][0])
    ring_c.hop()
    ring_c.finish()
    far_in, partial[0][0] = lax.optimization_barrier((far_in, partial[0][0]))
    weights_in = near_gather(far_in)
    partial[0] = list(
        run_mlp(info, 0, mlp_ins[0], cotangent, [ring_c], partial[0], sizes[2:])
    )
    started = [scatter_start(partial[0][:n_grp])]
    started[0][0][0], partial[1][0] = lax.optimization_barrier((started[0][0][0], partial[1][0]))
    partial[1] = list(
        run_mlp(info, 1, mlp_ins[1], cotangent, [ring_c], partial[1], sizes[2:])
    )

    def run_branch_of(batch):
        resid, mid = attended[batch][5:]
        d_resid, wide, *d_out = run_branch(
            info, batch, cotangent, resid, gain_mlp, mid, scatter_end(*started[batch]), weights_out
        )
        return d_resid, wide, group_exchange(d_out)

    def run_backward_of(batch, q, d_outs, sums_back):
        _, kv, ve, mids, normed, phi_key, states, fars, halo = saved[batch]
        att, weights, phi, sums, inverse = attended[batch][:5]
        d_q, d_kv, d_states, ends, back, *sums_back = run_backward(
            info, lengths, batch, q, kv, ve, halo, query_maps, o_in, att, weights, phi, sums,
            inverse, d_outs, sums_back,
        )
        fars, returned = exchange(ends[None], back, -1)
        d_qs = group_exchange([d_q[r] for r in range(n_grp)])
        return [d_q, d_qs, d_kv, d_states, fars, returned], sums_back

    def run_keys_of(batch, kv, gone, sums_keys):
        _, _, ve, mids, normed, phi_key, states, _, _ = saved[batch]
        d_q, d_qs, d_kv, d_states, fars, returned = gone
        rest, *sums_keys = run_keys(
            info, lengths, batch, kv, ve, key_maps, phi_key, d_kv, returned, d_states, d_q, q_up,
            kv_up, fars, sums_keys,
        )
        rests = group_exchange([rest[r] for r in range(n_grp)])
        return [rest, *rests[1:]], sums_keys

    def run_adapters_of(batch, d_q, rest, d_outs, prevs):
        return run_adapters(
            info, d_q, rest, saved[batch][3], saved[batch][4], attended[batch][0], d_outs, prevs
        )

    def run_tokens_of(batch, d_resid, gone, rests, prev):
        d_q, d_qs = gone[:2]
        return run_tokens(
            info, batch, tokens, gain_attn, d_resid, [d_q, *d_qs[1:]], rests, weights_in, prev
        )

    d_resid_a, wide_a, d_outs_a = run_branch_of(0)
    partial[1][0] = after(partial[1][0], d_resid_a)
    started.append(scatter_start(partial[1][:n_grp]))
    started[1][0][0] = after(started[1][0][0], *d_outs_a[1:])
    gone_a, sums_back = run_backward_of(0, saved[0][0], d_outs_a, None)
    attended[1][6] = after(attended[1][6], gone_a[0])
    d_resid_b, wide_b, d_outs_b = run_branch_of(1)
    rests_a, sums_keys = run_keys_of(0, after(saved[0][1], d_resid_b), gone_a, None)
    gone_b, sums_back = run_backward_of(
        1, after(saved[1][0], rests_a[0]), d_outs_b, sums_back
    )
    sums_adapters = run_adapters_of(
        0, after(gone_a[0], gone_b[0]), rests_a[0], d_outs_a, None
    )
    grad_tokens = run_tokens_of(
        0, after(d_resid_a, sums_adapters[0]), gone_a, rests_a, None
    )
    rests_b, sums_keys = run_keys_of(1, after(saved[1][1], grad_tokens), gone_b, sums_keys)
    sums_adapters = run_adapters_of(1, gone_b[0], rests_b[0], d_outs_b, sums_adapters)
    grad_tokens = run_tokens_of(
        1, after(d_resid_b, sums_adapters[0]), gone_b, rests_b, grad_tokens
    )
    wide_out = wide_a + wide_b
    block_rows = []
    for batch, ready in enumerate([rests_a[0], rests_b[0]]):
        blocks = partial[batch][n_grp:]
        blocks[0] = after(blocks[0], ready)
        blocks[1], blocks[-1] = after(blocks[1], ready), after(blocks[-1], ready)
        total = attended[batch][5]
        for summand in scatter_end(*scatter_start(blocks)):
            total = total + summand.astype(F32)
        block_rows.append(total.astype(BF))

    (map_grad,), (key_grad,) = sums_back, sums_keys
    up_grad, oin_grad, wide_in = sums_adapters
    wide = jnp.concatenate([wide_in[: 3 * rank], wide_out[:rank]])
    up_grad = ADAPTER_SCALE * up_grad
    kv_grad = up_grad[rank : 3 * rank, q_width + 32 :].reshape(2, rank, kv_heads, 2, STRETCH)
    kv_grad = jnp.stack([kv_grad[0, :, :, 0], kv_grad[1, :, :, 1]])
    map_blocks = map_grad.reshape(kv_heads, per, STRETCH, per, STRETCH)
    query_grad = jnp.stack([map_blocks[:, g, :, g] for g in range(per)], axis=1)
    pieces = [
        (up_grad[:rank, :q_width], query_up_factor.shape),
        (kv_grad, keyvalue_up_factor.shape),
        (oin_grad[:rank].T, output_input_factor.shape),
        (query_grad, query_feature_weight.shape),
        (key_grad[:, :STRETCH], key_feature_weight.shape),
    ]
    wide = summed(wide, "grp")
    packed = jnp.concatenate(
        [wide.reshape(-1)] + [piece.astype(BF).reshape(-1) for piece, _ in pieces]
    ).reshape(-1, PAIR)
    packed = summed(packed, "seq").reshape(-1).astype(F32)
    wide = packed[: wide.size].reshape(4, rank, n_seq * n_grp, model // (n_seq * n_grp))
    wide = lax.dynamic_index_in_dim(wide, seq_index * n_grp + group_index, 2, False)
    outs, first = [], 4 * rank * model
    for piece, shape in pieces:
        outs.append(packed[first : first + piece.size].reshape(shape))
        first += piece.size
    return (jnp.stack(block_rows), grad_tokens, wide.transpose(0, 2, 1), *outs)


def solution(mesh):
    return jax.shard_map(
        local,
        mesh=mesh,
        in_specs=(
            P(None, "seq", None),
            P(None, "seq", None),
            P(),
            P(),
            P(),
            P("seq", "grp"),
            P("seq", None, "grp"),
            P("grp", "seq"),
            P("seq", None, "grp"),
            P("grp", "seq"),
            P(None, "seq", None),
            P(None, "grp"),
            P(None, None, "grp"),
            P("grp", None),
            P("grp", None, None),
            P("grp", None, None),
        ),
        out_specs=(
            P(None, ("seq", "grp"), None),
            P(None, ("seq", "grp"), None),
            P(None, ("seq", "grp"), None),
            P(None, "grp"),
            P(None, None, "grp"),
            P("grp", None),
            P("grp", None, None),
            P("grp", None, None),
        ),
        check_vma=False,
    )
```

```python
import functools
import math

import jax
import jax.numpy as jnp
from jax import lax
from jax.experimental import pallas as pl
from jax.experimental.pallas import tpu as pltpu
from jax.sharding import PartitionSpec as P

STRETCH = 64
PAIR = 2 * STRETCH
WIN = 3 * STRETCH
EXT = 80
EPS = 1e-05
ADAPTER_SCALE = 2.0
BF = jnp.bfloat16
F32 = jnp.float32
VMEM_LIMIT = 58 * 1024 * 1024
CHUNK = 256
ROW_TILE = 512


def dotg(left, right, lc, rc):
    return lax.dot_general(left, right, (((lc,), (rc,)), ((), ())), preferred_element_type=F32)


def ring_order(count):
    if count % 8:
        return list(range(count))
    deep, wide = 4, count // 4
    path = [z * wide for z in range(deep)]
    for step, z in enumerate(reversed(range(deep))):
        ys = list(range(1, wide))
        path += [z * wide + y for y in (ys if step % 2 == 0 else ys[::-1])]
    return path


def ring_offsets(count):
    out = [0]
    for distance in range(1, (count + 1) // 2):
        out += [-distance, distance]
    return out + [count // 2]


def ring_sources(count):
    order = ring_order(count)
    return [[order[(order.index(s) + o) % count] for o in ring_offsets(count)] for s in range(count)]


def ring_cut(rows):
    return (rows // 2 + 15) // 16 * 16


def ring_layout(count, rows):
    cut = ring_cut(rows)
    return [(q, 0, rows) for q in range(count - 1)] + [
        (count - 1, 0, cut), (count - 1, cut, rows - cut),
    ]


def pieces_of(width):
    first = width // (2 * CHUNK) * CHUNK
    return [(0, first), (first, width - first)]


class Ring:
    def __init__(self, shard):
        self.count = lax.axis_size("seq")
        self.order = ring_order(self.count)
        self.parts = [shard]
        self.ahead = self.back = shard
        self.done = 0

    def move(self, value, step):
        pairs = [(self.order[i], self.order[(i + step) % self.count]) for i in range(self.count)]
        return lax.ppermute(value, "seq", pairs)

    def hop(self, *after):
        self.ahead, self.back, *_ = lax.optimization_barrier((self.ahead, self.back, *after))
        self.done += 1
        if self.done < (self.count + 1) // 2:
            self.ahead, self.back = self.move(self.ahead, 1), self.move(self.back, -1)
            self.parts += [self.ahead, self.back]
        else:
            cut = ring_cut(self.ahead.shape[0])
            self.parts += [self.move(self.ahead[:cut], 1), self.move(self.back[cut:], -1)]

    def hops(self):
        return (self.count + 1) // 2

    def tie(self, *values):
        self.ahead, self.back, *values = lax.optimization_barrier((self.ahead, self.back, *values))
        return values

    def finish(self):
        while self.done < self.hops():
            self.hop()
        return self


def after(value, *others):
    return lax.optimization_barrier((value, *others))[0]


def flip(value, axis, bit):
    count = lax.axis_size(axis)
    return lax.ppermute(value, axis, [(i, i ^ bit) for i in range(count)])


def shifted(value, axis, steps):
    count = lax.axis_size(axis)
    first, last = max(0, -steps), min(count, count - steps)
    return lax.ppermute(value, axis, [(i, i + steps) for i in range(first, last)])


def group_gather(share):
    count = lax.axis_size("grp")
    out = []
    for far in range(0, count, 2):
        mine = share if far == 0 else flip(share, "grp", far)
        out += [mine, flip(mine, "grp", 1)]
    return out


def far_gather(share):
    return [share] + [flip(share, "grp", far) for far in range(2, lax.axis_size("grp"), 2)]


def near_gather(fars):
    out = []
    for far in fars:
        out += [far, flip(far, "grp", 1)]
    return out


def group_exchange(blocks):
    return [blocks[0]] + [flip(blocks[r], "grp", r) for r in range(1, len(blocks))]


def far_pair(here, there):
    return (here.astype(F32) + flip(there, "grp", 1).astype(F32)).astype(BF)


def scatter_start(blocks):
    count = len(blocks)
    fars = []
    for far in range(2, count, 2):
        fars.append(far_pair(blocks[far], blocks[far + 1]))
    return fars, [blocks[0], flip(blocks[1], "grp", 1)]


def scatter_end(fars, nears):
    return nears + [flip(far, "grp", 2 * (i + 1)) for i, far in enumerate(fars)]


def exchange(table, ends, halo, sign):
    count = lax.axis_size("seq")
    wide = max(1, count // 4)
    here = [flip(ends, "seq", j) for j in range(1, wide)]
    full, inner = run_layer(table, [ends, *here], sign)
    out = here + [shifted(full, "seq", sign * wide), shifted(inner, "seq", sign * wide)]
    out += [shifted(full, "seq", sign * r * wide) for r in range(2, count // wide)]
    return out, shifted(halo, "seq", sign)


VALID, ONE, TWO = range(3)
FULL, INNER, NEXT, LAYER_FULL, LAYER_INNER, LAYER_NEXT = range(6)
TABLE_ROWS = 15


def side_row(sign, row):
    return 3 + row + (0 if sign > 0 else 6)


def table_width(blocks, count):
    return max(blocks + 4, 2 * count)


def layout_kernel(blocks, wide, count, info, lens, out):
    width = table_width(blocks, count)
    base, seq = info[0], info[2]
    z, y = seq // wide, seq % wide
    for batch in range(lens.shape[0]):
        starts, ends, at = [], [], 0
        for i in range(lens.shape[1]):
            length = lens[batch, i]
            starts.append(at)
            ends.append(at * STRETCH + length)
            at = at + ((length + STRETCH - 1) >> 6)

        def owner(c):
            total = -1
            for start in starts:
                total = total + jnp.where(start <= c, 1, 0)
            return total

        def put(row, i, value):
            out[(batch * TABLE_ROWS + row) * width + i] = value

        owned = [owner(base + c) for c in range(-3, blocks + 3)]
        for i in range(blocks + 4):
            c = base + i - 1
            end = 0
            for start, stop in zip(starts, ends):
                end = jnp.where(start <= c, stop, end)
            put(VALID, i, jnp.clip(end - c * STRETCH, 0, STRETCH))
            put(ONE, i, jnp.where(owned[i + 2] == owned[i + 1], 1, 0))
            put(TWO, i, jnp.where(owned[i + 2] == owned[i], 1, 0))
        for sign in (1, -1):
            edge = base - 1 if sign > 0 else base + blocks
            outer, inner = owner(edge), owner(edge - sign)
            end_of = lambda device: device * blocks + (blocks - 1 if sign > 0 else 0)
            last = wide - 1 if sign > 0 else 0
            first = wide - 1 - last
            layer_end = end_of(z * wide + last)
            layer_outer, layer_inner = owner(layer_end), owner(layer_end - sign)
            for j in range(wide):
                source = z * wide + (y ^ j)
                far = (seq - source) * sign
                there = owner(end_of(source))
                put(side_row(sign, FULL), j, jnp.where((far > 0) & (there == outer), 1, 0))
                put(side_row(sign, INNER), j, jnp.where((far > 1) & (there == inner), 1, 0))
                put(side_row(sign, NEXT), j, jnp.where(far == 1, 1, 0))
                put(side_row(sign, LAYER_FULL), j, jnp.where(there == layer_outer, 1, 0))
                outermost = (y ^ j) == last
                put(side_row(sign, LAYER_NEXT), j, jnp.where(outermost, 1, 0))
                put(
                    side_row(sign, LAYER_INNER), j,
                    jnp.where((there == layer_inner) & (~outermost), 1, 0),
                )
            for r in range(1, count // wide):
                layer = z - sign * r
                inside = (layer >= 0) & (layer < count // wide)
                there = owner(end_of(layer * wide + last))
                i = wide + r
                direct = (y == first) if r == 1 else (y != y)
                put(side_row(sign, FULL), i, jnp.where(inside & (there == outer), 1, 0))
                put(
                    side_row(sign, INNER), i,
                    jnp.where(inside & (there == inner) & (~direct), 1, 0),
                )
                put(side_row(sign, NEXT), i, jnp.where(inside & direct, 1, 0))


class Slots:
    def __init__(self, table, batch, blocks, count):
        self.table, self.batch, self.width = table, batch, table_width(blocks, count)

    def at(self, row, i):
        return self.table[(self.batch * TABLE_ROWS + row) * self.width + i]

    def valid(self, c):
        return self.at(VALID, c + 1)

    def one(self, c):
        return self.at(ONE, c + 1)

    def weight_one(self, c):
        return self.one(c).astype(F32)

    def weight_two(self, c):
        return self.at(TWO, c + 1).astype(F32)


def entering(slots, arrays, wide, count, sign, place, near_k):
    inner = outer = jnp.zeros((EXT, PAIR), F32)
    row = lambda name, i: slots.at(side_row(sign, name), i).astype(F32)
    for j in range(1, wide):
        array = arrays[j - 1]
        full = array[place, near_k, 1].astype(F32)
        outer = outer + row(FULL, j) * full
        inner = inner + row(INNER, j) * full + row(NEXT, j) * array[place, near_k, 0].astype(F32)
    layers = arrays[wide - 1 :]
    for r in range(1, count // wide):
        full = layers[0 if r == 1 else r][place, near_k].astype(F32)
        outer = outer + row(FULL, wide + r) * full
        inner = inner + row(INNER, wide + r) * full
        if r == 1:
            inner = inner + row(NEXT, wide + 1) * layers[1][place, near_k].astype(F32)
    return inner, outer


def layer_kernel(sign, blocks, count, wide, table, *refs):
    ends, (full_ref, inner_ref) = refs[:wide], refs[wide:]
    for batch in range(full_ref.shape[0]):
        slots = Slots(table, batch, blocks, count)
        row = lambda name, i: slots.at(side_row(sign, name), i).astype(F32)
        for k in range(full_ref.shape[1]):
            full = inner = jnp.zeros((EXT, PAIR), F32)
            for j in range(wide):
                value = ends[j][batch, k, 1].astype(F32)
                full = full + row(LAYER_FULL, j) * value
                inner = inner + row(LAYER_INNER, j) * value
                inner = inner + row(LAYER_NEXT, j) * ends[j][batch, k, 0].astype(F32)
            full_ref[batch, k] = full.astype(BF)
            inner_ref[batch, k] = inner.astype(BF)


def half_mask(shape):
    return (lax.broadcasted_iota(jnp.int32, shape, 1) & (PAIR - 1)) < STRETCH


def feature_softmax(u):
    top = jnp.exp(u - jnp.max(u, axis=0, keepdims=True))
    bottom = jnp.exp(jnp.min(u, axis=0, keepdims=True) - u)
    top = top * (1.0 / jnp.sum(top, axis=0, keepdims=True))
    bottom = bottom * (1.0 / jnp.sum(bottom, axis=0, keepdims=True))
    return jnp.concatenate([top, bottom], axis=0)


def feature_back(phi, d_phi):
    top, bottom = phi[:STRETCH].astype(F32), phi[STRETCH:].astype(F32)
    a, b = d_phi[:STRETCH], d_phi[STRETCH:]
    return top * (a - jnp.sum(top * a, axis=0, keepdims=True)) - bottom * (
        b - jnp.sum(bottom * b, axis=0, keepdims=True)
    )


def assemble_kernel(parts_of, width, splits, info, *refs):
    ins, outs = refs[: len(parts_of)], refs[len(parts_of) :]
    for (q, first, rows), ref in zip(parts_of, ins):
        column = pl.ds(pl.multiple_of(info[3 + q] * width, width), width)
        at = 0
        for out, size in zip(outs, splits):
            low, high = max(at, first), min(at + size, first + rows)
            if low < high:
                out[low - at : high - at, column] = ref[low - first : high - first, :]
            at += size


def project_kernel(
    batch, q_width, blocks, count, table, normed_ref, w_ref, up_ref, kv_up_ref, wk_ref,
    q_ref, kv_ref, ve_ref, mid_ref, phi_ref, st_ref, ends_ref, halo_ref, carry,
):
    step = pl.program_id(0)
    rows = normed_ref.shape[0]
    width = kv_ref.shape[1]
    heads = width // PAIR

    @pl.when(step == 0)
    def _():
        carry[...] = jnp.zeros_like(carry)

    normed = normed_ref[...]
    mixed = dotg(w_ref[: q_width + 32], normed, 1, 1)
    mids = mixed[q_width:].astype(BF)
    mid_ref[...] = mids
    query = mixed[:q_width] + ADAPTER_SCALE * dotg(up_ref[...], mids, 1, 0)
    q_ref[...] = query.astype(BF)
    kv_all = dotg(normed, w_ref[q_width + 32 :], 1, 1) + ADAPTER_SCALE * dotg(
        mids, kv_up_ref[...], 0, 0
    )
    kv_all = kv_all.astype(BF)
    kv_ref[...] = kv_all
    halo_ref[:, :width] = kv_all[rows - STRETCH :]

    slots = Slots(table, batch, blocks, count)
    lane = lax.broadcasted_iota(jnp.int32, (1, PAIR), 1)
    low = lane < STRETCH
    inside = lane & (STRETCH - 1)
    wide = lax.broadcasted_iota(jnp.int32, (PAIR, PAIR), 1)
    for sub in range(rows // PAIR):
        block = 2 * (step * (rows // PAIR) + sub)
        one_a, one_b = slots.weight_one(block), slots.weight_one(block + 1)
        valid = inside < jnp.where(low, slots.valid(block), slots.valid(block + 1))
        valid = jnp.where(valid, 1.0, 0.0)
        valid_low = jnp.where(low, valid, 0.0)
        valid_high = valid - valid_low
        at = sub * PAIR
        for k in range(heads):
            kv = kv_all[at : at + PAIR, k * PAIR : (k + 1) * PAIR]
            moved = pltpu.roll(kv.astype(F32), STRETCH, 1)
            ve = jnp.where(
                wide < STRETCH, moved, jnp.where(wide < STRETCH + 2, 1.0, 0.0)
            ).astype(BF)
            ve_ref[at : at + PAIR, k * PAIR : (k + 1) * PAIR] = ve
            if sub == rows // PAIR - 1:
                halo_ref[:, width + k * PAIR : width + (k + 1) * PAIR] = ve[STRETCH:]
            phi = feature_softmax(dotg(wk_ref[k], kv, 1, 1))
            phi_ref[k * PAIR : (k + 1) * PAIR, at : at + PAIR] = (phi * valid).astype(BF)
            first = dotg(ve, (phi * valid_low).astype(BF), 0, 1)[:EXT]
            second = dotg(ve, (phi * valid_high).astype(BF), 0, 1)[:EXT]
            st_ref[sub, k, :EXT] = first
            st_ref[sub, k, EXT:] = second
            mid = carry[k] * one_a + first
            tail = mid * one_b + second
            carry[k] = tail
            ends_ref[k, 0] = mid.astype(BF)
            ends_ref[k, 1] = tail.astype(BF)


def window_mask(slots, block):
    lane = lax.broadcasted_iota(jnp.int32, (1, PAIR), 1)
    low = lane < STRETCH
    before = slots.valid(block - 1) * slots.one(block)
    own = slots.valid(block)
    limits = [
        jnp.where(low, before, 0),
        jnp.where(low, jnp.minimum(lane + 1, own), own * slots.one(block + 1)),
        jnp.where(low, 0, jnp.minimum(lane - STRETCH + 1, slots.valid(block + 1))),
    ]
    row = lax.broadcasted_iota(jnp.int32, (STRETCH, PAIR), 0)
    return jnp.concatenate([jnp.where(row < limit, 1.0, 0.0) for limit in limits], axis=0)


def fill_window(batch, kv_ref, ve_ref, halo_ref, kv_all, ve_all):
    width = kv_ref.shape[1]
    kv_all[:STRETCH] = halo_ref[batch, :, :width]
    ve_all[:STRETCH] = halo_ref[batch, :, width:]
    kv_all[STRETCH:] = kv_ref[...]
    ve_all[STRETCH:] = ve_ref[...]


def forward_kernel(
    batch, per, blocks, wide, count, n_far, scale, info, table, q_ref, kv_ref, ve_ref, halo_ref,
    wq_ref, oin_ref, st_ref, *refs,
):
    fars = refs[:n_far]
    att_ref, w_ref, phi_ref, s_ref, r_ref, carry, kv_all, ve_all = refs[n_far:]
    step = pl.program_id(0)
    heads = kv_ref.shape[1] // PAIR
    slots = Slots(table, batch, blocks, count)
    block = 2 * step

    @pl.when(step == 0)
    def _():
        fill_window(batch, kv_ref, ve_ref, halo_ref, kv_all, ve_all)
        for k in range(heads):
            inner, outer = entering(slots, fars, wide, count, 1, batch, k)
            carry[k, 0] = inner
            carry[k, 1] = outer

    one_a, one_b = slots.weight_one(block), slots.weight_one(block + 1)
    two_a, two_b = slots.weight_two(block), slots.weight_two(block + 1)
    mask = window_mask(slots, block)
    mask = jnp.concatenate([mask] * per, axis=1)
    lanes = per * PAIR
    low = half_mask((EXT, lanes))
    rows = pl.ds(pl.multiple_of(step * PAIR, PAIR), WIN)
    out_mid = jnp.zeros((16, PAIR), F32)
    for k in range(heads):
        kv = kv_all[rows, k * PAIR : (k + 1) * PAIR]
        ve = ve_all[rows, k * PAIR : (k + 1) * PAIR]
        base = k * per * STRETCH
        stacked = q_ref[base : base + per * STRETCH, :]
        q = jnp.concatenate(
            [stacked[g * STRETCH : (g + 1) * STRETCH] for g in range(per)], axis=1
        )
        q = jnp.concatenate([q, jnp.zeros_like(q)], axis=0)
        scores = dotg(kv, q, 1, 0)
        weights = (jnp.exp2(scores * scale) * mask).astype(BF)
        w_ref[0, k] = weights
        mixed = dotg(wq_ref[k], stacked, 1, 0)
        phi = jnp.concatenate(
            [
                feature_softmax(mixed[g * STRETCH : (g + 1) * STRETCH]).astype(BF)
                for g in range(per)
            ],
            axis=1,
        )
        phi_ref[0, k] = phi
        older, old = carry[k, 0], carry[k, 1]
        states = jnp.concatenate([older * two_a, old * two_b], axis=0).astype(BF)
        s_ref[0, k] = states
        linear = dotg(states, phi, 1, 0)
        total = dotg(ve, weights, 0, 0)[:EXT] + jnp.where(low, linear[:EXT], linear[EXT:])
        inverse = 1.0 / total[STRETCH : STRETCH + 1]
        att = (total[:STRETCH] * inverse).astype(BF)
        att = jnp.concatenate([att[:, g * PAIR : (g + 1) * PAIR] for g in range(per)], axis=0)
        att_ref[0, base : base + per * STRETCH, :] = att
        out_mid = out_mid + dotg(oin_ref[base : base + per * STRETCH, :], att, 0, 0)
        for g in range(per):
            r_ref[0, k * per + g : k * per + g + 1, :] = inverse[:, g * PAIR : (g + 1) * PAIR]
        current = old * one_a + st_ref[0, k, :EXT]
        carry[k, 0] = current
        carry[k, 1] = current * one_b + st_ref[0, k, EXT:]
    att_ref[0, heads * per * STRETCH :, :] = (ADAPTER_SCALE * out_mid).astype(BF)


def residual_kernel(n_grp, info, x_ref, gain_ref, *refs):
    atts, weights = refs[:n_grp], refs[n_grp : 2 * n_grp]
    resid_ref, low_ref, mid_ref, buffer, sems = refs[2 * n_grp :]
    copies = [
        pltpu.make_async_copy(weights[r], buffer.at[r], sems.at[r]) for r in range(n_grp)
    ]
    for copy in copies:
        copy.start()
    q_width = buffer.shape[1] - 16
    resid_ref[...] = x_ref[0].astype(F32)
    mid = jnp.zeros(mid_ref.shape, F32)
    for r in range(n_grp):
        copies[r].wait()
        att = atts[r][0] if len(atts[r].shape) == 3 else atts[r][...]
        mid = mid + att[q_width:].astype(F32)
        resid_ref[...] += dotg(att, buffer[r], 0, 0)
    mid_ref[...] = mid.astype(BF)
    resid = resid_ref[...]
    factor = lax.rsqrt(jnp.mean(resid * resid, axis=1, keepdims=True) + EPS)
    low_ref[...] = (resid * factor * gain_ref[...]).astype(BF)


def branch_kernel(n_grp, n_sum, info, dy_ref, resid_ref, gain_ref, mid_ref, *refs):
    summands, refs = refs[:n_sum], refs[n_sum:]
    weights, refs = refs[:n_grp], refs[n_grp:]
    d_resid_ref, wide_ref, refs = refs[0], refs[1], refs[2:]
    outs, (buffer, sems) = refs[:n_grp], refs[n_grp:]
    copies = [
        pltpu.make_async_copy(weights[r], buffer.at[r], sems.at[r]) for r in range(n_grp)
    ]
    for copy in copies:
        copy.start()
    d_in = summands[0][...].astype(F32)
    for summand in summands[1:]:
        d_in = d_in + summand[...].astype(F32)
    resid = resid_ref[...]
    factor = lax.rsqrt(jnp.mean(resid * resid, axis=1, keepdims=True) + EPS)
    e = gain_ref[...] * d_in
    slope = factor * factor * factor * jnp.mean(resid * e, axis=1, keepdims=True)
    d_resid = dy_ref[0].astype(F32) + factor * e - resid * slope
    d_resid_ref[...] = d_resid
    low = d_resid.astype(BF)
    wide_ref[...] = dotg(mid_ref[...], low, 1, 0)
    for r in range(n_grp):
        copies[r].wait()
        outs[r][...] = dotg(buffer[r], low, 1, 1).astype(BF)


def tokens_kernel(n_grp, info, x_ref, gain_ref, d_resid_ref, *refs):
    dqs, rests, weights = refs[:n_grp], refs[n_grp : 2 * n_grp], refs[2 * n_grp : 3 * n_grp]
    out_ref, buffer, total, sems = refs[3 * n_grp :][-4:]
    copies = [
        pltpu.make_async_copy(weights[r], buffer.at[r], sems.at[r]) for r in range(n_grp)
    ]
    for copy in copies:
        copy.start()
    for r in range(n_grp):
        copies[r].wait()
        d_q = dqs[r][0] if len(dqs[r].shape) == 3 else dqs[r][...]
        rest = rests[r][0] if len(rests[r].shape) == 3 else rests[r][...]
        part = dotg(jnp.concatenate([d_q, rest], axis=0), buffer[r], 0, 0)
        if r:
            total[...] += part
        else:
            total[...] = part
    x = x_ref[0].astype(F32)
    factor = lax.rsqrt(jnp.mean(x * x, axis=1, keepdims=True) + EPS)
    e = gain_ref[...] * total[...]
    slope = factor * factor * factor * jnp.mean(x * e, axis=1, keepdims=True)
    out_ref[0] = d_resid_ref[...] + factor * e - x * slope


def mlp_kernel(
    batch, rels, layout, sizes, first_half, info, *refs,
):
    n_parts = len(layout)
    n_grp = len(rels)
    xs, refs = refs[:n_grp], refs[n_grp:]
    dy_hbm, refs = refs[0], refs[1:]
    part_sets = []
    for _ in sizes:
        part_sets.append(refs[:n_parts])
        refs = refs[n_parts:]
    n_prev = 0 if first_half else 2
    prevs, refs = refs[:n_prev], refs[n_prev:]
    n_out = 2 if first_half else 2 * n_grp
    outs, refs = refs[:n_out], refs[n_out:]
    x, dy, w, acc_out, acc_in, sem, wsem = refs[:7]
    j, n = pl.program_id(0), pl.num_programs(0)
    slot = j % 2
    share = xs[0].shape[0]
    rows_all = x.shape[0]
    depth = layout[0][2]

    def loads(jj, s, which):
        copies = []
        first_step = sum(sizes[:which]) // CHUNK
        for (q, first, rows), part in zip(layout, part_sets[which]):
            to = pl.ds(pl.multiple_of(info[3 + q] * depth + first, 16), rows)
            for kind in range(3):
                column = pl.multiple_of(kind * sizes[which] + (jj - first_step) * CHUNK, CHUNK)
                copies.append(
                    pltpu.make_async_copy(
                        part.at[:, pl.ds(column, CHUNK)],
                        w.at[s, to, pl.ds(kind * CHUNK, CHUNK)],
                        wsem.at[s],
                    )
                )
        return copies

    def start_loads(jj, s):
        for which in range(len(sizes)):
            low, high = sum(sizes[:which]) // CHUNK, sum(sizes[: which + 1]) // CHUNK

            @pl.when((jj >= low) & (jj < high))
            def _(which=which):
                for copy in loads(jj, s, which):
                    copy.start()

    per_tile = ROW_TILE // share

    def inputs(tile):
        copies = []
        for r in range(tile * per_tile, (tile + 1) * per_tile):
            rows = pl.ds(r * share, share)
            copies.append(pltpu.make_async_copy(xs[r], x.at[rows], sem.at[tile]))
            there = pl.ds(pl.multiple_of((info[1] ^ rels[r]) * share, share), share)
            copies.append(pltpu.make_async_copy(dy_hbm.at[batch, there], dy.at[rows], sem.at[tile]))
        return copies

    tiles = rows_all // ROW_TILE

    def earlier():
        part = pl.ds(rels[0] * share, rows_all)
        return [
            pltpu.make_async_copy(prev.at[part], refs[7 + i], sem.at[tiles])
            for i, prev in enumerate(prevs)
        ]

    def results():
        if first_half:
            return [
                pltpu.make_async_copy(x, outs[0], sem.at[0]),
                pltpu.make_async_copy(dy, outs[1], sem.at[1]),
            ]
        copies = []
        for r in range(n_grp):
            rows = pl.ds(r * share, share)
            copies.append(pltpu.make_async_copy(x.at[rows], outs[r], sem.at[0]))
            copies.append(pltpu.make_async_copy(dy.at[rows], outs[n_grp + r], sem.at[0]))
        return copies

    @pl.when(j == 0)
    def _():
        for copy in inputs(0):
            copy.start()
        start_loads(j, 0)
        for tile in range(1, tiles):
            for copy in inputs(tile):
                copy.start()
        for copy in earlier():
            copy.start()

    @pl.when(j + 1 < n)
    def _():
        start_loads(j + 1, 1 - slot)

    for copy in loads(0, slot, 0):
        copy.wait()
    gate_up_w = w.at[slot, :, pl.ds(0, 2 * CHUNK)]
    down_w = w.at[slot, :, pl.ds(2 * CHUNK, CHUNK)]

    def body(tile, start, end):
        rows = pl.ds(pl.multiple_of(tile * ROW_TILE, ROW_TILE), ROW_TILE)
        if start:
            for i in range(per_tile):
                part = pl.ds(pl.multiple_of(tile * ROW_TILE + i * share, share), share)
                pltpu.make_async_copy(xs[0], x.at[part], sem.at[tile]).wait()
                pltpu.make_async_copy(xs[0], dy.at[part], sem.at[tile]).wait()
        gate_up = dotg(x[rows, :], gate_up_w[...], 1, 0)
        d_hidden = dotg(dy[rows, :], down_w[...], 1, 0)
        gate, up = gate_up[:, :CHUNK], gate_up[:, CHUNK:]
        sig = 1.0 / (1.0 + jnp.exp(-gate))
        act = gate * sig
        hidden = (act * up).astype(BF)
        d_gate = (d_hidden * up * (sig + act * (1.0 - sig))).astype(BF)
        d_up = (d_hidden * act).astype(BF)
        out = dotg(hidden, down_w[...], 1, 1)
        d_in = dotg(jnp.concatenate([d_gate, d_up], axis=1), gate_up_w[...], 1, 1)
        if start:
            acc_out[rows, :] = out
            acc_in[rows, :] = d_in
        elif not end:
            acc_out[rows, :] += out
            acc_in[rows, :] += d_in
        else:
            out, d_in = acc_out[rows, :] + out, acc_in[rows, :] + d_in
            if not first_half:
                d_in = d_in + refs[7][rows, :].astype(F32)
                out = out + refs[8][rows, :].astype(F32)
            x[rows, :] = d_in.astype(BF)
            dy[rows, :] = out.astype(BF)
        return 0

    @pl.when(j == 0)
    def _():
        lax.fori_loop(0, tiles, lambda i, c: body(i, True, False), 0)

    @pl.when((j > 0) & (j < n - 1))
    def _():
        lax.fori_loop(0, tiles, lambda i, c: body(i, False, False), 0)

    @pl.when(j == n - 1)
    def _():
        for copy in earlier():
            copy.wait()
        lax.fori_loop(0, tiles, lambda i, c: body(i, False, True), 0)
        for copy in results():
            copy.start()
        for copy in results():
            copy.wait()


def backward_kernel(
    batch, per, pairs, n_grp, has_prev, count, scale, info, table, q_ref, kv_ref, ve_ref, halo_ref, wq_ref,
    oin_ref, att_ref, w_ref, phi_ref, s_ref, r_ref, *refs,
):
    blocks_in, refs = refs[:n_grp], refs[n_grp:]
    prevs, refs = (refs[:1], refs[1:]) if has_prev else (None, refs)
    (
        dq_ref, dkv_ref, ds_ref, ends_ref, back_ref, map_ref, carry, kv_all, ve_all, d_outs, sem,
    ) = refs
    step = pl.program_id(0)
    pair = pairs - 1 - step
    heads = kv_ref.shape[1] // PAIR
    slots = Slots(table, batch, 2 * pairs, count)
    block = 2 * pair
    q_width = q_ref.shape[0]
    per_block = blocks_in[0].shape[1] // PAIR

    @pl.when(step == 0)
    def _():
        copies = []
        for r in range(n_grp):
            for i in range(per_block):
                copies.append(
                    pltpu.make_async_copy(
                        blocks_in[r].at[:, pl.ds(i * PAIR, PAIR)],
                        d_outs.at[(info[1] ^ r) * per_block + i],
                        sem,
                    )
                )
        for copy in copies:
            copy.start()
        fill_window(batch, kv_ref, ve_ref, halo_ref, kv_all, ve_all)
        carry[...] = jnp.zeros_like(carry)
        dkv_ref[...] = jnp.zeros_like(dkv_ref)
        map_ref[...] = prevs[0][...] if has_prev else jnp.zeros_like(map_ref)
        for copy in copies:
            copy.wait()
    one_b = slots.weight_one(block + 1)
    one_c = slots.weight_one(block + 2)
    lanes = per * PAIR
    low = half_mask((EXT, lanes))
    rows = pl.ds(pl.multiple_of(pair * PAIR, PAIR), WIN)
    d_out = d_outs[pair]
    back_out = ADAPTER_SCALE * d_out[q_width:]
    d_att_all = d_out[:q_width].astype(F32) + dotg(oin_ref[...], back_out, 1, 0)
    for k in range(heads):
        kv = kv_all[rows, k * PAIR : (k + 1) * PAIR]
        ve = ve_all[rows, k * PAIR : (k + 1) * PAIR]
        base = k * per * STRETCH

        def side(value):
            return jnp.concatenate(
                [value[g * STRETCH : (g + 1) * STRETCH] for g in range(per)], axis=1
            )

        stacked = q_ref[base : base + per * STRETCH, :]
        q = side(stacked)
        d_att = side(d_att_all[base : base + per * STRETCH])
        att = side(att_ref[0, base : base + per * STRETCH, :]).astype(F32)
        inverse = jnp.concatenate(
            [r_ref[0, k * per + g : k * per + g + 1, :] for g in range(per)], axis=1
        )
        ratio = d_att * inverse
        d_den = -jnp.sum(ratio * att, axis=0, keepdims=True)
        d_high = d_den.astype(BF).astype(F32)
        row = lax.broadcasted_iota(jnp.int32, (EXT - STRETCH, lanes), 0)
        extra = jnp.where(row == 0, d_high, jnp.where(row == 1, d_den - d_high, 0.0))
        ratio_ext = jnp.concatenate([ratio, extra], axis=0)
        ratio_low = ratio_ext.astype(BF)
        weights = w_ref[0, k]
        padded = jnp.concatenate([ratio_low, jnp.zeros((PAIR - EXT, lanes), BF)], axis=0)
        d_weights = dotg(ve, padded, 1, 0)
        d_scores = (d_weights * weights.astype(F32)).astype(BF)
        d_query = dotg(kv, d_scores, 0, 0)[:STRETCH] * scale
        zeros = jnp.zeros((STRETCH, lanes), BF)
        q_scaled = (q.astype(F32) * scale).astype(BF)
        d_kv = dotg(d_scores, jnp.concatenate([q_scaled, zeros], axis=0), 1, 1) + dotg(
            weights, jnp.concatenate([zeros, ratio_low[:STRETCH]], axis=0), 1, 1
        )
        dkv_ref[rows, k * PAIR : (k + 1) * PAIR] += d_kv
        phi = phi_ref[0, k]
        both = jnp.concatenate(
            [jnp.where(low, ratio_ext, 0.0), jnp.where(low, 0.0, ratio_ext)], axis=0
        ).astype(BF)
        d_phi = dotg(s_ref[0, k], both, 0, 0)
        d_state = dotg(both, phi, 1, 1)
        ds_ref[0, k] = d_state
        d_mixed = feature_back(phi, d_phi).astype(BF)
        d_mixed = jnp.concatenate(
            [d_mixed[:, g * PAIR : (g + 1) * PAIR] for g in range(per)], axis=0
        )
        d_stacked = jnp.concatenate(
            [d_query[:, g * PAIR : (g + 1) * PAIR] for g in range(per)], axis=0
        ) + dotg(wq_ref[k], d_mixed, 0, 0)
        dq_ref[0, base : base + per * STRETCH, :] = d_stacked.astype(BF)
        map_ref[k] += dotg(stacked, d_mixed, 1, 1)
        rest = d_state[EXT:] + one_c * carry[k]
        head = d_state[:EXT] + one_b * rest
        carry[k] = head
        ends_ref[k, 0] = rest.astype(BF)
        ends_ref[k, 1] = head.astype(BF)

    @pl.when(step == pairs - 1)
    def _():
        back_ref[...] = dkv_ref[:STRETCH, :].astype(BF)


def keys_kernel(
    batch, pairs, per_block, wide_y, count, n_far, has_prev, info, table, kv_ref, ve_ref, wk_ref,
    phi_ref, dkv_ref, back_ref, ds_ref, dq_ref, q_up_ref, kv_up_ref, *refs,
):
    fars, refs = refs[:n_far], refs[n_far:]
    prevs, refs = (refs[:1], refs[1:]) if has_prev else (None, refs)
    out_ref, map_ref, carry = refs
    step = pl.program_id(0)
    pair = pairs - 1 - step
    heads = kv_ref.shape[1] // PAIR
    slots = Slots(table, batch, 2 * pairs, count)
    block = 2 * pair

    @pl.when(step == 0)
    def _():
        for k in range(heads):
            inner, outer = entering(slots, fars, wide_y, count, -1, batch, k)
            carry[k, 0] = outer
            carry[k, 1] = inner
        map_ref[...] = prevs[0][...] if has_prev else jnp.zeros_like(map_ref)

    one_b = slots.weight_one(block + 1)
    one_c = slots.weight_one(block + 2)
    two_c = slots.weight_two(block + 2)
    two_d = slots.weight_two(block + 3)
    row = lax.broadcasted_iota(jnp.int32, (PAIR, PAIR), 0)
    lane = lax.broadcasted_iota(jnp.int32, (PAIR, PAIR), 1)
    last = jnp.where(step == 0, 1.0, 0.0)
    rows = pl.ds(pl.multiple_of(pair * PAIR + STRETCH, STRETCH), PAIR)
    d_kvs = []
    for k in range(heads):
        kv = kv_ref[:, k * PAIR : (k + 1) * PAIR]
        ve = ve_ref[:, k * PAIR : (k + 1) * PAIR].astype(F32)
        next_one, next_two = carry[k, 0], carry[k, 1]
        pad = jnp.zeros((PAIR - EXT, PAIR), F32)
        grads = jnp.concatenate([next_one * two_c, pad, next_two * two_d, pad], axis=0).astype(BF)
        both = jnp.concatenate(
            [jnp.where(row < STRETCH, ve, 0.0), jnp.where(row < STRETCH, 0.0, ve)], axis=1
        ).astype(BF)
        d_phi = dotg(grads, both, 0, 1)
        phi = phi_ref[k * PAIR : (k + 1) * PAIR, :]
        d_both = dotg(phi, grads, 0, 1)
        d_value = jnp.where(row < STRETCH, d_both[:, :PAIR], d_both[:, PAIR:])
        d_value = jnp.where(lane < STRETCH, 0.0, pltpu.roll(d_value, STRETCH, 1))
        d_mixed = feature_back(phi, d_phi).astype(BF)
        d_key = dotg(d_mixed, wk_ref[k], 0, 0)
        map_ref[k] += dotg(kv, d_mixed, 0, 1)
        total = dkv_ref[rows, k * PAIR : (k + 1) * PAIR] + d_value + d_key
        returned = back_ref[batch, :, k * PAIR : (k + 1) * PAIR].astype(F32) * last
        total = total + jnp.concatenate([jnp.zeros_like(returned), returned], axis=0)
        d_kvs.append(jnp.transpose(total).astype(BF))
        state = ds_ref[0, k]
        rest = state[EXT:] + one_c * next_one
        carry[k, 1] = rest
        carry[k, 0] = state[:EXT] + one_b * rest
    d_kv = jnp.concatenate(d_kvs, axis=0)
    lanes = pl.ds(pl.multiple_of(pair % per_block * PAIR, PAIR), PAIR)
    out_ref[(pair // per_block) ^ info[1], 32:, lanes] = d_kv

    @pl.when(step == pairs - 1)
    def _():
        for r in range(out_ref.shape[0]):
            back_in = dotg(q_up_ref[...], dq_ref[r], 1, 0) + dotg(
                kv_up_ref[...], out_ref[r, 32:, :], 1, 0
            )
            out_ref[r, :32, :] = (ADAPTER_SCALE * back_in).astype(BF)


def adapter_kernel(
    n_grp, info, dq_ref, rest_ref, mid_ref, normed_ref, att_ref, *refs
):
    blocks_in, (up_ref, oin_ref, wide_ref) = refs[:n_grp], refs[n_grp:]
    share = blocks_in[0].shape[1]
    q_width = dq_ref.shape[1]
    for r in range(n_grp):
        there = pl.ds(pl.multiple_of((info[1] ^ r) * share, share), share)
        mids = mid_ref[:, there]
        rest = rest_ref[r]
        both = jnp.concatenate([dq_ref[r], rest], axis=0)
        up = dotg(mids, both, 1, 1)
        oin = dotg(ADAPTER_SCALE * blocks_in[r][q_width:], att_ref[r, :q_width, :], 1, 1)
        wide = dotg(rest[:32], normed_ref[there, :], 1, 0)
        up_ref[...] = up if r == 0 else up_ref[...] + up
        oin_ref[...] = oin if r == 0 else oin_ref[...] + oin
        wide_ref[...] = wide if r == 0 else wide_ref[...] + wide


def pack_early_kernel(per, map_ref, oin_a, oin_b, out_ref):
    heads = map_ref.shape[0]
    at = 0
    for k in range(heads):
        for g in range(0, per, 2):
            pair = [
                map_ref[k, h * STRETCH : (h + 1) * STRETCH, h * STRETCH : (h + 1) * STRETCH]
                for h in (g, g + 1)
            ]
            out_ref[at : at + STRETCH, :] = jnp.concatenate(pair, axis=1).astype(BF)
            at += STRETCH
    oin = oin_a[...] + oin_b[...]
    for c in range(oin.shape[1] // PAIR):
        out_ref[at : at + 16, :] = oin[:, c * PAIR : (c + 1) * PAIR].astype(BF)
        at += 16


def pack_late_kernel(
    q_width, up_a, up_b, key_ref, wide_in_a, wide_in_b, wide_out_a, wide_out_b, wide_ref, out_ref
):
    for c in range(wide_in_a.shape[1] // PAIR):
        cols = slice(c * PAIR, (c + 1) * PAIR)
        wide_in = wide_in_a[:24, cols] + wide_in_b[:24, cols]
        wide_out = wide_out_a[:8, cols] + wide_out_b[:8, cols]
        wide_ref[c * 32 : (c + 1) * 32, :] = jnp.concatenate([wide_in, wide_out], axis=0).astype(BF)
    up = ADAPTER_SCALE * (up_a[...] + up_b[...])
    at = 0
    for c in range(q_width // PAIR):
        out_ref[at : at + 16, :] = up[:16, c * PAIR : (c + 1) * PAIR].astype(BF)
        at += 16
    for k in range(key_ref.shape[0]):
        first = q_width + 32 + k * PAIR
        out_ref[at : at + 16, :] = up[8:24, first : first + PAIR].astype(BF)
        at += 16
    for k in range(key_ref.shape[0]):
        block = key_ref[k, :STRETCH, :]
        out_ref[at : at + STRETCH, :] = jnp.concatenate([block, block], axis=1).astype(BF)
        at += STRETCH


def unpack_kernel(
    n_grp, columns, info, early_a, early_b, late_a, late_b,
    wide_ref, q_ref, kv_ref, oin_ref, map_ref, key_ref, turned,
):
    early = early_a[...].astype(F32) + early_b[...].astype(F32)
    at = 0
    for h in range(0, map_ref.shape[0], 2):
        map_ref[h] = early[at : at + STRETCH, :STRETCH]
        map_ref[h + 1] = early[at : at + STRETCH, STRETCH:]
        at += STRETCH
    for c in range(oin_ref.shape[1] // PAIR):
        oin_ref[:, c * PAIR : (c + 1) * PAIR] = early[at : at + 8, :]
        at += 16
    first = (info[2] * n_grp + info[1]) * columns
    rows = pl.ds(pl.multiple_of((first // PAIR) * 32, 32), 32)
    sums = late_a[rows, :].astype(F32) + late_b[rows, :].astype(F32)
    turned[...] = jnp.transpose(sums)
    wide_ref[...] = turned[pl.ds(pl.multiple_of(first % PAIR, 8), columns), :]
    at = late_a.shape[0] - sum(
        [q_ref.shape[1] // PAIR * 16, key_ref.shape[0] * 16, key_ref.shape[0] * STRETCH]
    )
    late = late_a[at:, :].astype(F32) + late_b[at:, :].astype(F32)
    at = 0
    for c in range(q_ref.shape[1] // PAIR):
        q_ref[:, c * PAIR : (c + 1) * PAIR] = late[at : at + 8, :]
        at += 16
    for k in range(key_ref.shape[0]):
        cols = slice(k * STRETCH, (k + 1) * STRETCH)
        kv_ref[0, :, cols] = late[at : at + 8, :STRETCH]
        kv_ref[1, :, cols] = late[at + 8 : at + 16, STRETCH:]
        at += 16
    for k in range(key_ref.shape[0]):
        key_ref[k] = late[at : at + STRETCH, :STRETCH]
        at += STRETCH


def whole(shape):
    return pl.BlockSpec(shape, lambda i, *_: (0,) * len(shape))


def anywhere():
    return pl.BlockSpec(memory_space=pl.ANY)


def sds(shape, kind):
    return jax.ShapeDtypeStruct(shape, kind)


def call(
    kernel, name, grid, scalars, ins, in_specs, out_specs, out_shape, scratch=(), alias=None
):
    return pl.pallas_call(
        kernel,
        grid_spec=pltpu.PrefetchScalarGridSpec(
            num_scalar_prefetch=len(scalars),
            grid=(grid,),
            in_specs=in_specs,
            out_specs=out_specs,
            scratch_shapes=list(scratch),
        ),
        out_shape=out_shape,
        input_output_aliases=alias or {},
        cost_estimate=pl.CostEstimate(flops=0, transcendentals=0, bytes_accessed=1024),
        compiler_params=pltpu.CompilerParams(
            dimension_semantics=("arbitrary",), vmem_limit_bytes=VMEM_LIMIT
        ),
        name=name,
    )(*scalars, *ins)


def run_assemble(info, ring, splits):
    shape = ring.parts[0].shape
    parts_of = ring_layout(ring.count, shape[0])
    outs = [(size, shape[1] * ring.count) for size in splits]
    return call(
        functools.partial(assemble_kernel, parts_of, shape[1], splits), "assemble", 1, [info],
        ring.parts, [whole(part.shape) for part in ring.parts], [whole(out) for out in outs],
        [sds(out, BF) for out in outs],
    )


def run_layout(info, lens, blocks):
    count = lax.axis_size("seq")
    size = lens.shape[0] * TABLE_ROWS * table_width(blocks, count)
    return call(
        functools.partial(layout_kernel, blocks, max(1, count // 4), count), "layout", 1,
        [info, lens], [], [], pl.BlockSpec(memory_space=pltpu.SMEM), sds((size,), jnp.int32),
    )


def run_layer(table, ends, sign):
    count = lax.axis_size("seq")
    batches, heads = ends[0].shape[:2]
    out = sds((batches, heads, EXT, PAIR), BF)
    per_batch = table.shape[0] // batches // TABLE_ROWS
    blocks = max(per_batch - 4, 0)
    return call(
        functools.partial(layer_kernel, sign, blocks, count, len(ends)), "layer", 1, [table], ends,
        [whole(item.shape) for item in ends], [whole(out.shape)] * 2, [out] * 2,
    )


def run_project(table, batch, normed, weight, q_up, kv_up, maps):
    rows, model = normed.shape
    heads = maps.shape[0]
    width = heads * PAIR
    q_width = weight.shape[0] - 32 - width
    tile = 2 * PAIR
    pairs = rows // PAIR
    return call(
        functools.partial(
            project_kernel, batch, q_width, rows // STRETCH, lax.axis_size("seq")
        ),
        "project_states", rows // tile, [table],
        [normed, weight, q_up, kv_up, maps],
        [
            pl.BlockSpec((tile, model), lambda i, *_: (i, 0)),
            whole(weight.shape), whole(q_up.shape), whole(kv_up.shape), whole(maps.shape),
        ],
        [
            pl.BlockSpec((q_width, tile), lambda i, *_: (0, i)),
            pl.BlockSpec((tile, width), lambda i, *_: (i, 0)),
            pl.BlockSpec((tile, width), lambda i, *_: (i, 0)),
            pl.BlockSpec((32, tile), lambda i, *_: (0, i)),
            pl.BlockSpec((width, tile), lambda i, *_: (0, i)),
            pl.BlockSpec((2, heads, 2 * EXT, PAIR), lambda i, *_: (i, 0, 0, 0)),
            whole((heads, 2, EXT, PAIR)),
            whole((STRETCH, 2 * width)),
        ],
        [
            sds((q_width, rows), BF),
            sds((rows, width), BF),
            sds((rows, width), BF),
            sds((32, rows), BF),
            sds((width, rows), BF),
            sds((pairs, heads, 2 * EXT, PAIR), F32),
            sds((heads, 2, EXT, PAIR), BF),
            sds((STRETCH, 2 * width), BF),
        ],
        [pltpu.VMEM((heads, EXT, PAIR), F32)],
    )


def run_forward(info, table, batch, q, kv, ve, halo, maps, o_in, states, fars):
    q_width, rows = q.shape
    width = kv.shape[1]
    heads, pairs = width // PAIR, rows // PAIR
    per = q_width // STRETCH // heads
    count = lax.axis_size("seq")
    wide = max(1, count // 4)
    scale = STRETCH ** (-0.5) * math.log2(math.e)
    step = lambda *shape: pl.BlockSpec((1,) + shape, lambda i, *_: (i,) + (0,) * len(shape))
    column = lambda n: pl.BlockSpec((n, PAIR), lambda i, *_: (0, i))
    share = rows // lax.axis_size("grp")
    return call(
        functools.partial(
            forward_kernel, batch, per, rows // STRETCH, wide, count, len(fars), scale
        ),
        "attention_forward", pairs, [info, table],
        [q, kv, ve, halo, maps, o_in, states, *fars],
        [
            column(q_width), whole(kv.shape), whole(ve.shape), whole(halo.shape),
            whole(maps.shape), whole(o_in.shape), step(heads, 2 * EXT, PAIR),
            *[whole(far.shape) for far in fars],
        ],
        [
            block_spec(q_width + 16, share, lambda i: i), step(heads, WIN, per * PAIR),
            step(heads, PAIR, per * PAIR), step(heads, 2 * EXT, PAIR), step(heads * per, PAIR),
        ],
        [
            sds((rows // share, q_width + 16, share), BF),
            sds((pairs, heads, WIN, per * PAIR), BF),
            sds((pairs, heads, PAIR, per * PAIR), BF),
            sds((pairs, heads, 2 * EXT, PAIR), BF),
            sds((pairs, heads * per, PAIR), F32),
        ],
        [
            pltpu.VMEM((heads, 2, EXT, PAIR), F32),
            pltpu.VMEM((rows + STRETCH, width), BF),
            pltpu.VMEM((rows + STRETCH, width), BF),
        ],
    )


def block_spec(height, share, pair_of):
    per_block = share // PAIR
    return pl.BlockSpec(
        (1, height, PAIR),
        lambda i, info, *_: ((pair_of(i) // per_block) ^ info[1], 0, pair_of(i) % per_block),
    )


def own_spec(batch, share, model):
    return pl.BlockSpec((1, share, model), lambda i, info: (batch, info[1], 0))


def front(array):
    if len(array.shape) == 2:
        return whole(array.shape)
    return pl.BlockSpec((1,) + array.shape[1:], lambda i, *_: (0, 0, 0))


def run_residual(info, batch, tokens, gain, atts, weights):
    n_grp = len(atts)
    model = tokens.shape[2]
    share = atts[0].shape[-1]
    return call(
        functools.partial(residual_kernel, n_grp), "residual", 1, [info],
        [tokens, gain, *atts, *weights],
        [own_spec(batch, share, model), whole(gain.shape), *[front(att) for att in atts]]
        + [anywhere()] * n_grp,
        [whole((share, model)), whole((share, model)), whole((16, share))],
        [sds((share, model), F32), sds((share, model), BF), sds((16, share), BF)],
        [
            pltpu.VMEM((n_grp,) + weights[0].shape, BF),
            pltpu.SemaphoreType.DMA((n_grp,)),
        ],
    )


def run_branch(info, batch, cotangent, resid, gain, mid, summands, weights):
    n_grp = len(weights)
    share, model = resid.shape
    out = (weights[0].shape[0], share)
    return call(
        functools.partial(branch_kernel, n_grp, len(summands)), "branch_gradient", 1, [info],
        [cotangent, resid, gain, mid, *summands, *weights],
        [
            own_spec(batch, share, model), whole(resid.shape), whole(gain.shape),
            whole(mid.shape), *[whole(resid.shape) for _ in summands],
        ]
        + [anywhere()] * n_grp,
        [whole((share, model)), whole((16, model))] + [whole(out)] * n_grp,
        [sds((share, model), F32), sds((16, model), F32)] + [sds(out, BF)] * n_grp,
        [
            pltpu.VMEM((n_grp,) + weights[0].shape, BF),
            pltpu.SemaphoreType.DMA((n_grp,)),
        ],
    )


def run_tokens(info, batch, tokens, gain, d_resid, dqs, rests, weights, prev):
    n_grp = len(weights)
    batches, _, model = tokens.shape
    share = d_resid.shape[0]
    ins = [tokens, gain, d_resid, *dqs, *rests, *weights]
    specs = [
        own_spec(batch, share, model), whole(gain.shape), whole(d_resid.shape),
        *[front(a) for a in [*dqs, *rests]],
    ] + [anywhere()] * n_grp
    alias = {}
    if prev is not None:
        alias = {len(ins) + 1: 0}
        ins.append(prev)
        specs.append(anywhere())
    return call(
        functools.partial(tokens_kernel, n_grp), "token_gradient", 1, [info], ins, specs,
        pl.BlockSpec((1, share, model), lambda i, *_: (batch, 0, 0)),
        sds((batches, share, model), F32),
        [
            pltpu.VMEM((n_grp,) + weights[0].shape, BF),
            pltpu.VMEM((share, model), F32),
            pltpu.SemaphoreType.DMA((n_grp,)),
        ],
        alias,
    )


def run_mlp(info, batch, xs, rels, cotangent, rings, prevs, sizes):
    n_grp = len(xs)
    share, model = xs[0].shape
    rows = share * n_grp
    depth = rings[0].parts[0].shape[0]
    layout = ring_layout(rings[0].count, depth)
    first = prevs is None
    prevs = [] if first else list(prevs)
    ins = [*xs, cotangent, *[part for ring in rings for part in ring.parts], *prevs]
    if first:
        out_shape = [sds((rows, model), BF)] * 2
    else:
        out_shape = [sds((share, model), BF)] * (2 * n_grp)
    scratch = [
        pltpu.VMEM((rows, model), BF),
        pltpu.VMEM((rows, model), BF),
        pltpu.VMEM((2, model, 3 * CHUNK), BF),
        pltpu.VMEM((rows, model), F32),
        pltpu.VMEM((rows, model), F32),
        pltpu.SemaphoreType.DMA((rows // ROW_TILE + 1,)),
        pltpu.SemaphoreType.DMA((2,)),
    ] + [pltpu.VMEM((rows, model), BF) for _ in prevs]
    return call(
        functools.partial(mlp_kernel, batch, rels, layout, sizes, first),
        "feed_forward", sum(sizes) // CHUNK, [info], ins, [anywhere()] * len(ins),
        [anywhere()] * len(out_shape), out_shape, scratch,
    )


def run_backward(
    info, table, batch, q, kv, ve, halo, maps, o_in, att, weights, phi, states, inverse, d_outs, prevs,
):
    q_width, rows = q.shape
    width = kv.shape[1]
    heads, pairs = width // PAIR, rows // PAIR
    per = q_width // STRETCH // heads
    share = rows // len(d_outs)
    rev = lambda i: pairs - 1 - i
    step = lambda *shape: pl.BlockSpec((1,) + shape, lambda i, *_: (rev(i),) + (0,) * len(shape))
    column = lambda n: pl.BlockSpec((n, PAIR), lambda i, *_: (0, rev(i)))
    prevs = list(prevs or [])
    sums = [sds(maps.shape, F32)]
    return call(
        functools.partial(
            backward_kernel, batch, per, pairs, len(d_outs), bool(prevs), lax.axis_size("seq"),
            STRETCH ** (-0.5),
        ),
        "attention_backward", pairs, [info, table],
        [q, kv, ve, halo, maps, o_in, att, weights, phi, states, inverse, *d_outs, *prevs],
        [
            column(q_width), whole(kv.shape), whole(ve.shape), whole(halo.shape),
            whole(maps.shape), whole(o_in.shape), block_spec(q_width + 16, share, rev),
            step(heads, WIN, per * PAIR), step(heads, PAIR, per * PAIR),
            step(heads, 2 * EXT, PAIR), step(heads * per, PAIR),
            *[anywhere() for _ in d_outs], *[whole(prev.shape) for prev in prevs],
        ],
        [
            block_spec(q_width, share, rev), whole((rows + STRETCH, width)), step(heads, 2 * EXT, PAIR),
            whole((heads, 2, EXT, PAIR)), whole((STRETCH, width)),
            *[whole(item.shape) for item in sums],
        ],
        [
            sds((rows // share, q_width, share), BF),
            sds((rows + STRETCH, width), F32),
            sds((pairs, heads, 2 * EXT, PAIR), F32),
            sds((heads, 2, EXT, PAIR), BF),
            sds((STRETCH, width), BF),
            *sums,
        ],
        [
            pltpu.VMEM((heads, EXT, PAIR), F32),
            pltpu.VMEM((rows + STRETCH, width), BF),
            pltpu.VMEM((rows + STRETCH, width), BF),
            pltpu.VMEM((pairs, q_width + 16, PAIR), BF),
            pltpu.SemaphoreType.DMA,
        ],
    )


def run_keys(
    info, table, batch, kv, ve, maps, phi, d_kv, returned, d_states, d_q, q_up, kv_up, fars, prevs,
):
    width, rows = phi.shape
    heads, pairs = width // PAIR, rows // PAIR
    n_grp, q_width, share = d_q.shape
    count = lax.axis_size("seq")
    wide = max(1, count // 4)
    rev = lambda i: pairs - 1 - i
    column = lambda n: pl.BlockSpec((n, PAIR), lambda i, *_: (0, rev(i)))
    lines = lambda n: pl.BlockSpec((PAIR, n), lambda i, *_: (rev(i), 0))
    prevs = list(prevs or [])
    sums = [sds((heads, PAIR, STRETCH), F32)]
    return call(
        functools.partial(
            keys_kernel, batch, pairs, share // PAIR, wide, count, len(fars), bool(prevs)
        ),
        "attention_keys", pairs, [info, table],
        [
            kv, ve, maps, phi, d_kv, returned, d_states, d_q, q_up, kv_up, *fars, *prevs,
        ],
        [
            lines(width), lines(width), whole(maps.shape), column(width), whole(d_kv.shape),
            whole(returned.shape),
            pl.BlockSpec((1, heads, 2 * EXT, PAIR), lambda i, *_: (rev(i), 0, 0, 0)),
            whole(d_q.shape), whole(q_up.shape), whole(kv_up.shape),
            *[whole(far.shape) for far in fars], *[whole(prev.shape) for prev in prevs],
        ],
        [whole((n_grp, 32 + width, share)), *[whole(item.shape) for item in sums]],
        [sds((n_grp, 32 + width, share), BF), *sums],
        [pltpu.VMEM((heads, 2, EXT, PAIR), F32)],
    )


def run_adapters(info, d_q, rest, mids, normed, att, d_outs):
    model = normed.shape[1]
    ins = [d_q, rest, mids, normed, att, *d_outs]
    out_shape = [
        sds((32, d_q.shape[1] + rest.shape[1]), F32), sds((16, d_q.shape[1]), F32),
        sds((32, model), F32),
    ]
    return call(
        functools.partial(adapter_kernel, len(d_outs)),
        "adapter_gradients", 1, [info], ins, [whole(item.shape) for item in ins],
        [whole(item.shape) for item in out_shape], out_shape,
    )


def run_plain(kernel, name, scalars, ins, out_shape, scratch=()):
    return call(
        kernel, name, 1, scalars, ins, [whole(item.shape) for item in ins],
        [whole(item.shape) for item in out_shape], out_shape, scratch,
    )


def group_sum(value):
    total = value.astype(F32)
    for r in range(1, lax.axis_size("grp")):
        total = total + flip(value, "grp", r).astype(F32)
    return total.astype(BF)


def local(
    tokens,
    cotangent,
    lengths,
    attention_norm_gain,
    feedforward_norm_gain,
    query_weight,
    keyvalue_weight,
    output_weight,
    gate_up_weight,
    down_weight,
    adapter_width_factor,
    query_up_factor,
    keyvalue_up_factor,
    output_input_factor,
    query_feature_weight,
    key_feature_weight,
):
    batches, rows, model = tokens.shape
    n_seq, n_grp = lax.axis_size("seq"), lax.axis_size("grp")
    group_index, seq_index = lax.axis_index("grp"), lax.axis_index("seq")
    share = rows // n_grp
    rank = adapter_width_factor.shape[2]
    depth, q_width = query_weight.shape
    kv_heads = key_feature_weight.shape[0]
    kv_width = kv_heads * PAIR
    per = query_feature_weight.shape[0] // kv_heads
    hidden_width = down_weight.shape[0]
    gain_attn = attention_norm_gain.astype(F32)[None]
    gain_mlp = feedforward_norm_gain.astype(F32)[None]

    sources = lax.dynamic_index_in_dim(
        jnp.asarray(ring_sources(n_seq), jnp.int32), seq_index, 0, False
    )
    info = jnp.concatenate(
        [jnp.stack([seq_index * (rows // STRETCH), group_index, seq_index]).astype(jnp.int32), sources]
    )

    kv_shard = (
        keyvalue_weight.reshape(depth, 2, kv_heads, STRETCH)
        .transpose(2, 1, 3, 0)
        .reshape(kv_width, depth)
    )
    adapters = adapter_width_factor.transpose(0, 2, 1)
    pad = jnp.zeros((rank, depth), BF)
    in_ring = Ring(
        jnp.concatenate(
            [
                query_weight.T, adapters[:3].reshape(3 * rank, depth), pad, kv_shard,
                output_weight, adapters[3], pad,
            ],
            axis=0,
        )
    )
    down_t = down_weight.T
    half_shards = [
        jnp.concatenate(
            [
                gate_up_weight[:, 0, first : first + size],
                gate_up_weight[:, 1, first : first + size],
                down_t[:, first : first + size],
            ],
            axis=1,
        )
        for first, size in pieces_of(hidden_width)
    ]
    ring_a, ring_c = [Ring(shard) for shard in half_shards]
    kv_parts = keyvalue_up_factor.reshape(2, rank, kv_heads, STRETCH)
    kv_up = jnp.zeros((2, rank, kv_heads, 2, STRETCH), BF)
    kv_up = kv_up.at[0, :, :, 0].set(kv_parts[0]).at[1, :, :, 1].set(kv_parts[1])
    kv_up = kv_up.reshape(2 * rank, kv_width)
    kv_up = jnp.concatenate(
        [jnp.zeros((rank, kv_width), BF), kv_up, jnp.zeros((rank, kv_width), BF)]
    )
    q_up = jnp.concatenate([query_up_factor, jnp.zeros((3 * rank, q_width), BF)])
    q_up_t = q_up.T
    o_in = jnp.concatenate([output_input_factor, jnp.zeros((q_width, rank), BF)], axis=1)
    maps_t = query_feature_weight.transpose(0, 2, 1).reshape(kv_heads, per, STRETCH, STRETCH)
    query_maps = jnp.zeros((kv_heads, per, STRETCH, per, STRETCH), BF)
    for g in range(per):
        query_maps = query_maps.at[:, g, :, g, :].set(maps_t[:, g])
    query_maps = query_maps.reshape(kv_heads, per * STRETCH, per * STRETCH)
    key_maps = jnp.concatenate(
        [key_feature_weight.transpose(0, 2, 1), jnp.zeros((kv_heads, STRETCH, STRETCH), BF)], axis=2
    )

    normed_rows = []
    for batch in range(batches):
        x = tokens[batch].astype(F32)
        factor = lax.rsqrt(jnp.mean(x * x, axis=-1, keepdims=True) + EPS)
        normed_rows.append((x * factor * gain_attn).astype(BF))
    in_ring.hop()
    in_ring.hop()
    table = run_layout(info, lengths, rows // STRETCH)
    table, query_maps, key_maps, kv_up, q_up_t, normed_rows[0] = in_ring.tie(
        table, query_maps, key_maps, kv_up, q_up_t, normed_rows[0]
    )
    in_ring.hop()
    normed_rows[1] = in_ring.tie(normed_rows[1])[0]
    while in_ring.done < in_ring.hops():
        in_ring.hop()
    ring_a.hop(*in_ring.parts[-2:])
    weight_in, weight_out = run_assemble(
        info, in_ring, [q_width + 32 + kv_width, q_width + 2 * rank]
    )
    far_out = far_gather(weight_out)

    saved = []
    for batch in range(batches):
        normed = normed_rows[batch]
        q, kv, ve, mids, phi_key, states, ends, halo = run_project(
            table, batch, normed, weight_in, q_up_t, kv_up, key_maps
        )
        saved.append([q, kv, ve, mids, normed, phi_key, states, ends, halo])
    ends = jnp.stack([item[7] for item in saved])
    halo = jnp.stack([item[8] for item in saved])
    (ends,) = ring_a.tie(ends)
    fars, halo = exchange(table, ends, halo, 1)
    for item in saved:
        item[7:] = [fars, halo]
    ring_a.hop(*fars[1:], halo)

    attended, att_sets, far_mlp, mlp_ins = [], [], [], []
    for batch in range(batches):
        q, kv, ve, mids, normed, phi_key, states, fars, halo = saved[batch]
        if batch:
            q = after(q, att)
        att, weights, phi, sums, inverse = run_forward(
            info, table, batch, q, kv, ve, halo, query_maps, o_in, states, fars
        )
        atts = group_exchange([att[r] for r in range(n_grp)])
        att_sets.append([att, *atts[1:]])
        attended.append([att, weights, phi, sums, inverse])
    far_out = [far_out[0]] + [after(far, attended[0][0]) for far in far_out[1:]]
    weights_out = near_gather(far_out)
    att_sets[0][0] = after(att_sets[0][0], att_sets[1][0])
    for batch in range(batches):
        if batch:
            att_sets[1][0] = after(att_sets[1][0], mlp_in)
        resid, mlp_in, mid = run_residual(
            info, batch, tokens, gain_mlp, att_sets[batch], weights_out
        )
        attended[batch] += [resid, mid]
        (mlp_in,) = ring_a.tie(mlp_in)
        ring_a.hop()
        far_mlp.append(far_gather(mlp_in))
    ring_a.finish()
    held = ring_a.parts[-2:]
    held = lax.optimization_barrier((*far_mlp[0], *far_mlp[1], *held))
    far_mlp = [list(held[: len(far_mlp[0])]), list(held[len(far_mlp[0]) : 2 * len(far_mlp[0])])]
    ring_c.hop(held[0])
    for batch in range(batches):
        mlp_ins.append(near_gather(far_mlp[batch]))

    sizes = [size for _, size in pieces_of(hidden_width)]
    partial = [None] * batches
    every = list(range(n_grp))
    partial[0] = list(
        run_mlp(info, 0, mlp_ins[0], every, cotangent, [ring_a], None, sizes[:1])
    )
    partial[0][0], mlp_ins[1][0] = ring_c.tie(partial[0][0], mlp_ins[1][0])
    ring_c.hop()
    far_in = far_gather(after(weight_in, partial[0][0], *mlp_ins[1][2:]))
    partial[1] = list(
        run_mlp(info, 1, mlp_ins[1], every, cotangent, [ring_a], None, sizes[:1])
    )
    (partial[1][0],) = ring_c.tie(partial[1][0])
    ring_c.hop()
    ring_c.finish()
    far_in, partial[0][0] = lax.optimization_barrier((far_in, partial[0][0]))
    weights_in = near_gather(far_in)
    partial[0] = list(
        run_mlp(info, 0, mlp_ins[0], every, cotangent, [ring_c], partial[0], sizes[1:])
    )
    started = [scatter_start(partial[0][:n_grp])]
    started[0][0][0], partial[1][0] = lax.optimization_barrier((started[0][0][0], partial[1][0]))
    def run_branch_of(batch, summands):
        resid, mid = attended[batch][5:]
        d_resid, wide, *d_out = run_branch(
            info, batch, cotangent, resid, gain_mlp, mid, summands, weights_out
        )
        return d_resid, wide, group_exchange(d_out)

    def run_backward_of(batch, q, d_outs, sums_back):
        _, kv, ve, mids, normed, phi_key, states, fars, halo = saved[batch]
        att, weights, phi, sums, inverse = attended[batch][:5]
        d_q, d_kv, d_states, ends, back, *sums_back = run_backward(
            info, table, batch, q, kv, ve, halo, query_maps, o_in, att, weights, phi, sums,
            inverse, d_outs, sums_back,
        )
        return [d_q, None, d_kv, d_states], ends, back, sums_back

    def run_keys_of(batch, kv, gone, sums_keys):
        _, _, ve, mids, normed, phi_key, states, _, _ = saved[batch]
        d_q, d_qs, d_kv, d_states, fars, returned = gone
        rest, *sums_keys = run_keys(
            info, table, batch, kv, ve, key_maps, phi_key, d_kv, returned, d_states, d_q, q_up,
            kv_up, fars, sums_keys,
        )
        rests = group_exchange([rest[r] for r in range(n_grp)])
        return [rest, *rests[1:]], sums_keys

    def run_adapters_of(batch, d_q, rest, d_outs):
        return run_adapters(
            info, d_q, rest, saved[batch][3], saved[batch][4], attended[batch][0], d_outs
        )

    def run_tokens_of(batch, d_resid, gone, rests, prev):
        d_q, d_qs = gone[:2]
        return run_tokens(
            info, batch, tokens, gain_attn, d_resid, [d_q, *d_qs[1:]], rests, weights_in, prev
        )

    def finish_rows(batch, *ready):
        blocks = partial[batch][n_grp:]
        blocks[0] = after(blocks[0], *ready)
        blocks[1], blocks[-1] = after(blocks[1], *ready), after(blocks[-1], *ready)
        return scatter_start(blocks)

    def rows_of(batch, summands):
        total = attended[batch][5]
        for summand in summands:
            total = total + summand.astype(F32)
        return total.astype(BF)

    low = n_grp // 2
    upper = run_mlp(
        info, 1, mlp_ins[1][low:], every[low:], cotangent, [ring_c], partial[1], sizes[1:]
    )
    summands_a = scatter_end(*started[0])
    crossed = [flip(upper[far + 1 - low], "grp", 1) for far in range(low, n_grp, 2)]
    crossed[0], summands_a[-1] = lax.optimization_barrier((crossed[0], summands_a[-1]))
    far_b = [
        (upper[far - low].astype(F32) + there.astype(F32)).astype(BF)
        for far, there in zip(range(low, n_grp, 2), crossed)
    ]
    attended[0][6] = after(attended[0][6], far_b[0])
    d_resid_a, wide_a, d_outs_a = run_branch_of(0, summands_a)
    partial[1][0] = after(partial[1][0], d_resid_a)
    lower = list(
        run_mlp(info, 1, mlp_ins[1][:low], every[:low], cotangent, [ring_c], partial[1], sizes[1:])
    )
    late_b = scatter_end(far_b, [])
    lower[1], late_b[-1] = lax.optimization_barrier((lower[1], late_b[-1]))
    near_b = [lower[0], flip(lower[1], "grp", 1)]
    early_b = [far_pair(lower[far], lower[far + 1]) for far in range(2, low, 2)]
    summands_b = near_b + scatter_end(early_b, []) + late_b
    partial[1] = [None] * n_grp + list(lower[low:]) + list(upper[low:])
    d_resid_b, wide_b, d_outs_b = run_branch_of(1, summands_b)
    gone_a, ends_a, back_a, sums_back = run_backward_of(
        0, after(saved[0][0], d_resid_b), d_outs_a, None
    )
    rows_a = finish_rows(0, *d_outs_a[2:], *d_outs_b[2:])
    gone_b, ends_b, back_b, sums_back = run_backward_of(
        1, after(saved[1][0], gone_a[0]), d_outs_b, sums_back
    )
    fars, returned = exchange(table, jnp.stack([ends_a, ends_b]), jnp.stack([back_a, back_b]), -1)
    gone_a += [fars, returned]
    gone_b += [fars, returned]
    rows_a = scatter_end(*rows_a)
    kv_a, rows_a[-1] = lax.optimization_barrier((after(saved[0][1], gone_b[0]), rows_a[-1]))
    rests_a, sums_keys = run_keys_of(0, kv_a, gone_a, None)
    kv_b = after(saved[1][1], rests_a[0])
    d_q = after(gone_a[0], rests_a[0])
    gone_a[1] = group_exchange([d_q[r] for r in range(n_grp)])
    rests_b, sums_keys = run_keys_of(1, kv_b, gone_b, sums_keys)
    d_q = after(gone_b[0], rests_b[0])
    gone_b[1] = group_exchange([d_q[r] for r in range(n_grp)])
    sums_a = run_adapters_of(0, after(gone_a[0], rests_b[0]), rests_a[0], d_outs_a)
    rows_b = finish_rows(1, rests_b[0])
    sums_b = run_adapters_of(
        1, after(gone_b[0], sums_a[0], *rests_a[1:], *gone_a[1][1:]), rests_b[0], d_outs_b
    )

    (early,) = run_plain(
        functools.partial(pack_early_kernel, per), "pack_early", [],
        [sums_back[0], sums_a[1], sums_b[1]],
        [sds((STRETCH * kv_heads * per // 2 + 16 * (q_width // PAIR), PAIR), BF)],
    )
    late_rows = 16 * (q_width // PAIR) + (16 + STRETCH) * kv_heads
    wide, late = run_plain(
        functools.partial(pack_late_kernel, q_width), "pack_late", [],
        [sums_a[0], sums_b[0], sums_keys[0], sums_a[2], sums_b[2], wide_a, wide_b],
        [sds((32 * (model // PAIR), PAIR), BF), sds((late_rows, PAIR), BF)],
    )
    wide = group_sum(wide)
    wide = after(wide, *rests_b[1:], *gone_b[1][1:])
    first = early.shape[0]
    columns = model // (n_seq * n_grp)
    value, bits = jnp.concatenate([early, wide, late]), n_seq.bit_length() - 1
    grad_tokens, held = None, [d_resid_a, d_resid_b]
    for step in range(bits):
        there = flip(value, "seq", 1 << step)
        batch = step - (bits - 2)
        if batch >= 0:
            gone, rests = ((gone_a, rests_a), (gone_b, rests_b))[batch]
            grad_tokens = run_tokens_of(
                batch, after(held[batch], value), gone, rests, grad_tokens
            )
            there, grad_tokens = lax.optimization_barrier((there, grad_tokens))
        if step < bits - 1:
            value = (value.astype(F32) + there.astype(F32)).astype(BF)
    packed = (value, there)
    rows_b = scatter_end(*rows_b)
    block_rows = [rows_of(0, rows_a), rows_of(1, rows_b)]
    wide, q_grad, kv_grad, oin_grad, query_grad, key_grad = run_plain(
        functools.partial(unpack_kernel, n_grp, columns), "unpack", [info],
        [packed[0][:first], packed[1][:first], packed[0][first:], packed[1][first:]],
        [
            sds((columns, 32), F32), sds((rank, q_width), F32),
            sds((2, rank, kv_heads * STRETCH), F32), sds((rank, q_width), F32),
            sds(query_feature_weight.shape, F32), sds(key_feature_weight.shape, F32),
        ],
        [pltpu.VMEM((PAIR, 32), F32)],
    )
    return (
        jnp.stack(block_rows),
        grad_tokens,
        wide.reshape(columns, 4, rank).transpose(1, 0, 2),
        q_grad,
        kv_grad,
        oin_grad.T,
        query_grad,
        key_grad,
    )


def solution(mesh):
    return jax.shard_map(
        local,
        mesh=mesh,
        in_specs=(
            P(None, "seq", None),
            P(None, "seq", None),
            P(),
            P(),
            P(),
            P("seq", "grp"),
            P("seq", None, "grp"),
            P("grp", "seq"),
            P("seq", None, "grp"),
            P("grp", "seq"),
            P(None, "seq", None),
            P(None, "grp"),
            P(None, None, "grp"),
            P("grp", None),
            P("grp", None, None),
            P("grp", None, None),
        ),
        out_specs=(
            P(None, ("seq", "grp"), None),
            P(None, ("seq", "grp"), None),
            P(None, ("seq", "grp"), None),
            P(None, "grp"),
            P(None, None, "grp"),
            P("grp", None),
            P("grp", None, None),
            P("grp", None, None),
        ),
        check_vma=False,
    )
```

```python
import functools
import math

import jax
import jax.numpy as jnp
from jax import lax
from jax.experimental import pallas as pl
from jax.experimental.pallas import tpu as pltpu
from jax.sharding import PartitionSpec as P

STRETCH = 64
PAIR = 2 * STRETCH
WIN = 3 * STRETCH
EXT = 80
EPS = 1e-05
ADAPTER_SCALE = 2.0
BF = jnp.bfloat16
F32 = jnp.float32
VMEM_LIMIT = 58 * 1024 * 1024
CHUNK = 256
ROW_TILE = 512
LATE_COST = 2000000
SMALL_LIMIT = 32 * 1024 * 1024


def dotg(left, right, lc, rc):
    return lax.dot_general(left, right, (((lc,), (rc,)), ((), ())), preferred_element_type=F32)


def ring_order(count):
    if count % 8:
        return list(range(count))
    deep, wide = 4, count // 4
    path = [z * wide for z in range(deep)]
    for step, z in enumerate(reversed(range(deep))):
        ys = list(range(1, wide))
        path += [z * wide + y for y in (ys if step % 2 == 0 else ys[::-1])]
    return path


def ring_offsets(count):
    out = [0]
    for distance in range(1, (count + 1) // 2):
        out += [-distance, distance]
    return out + [count // 2]


def ring_sources(count):
    order = ring_order(count)
    return [[order[(order.index(s) + o) % count] for o in ring_offsets(count)] for s in range(count)]


def ring_cut(rows):
    return (rows // 2 + 15) // 16 * 16


def ring_layout(count, rows):
    cut = ring_cut(rows)
    return [(q, 0, rows) for q in range(count - 1)] + [
        (count - 1, 0, cut), (count - 1, cut, rows - cut),
    ]


def pieces_of(width):
    first = width // (2 * CHUNK) * CHUNK
    return [(0, first), (first, width - first)]


class Ring:
    def __init__(self, shard):
        self.count = lax.axis_size("seq")
        self.order = ring_order(self.count)
        self.parts = [shard]
        self.ahead = self.back = shard
        self.done = 0

    def move(self, value, step):
        pairs = [(self.order[i], self.order[(i + step) % self.count]) for i in range(self.count)]
        return lax.ppermute(value, "seq", pairs)

    def hop(self, *after):
        self.ahead, self.back, *_ = lax.optimization_barrier((self.ahead, self.back, *after))
        self.done += 1
        if self.done < (self.count + 1) // 2:
            self.ahead, self.back = self.move(self.ahead, 1), self.move(self.back, -1)
            self.parts += [self.ahead, self.back]
        else:
            cut = ring_cut(self.ahead.shape[0])
            self.parts += [self.move(self.ahead[:cut], 1), self.move(self.back[cut:], -1)]

    def hops(self):
        return (self.count + 1) // 2

    def tie(self, *values):
        self.ahead, self.back, *values = lax.optimization_barrier((self.ahead, self.back, *values))
        return values

    def finish(self):
        while self.done < self.hops():
            self.hop()
        return self


def after(value, *others):
    return lax.optimization_barrier((value, *others))[0]


def flip(value, axis, bit):
    count = lax.axis_size(axis)
    return lax.ppermute(value, axis, [(i, i ^ bit) for i in range(count)])


def shifted(value, axis, steps):
    count = lax.axis_size(axis)
    first, last = max(0, -steps), min(count, count - steps)
    return lax.ppermute(value, axis, [(i, i + steps) for i in range(first, last)])


def group_gather(share):
    count = lax.axis_size("grp")
    out = []
    for far in range(0, count, 2):
        mine = share if far == 0 else flip(share, "grp", far)
        out += [mine, flip(mine, "grp", 1)]
    return out


def far_gather(share):
    return [share] + [flip(share, "grp", far) for far in range(2, lax.axis_size("grp"), 2)]


def near_gather(fars):
    out = []
    for far in fars:
        out += [far, flip(far, "grp", 1)]
    return out


def group_exchange(blocks):
    return [blocks[0]] + [flip(blocks[r], "grp", r) for r in range(1, len(blocks))]


def far_pair(here, there):
    return (here.astype(F32) + flip(there, "grp", 1).astype(F32)).astype(BF)


def scatter_start(blocks):
    count = len(blocks)
    fars = []
    for far in range(2, count, 2):
        fars.append(far_pair(blocks[far], blocks[far + 1]))
    return fars, [blocks[0], flip(blocks[1], "grp", 1)]


def scatter_end(fars, nears):
    return nears + [flip(far, "grp", 2 * (i + 1)) for i, far in enumerate(fars)]


def exchange(table, ends, sign):
    count = lax.axis_size("seq")
    wide = max(1, count // 4)
    here = [flip(ends, "seq", j) for j in range(1, wide)]
    near, full = run_layer(table, [ends, *here], sign)
    out = here + [shifted(near, "seq", sign * wide)]
    return out + [shifted(full, "seq", sign * r * wide) for r in range(2, count // wide)]


VALID, ONE, TWO = range(3)
FULL, INNER, NEXT, LAYER_FULL, LAYER_INNER, LAYER_NEXT = range(6)
TABLE_ROWS = 15


def side_row(sign, row):
    return 3 + row + (0 if sign > 0 else 6)


def table_width(blocks, count):
    return max(blocks + 4, 2 * count)


def layout_kernel(blocks, wide, count, info, lens, out):
    width = table_width(blocks, count)
    base, seq = info[0], info[2]
    z, y = seq // wide, seq % wide
    for batch in range(lens.shape[0]):
        starts, ends, at = [], [], 0
        for i in range(lens.shape[1]):
            length = lens[batch, i]
            starts.append(at)
            ends.append(at * STRETCH + length)
            at = at + ((length + STRETCH - 1) >> 6)

        def owner(c):
            total = -1
            for start in starts:
                total = total + jnp.where(start <= c, 1, 0)
            return total

        def put(row, i, value):
            out[(batch * TABLE_ROWS + row) * width + i] = value

        owned = [owner(base + c) for c in range(-3, blocks + 3)]
        for i in range(blocks + 4):
            c = base + i - 1
            end = 0
            for start, stop in zip(starts, ends):
                end = jnp.where(start <= c, stop, end)
            put(VALID, i, jnp.clip(end - c * STRETCH, 0, STRETCH))
            put(ONE, i, jnp.where(owned[i + 2] == owned[i + 1], 1, 0))
            put(TWO, i, jnp.where(owned[i + 2] == owned[i], 1, 0))
        for sign in (1, -1):
            edge = base - 1 if sign > 0 else base + blocks
            outer, inner = owner(edge), owner(edge - sign)
            end_of = lambda device: device * blocks + (blocks - 1 if sign > 0 else 0)
            last = wide - 1 if sign > 0 else 0
            first = wide - 1 - last
            layer_end = end_of(z * wide + last)
            layer_outer, layer_inner = owner(layer_end), owner(layer_end - sign)
            for j in range(wide):
                source = z * wide + (y ^ j)
                far = (seq - source) * sign
                there = owner(end_of(source))
                put(side_row(sign, FULL), j, jnp.where((far > 0) & (there == outer), 1, 0))
                put(side_row(sign, INNER), j, jnp.where((far > 1) & (there == inner), 1, 0))
                put(side_row(sign, NEXT), j, jnp.where(far == 1, 1, 0))
                put(side_row(sign, LAYER_FULL), j, jnp.where(there == layer_outer, 1, 0))
                outermost = (y ^ j) == last
                put(side_row(sign, LAYER_NEXT), j, jnp.where(outermost, 1, 0))
                put(
                    side_row(sign, LAYER_INNER), j,
                    jnp.where((there == layer_inner) & (~outermost), 1, 0),
                )
            for r in range(1, count // wide):
                layer = z - sign * r
                inside = (layer >= 0) & (layer < count // wide)
                there = owner(end_of(layer * wide + last))
                i = wide + r
                direct = (y == first) if r == 1 else (y != y)
                put(side_row(sign, FULL), i, jnp.where(inside & (there == outer), 1, 0))
                put(
                    side_row(sign, INNER), i,
                    jnp.where(inside & (there == inner) & (~direct), 1, 0),
                )
                put(side_row(sign, NEXT), i, jnp.where(inside & direct, 1, 0))


class Slots:
    def __init__(self, table, batch, blocks, count):
        self.table, self.batch, self.width = table, batch, table_width(blocks, count)

    def at(self, row, i):
        return self.table[(self.batch * TABLE_ROWS + row) * self.width + i]

    def valid(self, c):
        return self.at(VALID, c + 1)

    def one(self, c):
        return self.at(ONE, c + 1)

    def weight_one(self, c):
        return self.one(c).astype(F32)

    def weight_two(self, c):
        return self.at(TWO, c + 1).astype(F32)


def entering(slots, arrays, wide, count, sign, place, near_k):
    inner = outer = jnp.zeros((EXT, PAIR), F32)
    rows = jnp.zeros((arrays[0].shape[2] - 2 * EXT, PAIR), F32)
    row = lambda name, i: slots.at(side_row(sign, name), i).astype(F32)
    for r in range(1, count // wide + wide - 1):
        layer = r >= wide
        i = r + 1 if layer else r
        array = arrays[r - 1]
        if r > wide:
            full = array[place, near_k].astype(F32)
        else:
            full = array[place, near_k, EXT : 2 * EXT].astype(F32)
            inner = inner + row(NEXT, i) * array[place, near_k, :EXT].astype(F32)
            rows = rows + row(NEXT, i) * array[place, near_k, 2 * EXT :].astype(F32)
        outer = outer + row(FULL, i) * full
        inner = inner + row(INNER, i) * full
    return inner, outer, rows


def layer_kernel(sign, blocks, count, wide, table, *refs):
    ends, (near_ref, full_ref) = refs[:wide], refs[wide:]
    for batch in range(near_ref.shape[0]):
        slots = Slots(table, batch, blocks, count)
        row = lambda name, i: slots.at(side_row(sign, name), i).astype(F32)
        for k in range(near_ref.shape[1]):
            full = inner = jnp.zeros((EXT, PAIR), F32)
            rows = jnp.zeros((near_ref.shape[2] - 2 * EXT, PAIR), F32)
            for j in range(wide):
                value = ends[j][batch, k, EXT : 2 * EXT].astype(F32)
                full = full + row(LAYER_FULL, j) * value
                inner = inner + row(LAYER_INNER, j) * value
                inner = inner + row(LAYER_NEXT, j) * ends[j][batch, k, :EXT].astype(F32)
                rows = rows + row(LAYER_NEXT, j) * ends[j][batch, k, 2 * EXT :].astype(F32)
            near_ref[batch, k, :EXT] = inner.astype(BF)
            near_ref[batch, k, EXT : 2 * EXT] = full.astype(BF)
            near_ref[batch, k, 2 * EXT :] = rows.astype(BF)
            full_ref[batch, k] = full.astype(BF)


def half_mask(shape):
    return (lax.broadcasted_iota(jnp.int32, shape, 1) & (PAIR - 1)) < STRETCH


def feature_softmax(u):
    top = jnp.exp(u - jnp.max(u, axis=0, keepdims=True))
    bottom = jnp.exp(jnp.min(u, axis=0, keepdims=True) - u)
    top = top * (1.0 / jnp.sum(top, axis=0, keepdims=True))
    bottom = bottom * (1.0 / jnp.sum(bottom, axis=0, keepdims=True))
    return jnp.concatenate([top, bottom], axis=0)


def feature_back(phi, d_phi):
    top, bottom = phi[:STRETCH].astype(F32), phi[STRETCH:].astype(F32)
    a, b = d_phi[:STRETCH], d_phi[STRETCH:]
    return top * (a - jnp.sum(top * a, axis=0, keepdims=True)) - bottom * (
        b - jnp.sum(bottom * b, axis=0, keepdims=True)
    )


def assemble_kernel(parts_of, width, splits, info, *refs):
    ins, outs = refs[: len(parts_of)], refs[len(parts_of) :]
    for (q, first, rows), ref in zip(parts_of, ins):
        column = pl.ds(pl.multiple_of(info[3 + q] * width, width), width)
        at = 0
        for out, size in zip(outs, splits):
            low, high = max(at, first), min(at + size, first + rows)
            if low < high:
                out[low - at : high - at, column] = ref[low - first : high - first, :]
            at += size


def project_kernel(
    batch, q_width, blocks, count, table, normed_ref, w_ref, up_ref, kv_up_ref, wk_ref,
    q_ref, kv_ref, ve_ref, mid_ref, phi_ref, st_ref, ends_ref, carry,
):
    step = pl.program_id(0)
    rows = normed_ref.shape[0]
    width = kv_ref.shape[1]
    heads = width // PAIR

    @pl.when(step == 0)
    def _():
        carry[...] = jnp.zeros_like(carry)

    normed = normed_ref[...]
    product = dotg(w_ref[...], normed, 1, 1)
    mixed = product[: q_width + 32]
    mids = mixed[q_width:].astype(BF)
    mid_ref[...] = mids
    query = mixed[:q_width] + ADAPTER_SCALE * dotg(up_ref[...], mids, 1, 0)
    q_ref[...] = query.astype(BF)
    kv_all = jnp.transpose(product[q_width + 32 :]) + ADAPTER_SCALE * dotg(
        mids, kv_up_ref[...], 0, 0
    )
    kv_all = kv_all.astype(BF)
    kv_ref[...] = kv_all

    slots = Slots(table, batch, blocks, count)
    lane = lax.broadcasted_iota(jnp.int32, (1, PAIR), 1)
    low = lane < STRETCH
    inside = lane & (STRETCH - 1)
    wide = lax.broadcasted_iota(jnp.int32, (PAIR, PAIR), 1)
    for sub in range(rows // PAIR):
        block = 2 * (step * (rows // PAIR) + sub)
        one_a, one_b = slots.weight_one(block), slots.weight_one(block + 1)
        valid = inside < jnp.where(low, slots.valid(block), slots.valid(block + 1))
        valid = jnp.where(valid, 1.0, 0.0)
        valid_low = jnp.where(low, valid, 0.0)
        valid_high = valid - valid_low
        at = sub * PAIR
        for k in range(heads):
            kv = kv_all[at : at + PAIR, k * PAIR : (k + 1) * PAIR]
            moved = pltpu.roll(kv.astype(F32), STRETCH, 1)
            ve = jnp.where(
                wide < STRETCH, moved, jnp.where(wide < STRETCH + 2, 1.0, 0.0)
            ).astype(BF)
            ve_ref[at : at + PAIR, k * PAIR : (k + 1) * PAIR] = ve
            if sub == rows // PAIR - 1:
                ends_ref[k, 2 * EXT : 2 * EXT + STRETCH] = kv[STRETCH:]
                ends_ref[k, 2 * EXT + STRETCH :] = ve[STRETCH:]
            phi = feature_softmax(dotg(wk_ref[k], kv, 1, 1))
            phi_ref[k * PAIR : (k + 1) * PAIR, at : at + PAIR] = (phi * valid).astype(BF)
            first = dotg(ve, (phi * valid_low).astype(BF), 0, 1)[:EXT]
            second = dotg(ve, (phi * valid_high).astype(BF), 0, 1)[:EXT]
            st_ref[sub, k, :EXT] = first
            st_ref[sub, k, EXT:] = second
            mid = carry[k] * one_a + first
            tail = mid * one_b + second
            carry[k] = tail
            ends_ref[k, :EXT] = mid.astype(BF)
            ends_ref[k, EXT : 2 * EXT] = tail.astype(BF)


def window_mask(slots, block):
    lane = lax.broadcasted_iota(jnp.int32, (1, PAIR), 1)
    low = lane < STRETCH
    before = slots.valid(block - 1) * slots.one(block)
    own = slots.valid(block)
    limits = [
        jnp.where(low, before, 0),
        jnp.where(low, jnp.minimum(lane + 1, own), own * slots.one(block + 1)),
        jnp.where(low, 0, jnp.minimum(lane - STRETCH + 1, slots.valid(block + 1))),
    ]
    row = lax.broadcasted_iota(jnp.int32, (STRETCH, PAIR), 0)
    return jnp.concatenate([jnp.where(row < limit, 1.0, 0.0) for limit in limits], axis=0)


def fill_window(k, kv_ref, ve_ref, rows, kv_all, ve_all):
    cols = slice(k * PAIR, (k + 1) * PAIR)
    kv_all[:STRETCH, cols] = rows[:STRETCH].astype(BF)
    ve_all[:STRETCH, cols] = rows[STRETCH:].astype(BF)
    kv_all[STRETCH:, cols] = kv_ref[:, cols]
    ve_all[STRETCH:, cols] = ve_ref[:, cols]


def forward_kernel(
    batch, per, blocks, wide, count, n_far, scale, info, table, q_ref, kv_ref, ve_ref,
    wq_ref, oin_ref, st_ref, *refs,
):
    fars = refs[:n_far]
    att_ref, w_ref, phi_ref, s_ref, r_ref, carry, kv_all, ve_all = refs[n_far:]
    step = pl.program_id(0)
    heads = kv_ref.shape[1] // PAIR
    slots = Slots(table, batch, blocks, count)
    block = 2 * step

    @pl.when(step == 0)
    def _():
        for k in range(heads):
            inner, outer, rows = entering(slots, fars, wide, count, 1, batch, k)
            fill_window(k, kv_ref, ve_ref, rows, kv_all, ve_all)
            carry[k, 0] = inner
            carry[k, 1] = outer

    one_a, one_b = slots.weight_one(block), slots.weight_one(block + 1)
    two_a, two_b = slots.weight_two(block), slots.weight_two(block + 1)
    mask = window_mask(slots, block)
    mask = jnp.concatenate([mask] * per, axis=1)
    lanes = per * PAIR
    low = half_mask((EXT, lanes))
    rows = pl.ds(pl.multiple_of(step * PAIR, PAIR), WIN)
    out_mid = jnp.zeros((16, PAIR), F32)
    for k in range(heads):
        kv = kv_all[rows, k * PAIR : (k + 1) * PAIR]
        ve = ve_all[rows, k * PAIR : (k + 1) * PAIR]
        base = k * per * STRETCH
        stacked = q_ref[base : base + per * STRETCH, :]
        q = jnp.concatenate(
            [stacked[g * STRETCH : (g + 1) * STRETCH] for g in range(per)], axis=1
        )
        q = jnp.concatenate([q, jnp.zeros_like(q)], axis=0)
        scores = dotg(kv, q, 1, 0)
        weights = (jnp.exp2(scores * scale) * mask).astype(BF)
        w_ref[0, k] = weights
        mixed = dotg(wq_ref[k], stacked, 1, 0)
        phi = jnp.concatenate(
            [
                feature_softmax(mixed[g * STRETCH : (g + 1) * STRETCH]).astype(BF)
                for g in range(per)
            ],
            axis=1,
        )
        phi_ref[0, k] = phi
        older, old = carry[k, 0], carry[k, 1]
        states = jnp.concatenate([older * two_a, old * two_b], axis=0).astype(BF)
        s_ref[0, k] = states
        linear = dotg(states, phi, 1, 0)
        total = dotg(ve, weights, 0, 0)[:EXT] + jnp.where(low, linear[:EXT], linear[EXT:])
        inverse = 1.0 / total[STRETCH : STRETCH + 1]
        att = (total[:STRETCH] * inverse).astype(BF)
        att = jnp.concatenate([att[:, g * PAIR : (g + 1) * PAIR] for g in range(per)], axis=0)
        att_ref[0, base : base + per * STRETCH, :] = att
        out_mid = out_mid + dotg(oin_ref[base : base + per * STRETCH, :], att, 0, 0)
        for g in range(per):
            r_ref[0, k * per + g : k * per + g + 1, :] = inverse[:, g * PAIR : (g + 1) * PAIR]
        current = old * one_a + st_ref[0, k, :EXT]
        carry[k, 0] = current
        carry[k, 1] = current * one_b + st_ref[0, k, EXT:]
    att_ref[0, heads * per * STRETCH :, :] = (ADAPTER_SCALE * out_mid).astype(BF)


def residual_kernel(n_grp, info, x_ref, gain_ref, *refs):
    atts, weights = refs[:n_grp], refs[n_grp : 2 * n_grp]
    resid_ref, low_ref, mid_ref, buffer, sems = refs[2 * n_grp :]
    copies = [
        pltpu.make_async_copy(weights[r], buffer.at[r], sems.at[r]) for r in range(n_grp)
    ]
    for copy in copies:
        copy.start()
    q_width = buffer.shape[1] - 16
    resid_ref[...] = x_ref[0].astype(F32)
    mid = jnp.zeros(mid_ref.shape, F32)
    for r in range(n_grp):
        copies[r].wait()
        att = atts[r][0] if len(atts[r].shape) == 3 else atts[r][...]
        mid = mid + att[q_width:].astype(F32)
        resid_ref[...] += dotg(att, buffer[r], 0, 0)
    mid_ref[...] = mid.astype(BF)
    resid = resid_ref[...]
    factor = lax.rsqrt(jnp.mean(resid * resid, axis=1, keepdims=True) + EPS)
    low_ref[...] = (resid * factor * gain_ref[...]).astype(BF)


def branch_kernel(n_grp, n_sum, info, dy_ref, resid_ref, gain_ref, mid_ref, *refs):
    summands, refs = refs[:n_sum], refs[n_sum:]
    weights, refs = refs[:n_grp], refs[n_grp:]
    d_resid_ref, wide_ref, refs = refs[0], refs[1], refs[2:]
    outs, (buffer, sems) = refs[:n_grp], refs[n_grp:]
    copies = [
        pltpu.make_async_copy(weights[r], buffer.at[r], sems.at[r]) for r in range(n_grp)
    ]
    for copy in copies:
        copy.start()
    d_in = summands[0][...].astype(F32)
    for summand in summands[1:]:
        d_in = d_in + summand[...].astype(F32)
    resid = resid_ref[...]
    factor = lax.rsqrt(jnp.mean(resid * resid, axis=1, keepdims=True) + EPS)
    e = gain_ref[...] * d_in
    slope = factor * factor * factor * jnp.mean(resid * e, axis=1, keepdims=True)
    d_resid = dy_ref[0].astype(F32) + factor * e - resid * slope
    d_resid_ref[...] = d_resid
    low = d_resid.astype(BF)
    wide_ref[...] = dotg(mid_ref[...], low, 1, 0)
    for r in range(n_grp):
        copies[r].wait()
        outs[r][...] = dotg(buffer[r], low, 1, 1).astype(BF)


def tokens_kernel(n_grp, info, x_ref, gain_ref, d_resid_ref, *refs):
    dqs, rests, weights = refs[:n_grp], refs[n_grp : 2 * n_grp], refs[2 * n_grp : 3 * n_grp]
    out_ref, buffer, total, sems = refs[3 * n_grp :][-4:]
    copies = [
        pltpu.make_async_copy(weights[r], buffer.at[r], sems.at[r]) for r in range(n_grp)
    ]
    for copy in copies:
        copy.start()
    for r in range(n_grp):
        copies[r].wait()
        d_q = dqs[r][0] if len(dqs[r].shape) == 3 else dqs[r][...]
        rest = rests[r][0] if len(rests[r].shape) == 3 else rests[r][...]
        part = dotg(jnp.concatenate([d_q, rest], axis=0), buffer[r], 0, 0)
        if r:
            total[...] += part
        else:
            total[...] = part
    x = x_ref[0].astype(F32)
    factor = lax.rsqrt(jnp.mean(x * x, axis=1, keepdims=True) + EPS)
    e = gain_ref[...] * total[...]
    slope = factor * factor * factor * jnp.mean(x * e, axis=1, keepdims=True)
    out_ref[0] = d_resid_ref[...] + factor * e - x * slope


def mlp_kernel(
    batch, rels, layout, sizes, first_half, info, *refs,
):
    n_parts = len(layout)
    n_grp = len(rels)
    xs, refs = refs[:n_grp], refs[n_grp:]
    dy_hbm, refs = refs[0], refs[1:]
    part_sets = []
    for _ in sizes:
        part_sets.append(refs[:n_parts])
        refs = refs[n_parts:]
    n_prev = 0 if first_half else 2
    prevs, refs = refs[:n_prev], refs[n_prev:]
    n_out = 2 if first_half else 2 * n_grp
    outs, refs = refs[:n_out], refs[n_out:]
    x, dy, w, acc_out, acc_in, sem, wsem = refs[:7]
    j, n = pl.program_id(0), pl.num_programs(0)
    slot = j % 2
    share = xs[0].shape[0]
    rows_all = x.shape[0]
    depth = layout[0][2]

    def loads(jj, s, which):
        copies = []
        first_step = sum(sizes[:which]) // CHUNK
        for (q, first, rows), part in zip(layout, part_sets[which]):
            to = pl.ds(pl.multiple_of(info[3 + q] * depth + first, 16), rows)
            for kind in range(3):
                column = pl.multiple_of(kind * sizes[which] + (jj - first_step) * CHUNK, CHUNK)
                copies.append(
                    pltpu.make_async_copy(
                        part.at[:, pl.ds(column, CHUNK)],
                        w.at[s, to, pl.ds(kind * CHUNK, CHUNK)],
                        wsem.at[s],
                    )
                )
        return copies

    def start_loads(jj, s):
        for which in range(len(sizes)):
            low, high = sum(sizes[:which]) // CHUNK, sum(sizes[: which + 1]) // CHUNK

            @pl.when((jj >= low) & (jj < high))
            def _(which=which):
                for copy in loads(jj, s, which):
                    copy.start()

    per_tile = ROW_TILE // share

    def inputs(tile):
        copies = []
        for r in range(tile * per_tile, (tile + 1) * per_tile):
            rows = pl.ds(r * share, share)
            copies.append(pltpu.make_async_copy(xs[r], x.at[rows], sem.at[tile]))
            there = pl.ds(pl.multiple_of((info[1] ^ rels[r]) * share, share), share)
            copies.append(pltpu.make_async_copy(dy_hbm.at[batch, there], dy.at[rows], sem.at[tile]))
        return copies

    tiles = rows_all // ROW_TILE

    def earlier():
        part = pl.ds(rels[0] * share, rows_all)
        return [
            pltpu.make_async_copy(prev.at[part], refs[7 + i], sem.at[tiles])
            for i, prev in enumerate(prevs)
        ]

    def results():
        if first_half:
            return [
                pltpu.make_async_copy(x, outs[0], sem.at[0]),
                pltpu.make_async_copy(dy, outs[1], sem.at[1]),
            ]
        copies = []
        for r in range(n_grp):
            rows = pl.ds(r * share, share)
            copies.append(pltpu.make_async_copy(x.at[rows], outs[r], sem.at[0]))
            copies.append(pltpu.make_async_copy(dy.at[rows], outs[n_grp + r], sem.at[0]))
        return copies

    @pl.when(j == 0)
    def _():
        for copy in inputs(0):
            copy.start()
        start_loads(j, 0)
        for tile in range(1, tiles):
            for copy in inputs(tile):
                copy.start()
        for copy in earlier():
            copy.start()

    @pl.when(j + 1 < n)
    def _():
        start_loads(j + 1, 1 - slot)

    for copy in loads(0, slot, 0):
        copy.wait()
    gate_up_w = w.at[slot, :, pl.ds(0, 2 * CHUNK)]
    down_w = w.at[slot, :, pl.ds(2 * CHUNK, CHUNK)]

    def body(tile, start, end):
        rows = pl.ds(pl.multiple_of(tile * ROW_TILE, ROW_TILE), ROW_TILE)
        if start:
            for i in range(per_tile):
                part = pl.ds(pl.multiple_of(tile * ROW_TILE + i * share, share), share)
                pltpu.make_async_copy(xs[0], x.at[part], sem.at[tile]).wait()
                pltpu.make_async_copy(xs[0], dy.at[part], sem.at[tile]).wait()
        gate_up = dotg(x[rows, :], gate_up_w[...], 1, 0)
        d_hidden = dotg(dy[rows, :], down_w[...], 1, 0)
        gate, up = gate_up[:, :CHUNK], gate_up[:, CHUNK:]
        sig = 1.0 / (1.0 + jnp.exp(-gate))
        act = gate * sig
        hidden = (act * up).astype(BF)
        d_gate = (d_hidden * up * (sig + act * (1.0 - sig))).astype(BF)
        d_up = (d_hidden * act).astype(BF)
        out = dotg(hidden, down_w[...], 1, 1)
        d_in = dotg(jnp.concatenate([d_gate, d_up], axis=1), gate_up_w[...], 1, 1)
        if start:
            acc_out[rows, :] = out
            acc_in[rows, :] = d_in
        elif not end:
            acc_out[rows, :] += out
            acc_in[rows, :] += d_in
        else:
            out, d_in = acc_out[rows, :] + out, acc_in[rows, :] + d_in
            if not first_half:
                d_in = d_in + refs[7][rows, :].astype(F32)
                out = out + refs[8][rows, :].astype(F32)
            x[rows, :] = d_in.astype(BF)
            dy[rows, :] = out.astype(BF)
        return 0

    @pl.when(j == 0)
    def _():
        lax.fori_loop(0, tiles, lambda i, c: body(i, True, False), 0)

    @pl.when((j > 0) & (j < n - 1))
    def _():
        lax.fori_loop(0, tiles, lambda i, c: body(i, False, False), 0)

    @pl.when(j == n - 1)
    def _():
        for copy in earlier():
            copy.wait()
        lax.fori_loop(0, tiles, lambda i, c: body(i, False, True), 0)
        for copy in results():
            copy.start()
        for copy in results():
            copy.wait()


def backward_kernel(
    batch, per, pairs, n_grp, has_prev, count, wide, n_far, scale, info, table, q_ref, kv_ref, ve_ref, wq_ref,
    oin_ref, att_ref, w_ref, phi_ref, s_ref, r_ref, *refs,
):
    fars, refs = refs[:n_far], refs[n_far:]
    blocks_in, refs = refs[:n_grp], refs[n_grp:]
    prevs, refs = (refs[:1], refs[1:]) if has_prev else (None, refs)
    (
        dq_ref, dkv_ref, ds_ref, ends_ref, map_ref, carry, kv_all, ve_all, d_outs, sem,
    ) = refs
    step = pl.program_id(0)
    pair = pairs - 1 - step
    heads = kv_ref.shape[1] // PAIR
    slots = Slots(table, batch, 2 * pairs, count)
    block = 2 * pair
    q_width = q_ref.shape[0]
    per_block = blocks_in[0].shape[1] // PAIR

    @pl.when(step == 0)
    def _():
        copies = []
        for r in range(n_grp):
            for i in range(per_block):
                copies.append(
                    pltpu.make_async_copy(
                        blocks_in[r].at[:, pl.ds(i * PAIR, PAIR)],
                        d_outs.at[(info[1] ^ r) * per_block + i],
                        sem,
                    )
                )
        for copy in copies:
            copy.start()
        for k in range(heads):
            rows = entering(slots, fars, wide, count, 1, batch, k)[2]
            fill_window(k, kv_ref, ve_ref, rows, kv_all, ve_all)
        carry[...] = jnp.zeros_like(carry)
        dkv_ref[...] = jnp.zeros_like(dkv_ref)
        map_ref[...] = prevs[0][...] if has_prev else jnp.zeros_like(map_ref)
        for copy in copies:
            copy.wait()
    one_b = slots.weight_one(block + 1)
    one_c = slots.weight_one(block + 2)
    lanes = per * PAIR
    low = half_mask((EXT, lanes))
    rows = pl.ds(pl.multiple_of(pair * PAIR, PAIR), WIN)
    d_out = d_outs[pair]
    back_out = ADAPTER_SCALE * d_out[q_width:]
    d_att_all = d_out[:q_width].astype(F32) + dotg(oin_ref[...], back_out, 1, 0)
    for k in range(heads):
        kv = kv_all[rows, k * PAIR : (k + 1) * PAIR]
        ve = ve_all[rows, k * PAIR : (k + 1) * PAIR]
        base = k * per * STRETCH

        def side(value):
            return jnp.concatenate(
                [value[g * STRETCH : (g + 1) * STRETCH] for g in range(per)], axis=1
            )

        stacked = q_ref[base : base + per * STRETCH, :]
        q = side(stacked)
        d_att = side(d_att_all[base : base + per * STRETCH])
        att = side(att_ref[0, base : base + per * STRETCH, :]).astype(F32)
        inverse = jnp.concatenate(
            [r_ref[0, k * per + g : k * per + g + 1, :] for g in range(per)], axis=1
        )
        ratio = d_att * inverse
        d_den = -jnp.sum(ratio * att, axis=0, keepdims=True)
        d_high = d_den.astype(BF).astype(F32)
        row = lax.broadcasted_iota(jnp.int32, (EXT - STRETCH, lanes), 0)
        extra = jnp.where(row == 0, d_high, jnp.where(row == 1, d_den - d_high, 0.0))
        ratio_ext = jnp.concatenate([ratio, extra], axis=0)
        ratio_low = ratio_ext.astype(BF)
        weights = w_ref[0, k]
        padded = jnp.concatenate([ratio_low, jnp.zeros((PAIR - EXT, lanes), BF)], axis=0)
        d_weights = dotg(ve, padded, 1, 0)
        d_scores = (d_weights * weights.astype(F32)).astype(BF)
        d_query = dotg(kv, d_scores, 0, 0)[:STRETCH] * scale
        zeros = jnp.zeros((STRETCH, lanes), BF)
        q_scaled = (q.astype(F32) * scale).astype(BF)
        d_kv = dotg(d_scores, jnp.concatenate([q_scaled, zeros], axis=0), 1, 1) + dotg(
            weights, jnp.concatenate([zeros, ratio_low[:STRETCH]], axis=0), 1, 1
        )
        dkv_ref[rows, k * PAIR : (k + 1) * PAIR] += d_kv
        phi = phi_ref[0, k]
        both = jnp.concatenate(
            [jnp.where(low, ratio_ext, 0.0), jnp.where(low, 0.0, ratio_ext)], axis=0
        ).astype(BF)
        d_phi = dotg(s_ref[0, k], both, 0, 0)
        d_state = dotg(both, phi, 1, 1)
        ds_ref[0, k] = d_state
        d_mixed = feature_back(phi, d_phi).astype(BF)
        d_mixed = jnp.concatenate(
            [d_mixed[:, g * PAIR : (g + 1) * PAIR] for g in range(per)], axis=0
        )
        d_stacked = jnp.concatenate(
            [d_query[:, g * PAIR : (g + 1) * PAIR] for g in range(per)], axis=0
        ) + dotg(wq_ref[k], d_mixed, 0, 0)
        dq_ref[0, base : base + per * STRETCH, :] = d_stacked.astype(BF)
        map_ref[k] += dotg(stacked, d_mixed, 1, 1)
        rest = d_state[EXT:] + one_c * carry[k]
        head = d_state[:EXT] + one_b * rest
        carry[k] = head
        ends_ref[k, :EXT] = rest.astype(BF)
        ends_ref[k, EXT : 2 * EXT] = head.astype(BF)

    @pl.when(step == pairs - 1)
    def _():
        for k in range(heads):
            ends_ref[k, 2 * EXT :] = dkv_ref[:STRETCH, k * PAIR : (k + 1) * PAIR].astype(BF)


def keys_kernel(
    batch, pairs, per_block, wide_y, count, n_far, has_prev, info, table, kv_ref, ve_ref, wk_ref,
    phi_ref, dkv_ref, ds_ref, dq_ref, q_up_ref, kv_up_ref, *refs,
):
    fars, refs = refs[:n_far], refs[n_far:]
    prevs, refs = (refs[:1], refs[1:]) if has_prev else (None, refs)
    out_ref, map_ref, carry, back = refs
    step = pl.program_id(0)
    pair = pairs - 1 - step
    heads = kv_ref.shape[1] // PAIR
    slots = Slots(table, batch, 2 * pairs, count)
    block = 2 * pair

    @pl.when(step == 0)
    def _():
        for k in range(heads):
            inner, outer, back[k] = entering(slots, fars, wide_y, count, -1, batch, k)
            carry[k, 0] = outer
            carry[k, 1] = inner
        map_ref[...] = prevs[0][...] if has_prev else jnp.zeros_like(map_ref)

    one_b = slots.weight_one(block + 1)
    one_c = slots.weight_one(block + 2)
    two_c = slots.weight_two(block + 2)
    two_d = slots.weight_two(block + 3)
    row = lax.broadcasted_iota(jnp.int32, (PAIR, PAIR), 0)
    lane = lax.broadcasted_iota(jnp.int32, (PAIR, PAIR), 1)
    last = jnp.where(step == 0, 1.0, 0.0)
    rows = pl.ds(pl.multiple_of(pair * PAIR + STRETCH, STRETCH), PAIR)
    d_kvs = []
    for k in range(heads):
        kv = kv_ref[:, k * PAIR : (k + 1) * PAIR]
        ve = ve_ref[:, k * PAIR : (k + 1) * PAIR].astype(F32)
        next_one, next_two = carry[k, 0], carry[k, 1]
        pad = jnp.zeros((PAIR - EXT, PAIR), F32)
        grads = jnp.concatenate([next_one * two_c, pad, next_two * two_d, pad], axis=0).astype(BF)
        both = jnp.concatenate(
            [jnp.where(row < STRETCH, ve, 0.0), jnp.where(row < STRETCH, 0.0, ve)], axis=1
        ).astype(BF)
        d_phi = dotg(grads, both, 0, 1)
        phi = phi_ref[k * PAIR : (k + 1) * PAIR, :]
        d_both = dotg(phi, grads, 0, 1)
        d_value = jnp.where(row < STRETCH, d_both[:, :PAIR], d_both[:, PAIR:])
        d_value = jnp.where(lane < STRETCH, 0.0, pltpu.roll(d_value, STRETCH, 1))
        d_mixed = feature_back(phi, d_phi).astype(BF)
        d_key = dotg(d_mixed, wk_ref[k], 0, 0)
        map_ref[k] += dotg(kv, d_mixed, 0, 1)
        total = dkv_ref[rows, k * PAIR : (k + 1) * PAIR] + d_value + d_key
        returned = back[k] * last
        total = total + jnp.concatenate([jnp.zeros_like(returned), returned], axis=0)
        d_kvs.append(jnp.transpose(total).astype(BF))
        state = ds_ref[0, k]
        rest = state[EXT:] + one_c * next_one
        carry[k, 1] = rest
        carry[k, 0] = state[:EXT] + one_b * rest
    d_kv = jnp.concatenate(d_kvs, axis=0)
    lanes = pl.ds(pl.multiple_of(pair % per_block * PAIR, PAIR), PAIR)
    out_ref[(pair // per_block) ^ info[1], 32:, lanes] = d_kv

    @pl.when(step == pairs - 1)
    def _():
        for r in range(out_ref.shape[0]):
            back_in = dotg(q_up_ref[...], dq_ref[r], 1, 0) + dotg(
                kv_up_ref[...], out_ref[r, 32:, :], 1, 0
            )
            out_ref[r, :32, :] = (ADAPTER_SCALE * back_in).astype(BF)


def adapter_kernel(
    n_grp, info, dq_ref, rest_ref, mid_ref, normed_ref, att_ref, *refs
):
    blocks_in, (up_ref, oin_ref, wide_ref) = refs[:n_grp], refs[n_grp:]
    share = blocks_in[0].shape[1]
    q_width = dq_ref.shape[1]
    for r in range(n_grp):
        there = pl.ds(pl.multiple_of((info[1] ^ r) * share, share), share)
        mids = mid_ref[:, there]
        rest = rest_ref[r]
        both = jnp.concatenate([dq_ref[r], rest], axis=0)
        up = dotg(mids, both, 1, 1)
        oin = dotg(ADAPTER_SCALE * blocks_in[r][q_width:], att_ref[r, :q_width, :], 1, 1)
        wide = dotg(rest[:32], normed_ref[there, :], 1, 0)
        up_ref[...] = up if r == 0 else up_ref[...] + up
        oin_ref[...] = oin if r == 0 else oin_ref[...] + oin
        wide_ref[...] = wide if r == 0 else wide_ref[...] + wide


def pack_early_kernel(per, map_ref, oin_a, oin_b, out_ref):
    heads = map_ref.shape[0]
    at = 0
    for k in range(heads):
        for g in range(0, per, 2):
            pair = [
                map_ref[k, h * STRETCH : (h + 1) * STRETCH, h * STRETCH : (h + 1) * STRETCH]
                for h in (g, g + 1)
            ]
            out_ref[at : at + STRETCH, :] = jnp.concatenate(pair, axis=1).astype(BF)
            at += STRETCH
    oin = oin_a[...] + oin_b[...]
    for c in range(oin.shape[1] // PAIR):
        out_ref[at : at + 16, :] = oin[:, c * PAIR : (c + 1) * PAIR].astype(BF)
        at += 16


def pack_late_kernel(
    q_width, up_a, up_b, key_ref, wide_in_a, wide_in_b, wide_out_a, wide_out_b, wide_ref, out_ref
):
    for c in range(wide_in_a.shape[1] // PAIR):
        cols = slice(c * PAIR, (c + 1) * PAIR)
        wide_in = wide_in_a[:24, cols] + wide_in_b[:24, cols]
        wide_out = wide_out_a[:8, cols] + wide_out_b[:8, cols]
        wide_ref[c * 32 : (c + 1) * 32, :] = jnp.concatenate([wide_in, wide_out], axis=0).astype(BF)
    up = ADAPTER_SCALE * (up_a[...] + up_b[...])
    at = 0
    for c in range(q_width // PAIR):
        out_ref[at : at + 16, :] = up[:16, c * PAIR : (c + 1) * PAIR].astype(BF)
        at += 16
    for k in range(key_ref.shape[0]):
        first = q_width + 32 + k * PAIR
        out_ref[at : at + 16, :] = up[8:24, first : first + PAIR].astype(BF)
        at += 16
    for k in range(key_ref.shape[0]):
        block = key_ref[k, :STRETCH, :]
        out_ref[at : at + STRETCH, :] = jnp.concatenate([block, block], axis=1).astype(BF)
        at += STRETCH


def unpack_kernel(
    n_grp, columns, info, early_a, early_b, late_a, late_b,
    wide_ref, q_ref, kv_ref, oin_ref, map_ref, key_ref, turned,
):
    early = early_a[...].astype(F32) + early_b[...].astype(F32)
    at = 0
    for h in range(0, map_ref.shape[0], 2):
        map_ref[h] = early[at : at + STRETCH, :STRETCH]
        map_ref[h + 1] = early[at : at + STRETCH, STRETCH:]
        at += STRETCH
    for c in range(oin_ref.shape[1] // PAIR):
        oin_ref[:, c * PAIR : (c + 1) * PAIR] = early[at : at + 8, :]
        at += 16
    first = (info[2] * n_grp + info[1]) * columns
    rows = pl.ds(pl.multiple_of((first // PAIR) * 32, 32), 32)
    sums = late_a[rows, :].astype(F32) + late_b[rows, :].astype(F32)
    turned[...] = jnp.transpose(sums)
    wide_ref[...] = turned[pl.ds(pl.multiple_of(first % PAIR, 8), columns), :]
    at = late_a.shape[0] - sum(
        [q_ref.shape[1] // PAIR * 16, key_ref.shape[0] * 16, key_ref.shape[0] * STRETCH]
    )
    late = late_a[at:, :].astype(F32) + late_b[at:, :].astype(F32)
    at = 0
    for c in range(q_ref.shape[1] // PAIR):
        q_ref[:, c * PAIR : (c + 1) * PAIR] = late[at : at + 8, :]
        at += 16
    for k in range(key_ref.shape[0]):
        cols = slice(k * STRETCH, (k + 1) * STRETCH)
        kv_ref[0, :, cols] = late[at : at + 8, :STRETCH]
        kv_ref[1, :, cols] = late[at + 8 : at + 16, STRETCH:]
        at += 16
    for k in range(key_ref.shape[0]):
        key_ref[k] = late[at : at + STRETCH, :STRETCH]
        at += STRETCH


def whole(shape):
    return pl.BlockSpec(shape, lambda i, *_: (0,) * len(shape))


def anywhere():
    return pl.BlockSpec(memory_space=pl.ANY)


def sds(shape, kind):
    return jax.ShapeDtypeStruct(shape, kind)


def call(
    kernel, name, grid, scalars, ins, in_specs, out_specs, out_shape, scratch=(), alias=None,
    cost=1024,
):
    return pl.pallas_call(
        kernel,
        grid_spec=pltpu.PrefetchScalarGridSpec(
            num_scalar_prefetch=len(scalars),
            grid=(grid,),
            in_specs=in_specs,
            out_specs=out_specs,
            scratch_shapes=list(scratch),
        ),
        out_shape=out_shape,
        input_output_aliases=alias or {},
        cost_estimate=pl.CostEstimate(flops=0, transcendentals=0, bytes_accessed=cost),
        compiler_params=pltpu.CompilerParams(
            dimension_semantics=("arbitrary",),
            vmem_limit_bytes=VMEM_LIMIT if name == "feed_forward" else SMALL_LIMIT,
        ),
        name=name,
    )(*scalars, *ins)


def run_assemble(info, ring, splits):
    shape = ring.parts[0].shape
    parts_of = ring_layout(ring.count, shape[0])
    outs = [(size, shape[1] * ring.count) for size in splits]
    return call(
        functools.partial(assemble_kernel, parts_of, shape[1], splits), "assemble", 1, [info],
        ring.parts, [whole(part.shape) for part in ring.parts], [whole(out) for out in outs],
        [sds(out, BF) for out in outs],
    )


def run_layout(info, lens, blocks):
    count = lax.axis_size("seq")
    size = lens.shape[0] * TABLE_ROWS * table_width(blocks, count)
    return call(
        functools.partial(layout_kernel, blocks, max(1, count // 4), count), "layout", 1,
        [info, lens], [], [], pl.BlockSpec(memory_space=pltpu.SMEM), sds((size,), jnp.int32),
    )


def run_layer(table, ends, sign):
    count = lax.axis_size("seq")
    batches, heads = ends[0].shape[:2]
    full = sds((batches, heads, EXT, PAIR), BF)
    out = [sds(ends[0].shape, BF), full]
    per_batch = table.shape[0] // batches // TABLE_ROWS
    blocks = max(per_batch - 4, 0)
    return call(
        functools.partial(layer_kernel, sign, blocks, count, len(ends)), "layer", 1, [table], ends,
        [whole(item.shape) for item in ends], [whole(item.shape) for item in out], out,
    )


def run_project(table, batch, normed, weight, q_up, kv_up, maps):
    rows, model = normed.shape
    heads = maps.shape[0]
    width = heads * PAIR
    q_width = weight.shape[0] - 32 - width
    tile = 4 * PAIR
    pairs = rows // PAIR
    return call(
        functools.partial(
            project_kernel, batch, q_width, rows // STRETCH, lax.axis_size("seq")
        ),
        "project_states", rows // tile, [table],
        [normed, weight, q_up, kv_up, maps],
        [
            pl.BlockSpec((tile, model), lambda i, *_: (i, 0)),
            whole(weight.shape), whole(q_up.shape), whole(kv_up.shape), whole(maps.shape),
        ],
        [
            pl.BlockSpec((q_width, tile), lambda i, *_: (0, i)),
            pl.BlockSpec((tile, width), lambda i, *_: (i, 0)),
            pl.BlockSpec((tile, width), lambda i, *_: (i, 0)),
            pl.BlockSpec((32, tile), lambda i, *_: (0, i)),
            pl.BlockSpec((width, tile), lambda i, *_: (0, i)),
            pl.BlockSpec((4, heads, 2 * EXT, PAIR), lambda i, *_: (i, 0, 0, 0)),
            whole((heads, 2 * PAIR + 32, PAIR)),
        ],
        [
            sds((q_width, rows), BF),
            sds((rows, width), BF),
            sds((rows, width), BF),
            sds((32, rows), BF),
            sds((width, rows), BF),
            sds((pairs, heads, 2 * EXT, PAIR), F32),
            sds((heads, 2 * PAIR + 32, PAIR), BF),
        ],
        [pltpu.VMEM((heads, EXT, PAIR), F32)],
    )


def run_forward(info, table, batch, q, kv, ve, maps, o_in, states, fars):
    q_width, rows = q.shape
    width = kv.shape[1]
    heads, pairs = width // PAIR, rows // PAIR
    per = q_width // STRETCH // heads
    count = lax.axis_size("seq")
    wide = max(1, count // 4)
    scale = STRETCH ** (-0.5) * math.log2(math.e)
    step = lambda *shape: pl.BlockSpec((1,) + shape, lambda i, *_: (i,) + (0,) * len(shape))
    column = lambda n: pl.BlockSpec((n, PAIR), lambda i, *_: (0, i))
    share = rows // lax.axis_size("grp")
    return call(
        functools.partial(
            forward_kernel, batch, per, rows // STRETCH, wide, count, len(fars), scale
        ),
        "attention_forward", pairs, [info, table],
        [q, kv, ve, maps, o_in, states, *fars],
        [
            column(q_width), whole(kv.shape), whole(ve.shape),
            whole(maps.shape), whole(o_in.shape), step(heads, 2 * EXT, PAIR),
            *[whole(far.shape) for far in fars],
        ],
        [
            block_spec(q_width + 16, share, lambda i: i), step(heads, WIN, per * PAIR),
            step(heads, PAIR, per * PAIR), step(heads, 2 * EXT, PAIR), step(heads * per, PAIR),
        ],
        [
            sds((rows // share, q_width + 16, share), BF),
            sds((pairs, heads, WIN, per * PAIR), BF),
            sds((pairs, heads, PAIR, per * PAIR), BF),
            sds((pairs, heads, 2 * EXT, PAIR), BF),
            sds((pairs, heads * per, PAIR), F32),
        ],
        [
            pltpu.VMEM((heads, 2, EXT, PAIR), F32),
            pltpu.VMEM((rows + STRETCH, width), BF),
            pltpu.VMEM((rows + STRETCH, width), BF),
        ],
    )


def block_spec(height, share, pair_of):
    per_block = share // PAIR
    return pl.BlockSpec(
        (1, height, PAIR),
        lambda i, info, *_: ((pair_of(i) // per_block) ^ info[1], 0, pair_of(i) % per_block),
    )


def own_spec(batch, share, model):
    return pl.BlockSpec((1, share, model), lambda i, info: (batch, info[1], 0))


def front(array):
    if len(array.shape) == 2:
        return whole(array.shape)
    return pl.BlockSpec((1,) + array.shape[1:], lambda i, *_: (0, 0, 0))


def run_residual(info, batch, tokens, gain, atts, weights):
    n_grp = len(atts)
    model = tokens.shape[2]
    share = atts[0].shape[-1]
    return call(
        functools.partial(residual_kernel, n_grp), "residual", 1, [info],
        [tokens, gain, *atts, *weights],
        [own_spec(batch, share, model), whole(gain.shape), *[front(att) for att in atts]]
        + [anywhere()] * n_grp,
        [whole((share, model)), whole((share, model)), whole((16, share))],
        [sds((share, model), F32), sds((share, model), BF), sds((16, share), BF)],
        [
            pltpu.VMEM((n_grp,) + weights[0].shape, BF),
            pltpu.SemaphoreType.DMA((n_grp,)),
        ],
    )


def run_branch(info, batch, cotangent, resid, gain, mid, summands, weights):
    n_grp = len(weights)
    share, model = resid.shape
    out = (weights[0].shape[0], share)
    return call(
        functools.partial(branch_kernel, n_grp, len(summands)), "branch_gradient", 1, [info],
        [cotangent, resid, gain, mid, *summands, *weights],
        [
            own_spec(batch, share, model), whole(resid.shape), whole(gain.shape),
            whole(mid.shape), *[whole(resid.shape) for _ in summands],
        ]
        + [anywhere()] * n_grp,
        [whole((share, model)), whole((16, model))] + [whole(out)] * n_grp,
        [sds((share, model), F32), sds((16, model), F32)] + [sds(out, BF)] * n_grp,
        [
            pltpu.VMEM((n_grp,) + weights[0].shape, BF),
            pltpu.SemaphoreType.DMA((n_grp,)),
        ],
        cost=LATE_COST,
    )


def run_tokens(info, batch, tokens, gain, d_resid, dqs, rests, weights, prev):
    n_grp = len(weights)
    batches, _, model = tokens.shape
    share = d_resid.shape[0]
    ins = [tokens, gain, d_resid, *dqs, *rests, *weights]
    specs = [
        own_spec(batch, share, model), whole(gain.shape), whole(d_resid.shape),
        *[front(a) for a in [*dqs, *rests]],
    ] + [anywhere()] * n_grp
    alias = {}
    if prev is not None:
        alias = {len(ins) + 1: 0}
        ins.append(prev)
        specs.append(anywhere())
    return call(
        functools.partial(tokens_kernel, n_grp), "token_gradient", 1, [info], ins, specs,
        pl.BlockSpec((1, share, model), lambda i, *_: (batch, 0, 0)),
        sds((batches, share, model), F32),
        [
            pltpu.VMEM((n_grp,) + weights[0].shape, BF),
            pltpu.VMEM((share, model), F32),
            pltpu.SemaphoreType.DMA((n_grp,)),
        ],
        alias,
        LATE_COST,
    )


def run_mlp(info, batch, xs, rels, cotangent, rings, prevs, sizes):
    n_grp = len(xs)
    share, model = xs[0].shape
    rows = share * n_grp
    depth = rings[0].parts[0].shape[0]
    layout = ring_layout(rings[0].count, depth)
    first = prevs is None
    prevs = [] if first else list(prevs)
    ins = [*xs, cotangent, *[part for ring in rings for part in ring.parts], *prevs]
    if first:
        out_shape = [sds((rows, model), BF)] * 2
    else:
        out_shape = [sds((share, model), BF)] * (2 * n_grp)
    scratch = [
        pltpu.VMEM((rows, model), BF),
        pltpu.VMEM((rows, model), BF),
        pltpu.VMEM((2, model, 3 * CHUNK), BF),
        pltpu.VMEM((rows, model), F32),
        pltpu.VMEM((rows, model), F32),
        pltpu.SemaphoreType.DMA((rows // ROW_TILE + 1,)),
        pltpu.SemaphoreType.DMA((2,)),
    ] + [pltpu.VMEM((rows, model), BF) for _ in prevs]
    return call(
        functools.partial(mlp_kernel, batch, rels, layout, sizes, first),
        "feed_forward", sum(sizes) // CHUNK, [info], ins, [anywhere()] * len(ins),
        [anywhere()] * len(out_shape), out_shape, scratch,
    )


def run_backward(
    info, table, batch, q, kv, ve, maps, o_in, att, weights, phi, states, inverse, fars, d_outs, prevs,
):
    q_width, rows = q.shape
    width = kv.shape[1]
    heads, pairs = width // PAIR, rows // PAIR
    per = q_width // STRETCH // heads
    share = rows // len(d_outs)
    count = lax.axis_size("seq")
    rev = lambda i: pairs - 1 - i
    step = lambda *shape: pl.BlockSpec((1,) + shape, lambda i, *_: (rev(i),) + (0,) * len(shape))
    column = lambda n: pl.BlockSpec((n, PAIR), lambda i, *_: (0, rev(i)))
    prevs = list(prevs or [])
    sums = [sds(maps.shape, F32)]
    return call(
        functools.partial(
            backward_kernel, batch, per, pairs, len(d_outs), bool(prevs), count, max(1, count // 4),
            len(fars), STRETCH ** (-0.5),
        ),
        "attention_backward", pairs, [info, table],
        [q, kv, ve, maps, o_in, att, weights, phi, states, inverse, *fars, *d_outs, *prevs],
        [
            column(q_width), whole(kv.shape), whole(ve.shape),
            whole(maps.shape), whole(o_in.shape), block_spec(q_width + 16, share, rev),
            step(heads, WIN, per * PAIR), step(heads, PAIR, per * PAIR),
            step(heads, 2 * EXT, PAIR), step(heads * per, PAIR),
            *[whole(far.shape) for far in fars], *[anywhere() for _ in d_outs],
            *[whole(prev.shape) for prev in prevs],
        ],
        [
            block_spec(q_width, share, rev), whole((rows + STRETCH, width)), step(heads, 2 * EXT, PAIR),
            whole((heads, 2 * EXT + STRETCH, PAIR)), *[whole(item.shape) for item in sums],
        ],
        [
            sds((rows // share, q_width, share), BF),
            sds((rows + STRETCH, width), F32),
            sds((pairs, heads, 2 * EXT, PAIR), F32),
            sds((heads, 2 * EXT + STRETCH, PAIR), BF),
            *sums,
        ],
        [
            pltpu.VMEM((heads, EXT, PAIR), F32),
            pltpu.VMEM((rows + STRETCH, width), BF),
            pltpu.VMEM((rows + STRETCH, width), BF),
            pltpu.VMEM((pairs, q_width + 16, PAIR), BF),
            pltpu.SemaphoreType.DMA,
        ],
        cost=LATE_COST,
    )


def run_keys(
    info, table, batch, kv, ve, maps, phi, d_kv, d_states, d_q, q_up, kv_up, fars, prevs,
):
    width, rows = phi.shape
    heads, pairs = width // PAIR, rows // PAIR
    n_grp, q_width, share = d_q.shape
    count = lax.axis_size("seq")
    wide = max(1, count // 4)
    rev = lambda i: pairs - 1 - i
    column = lambda n: pl.BlockSpec((n, PAIR), lambda i, *_: (0, rev(i)))
    lines = lambda n: pl.BlockSpec((PAIR, n), lambda i, *_: (rev(i), 0))
    prevs = list(prevs or [])
    sums = [sds((heads, PAIR, STRETCH), F32)]
    return call(
        functools.partial(
            keys_kernel, batch, pairs, share // PAIR, wide, count, len(fars), bool(prevs)
        ),
        "attention_keys", pairs, [info, table],
        [
            kv, ve, maps, phi, d_kv, d_states, d_q, q_up, kv_up, *fars, *prevs,
        ],
        [
            lines(width), lines(width), whole(maps.shape), column(width), whole(d_kv.shape),
            pl.BlockSpec((1, heads, 2 * EXT, PAIR), lambda i, *_: (rev(i), 0, 0, 0)),
            whole(d_q.shape), whole(q_up.shape), whole(kv_up.shape),
            *[whole(far.shape) for far in fars], *[whole(prev.shape) for prev in prevs],
        ],
        [whole((n_grp, 32 + width, share)), *[whole(item.shape) for item in sums]],
        [sds((n_grp, 32 + width, share), BF), *sums],
        [pltpu.VMEM((heads, 2, EXT, PAIR), F32), pltpu.VMEM((heads, STRETCH, PAIR), F32)],
        cost=LATE_COST,
    )


def run_adapters(info, d_q, rest, mids, normed, att, d_outs):
    model = normed.shape[1]
    ins = [d_q, rest, mids, normed, att, *d_outs]
    out_shape = [
        sds((32, d_q.shape[1] + rest.shape[1]), F32), sds((16, d_q.shape[1]), F32),
        sds((32, model), F32),
    ]
    return call(
        functools.partial(adapter_kernel, len(d_outs)),
        "adapter_gradients", 1, [info], ins, [whole(item.shape) for item in ins],
        [whole(item.shape) for item in out_shape], out_shape,
        cost=LATE_COST,
    )


def run_plain(kernel, name, scalars, ins, out_shape, scratch=()):
    return call(
        kernel, name, 1, scalars, ins, [whole(item.shape) for item in ins],
        [whole(item.shape) for item in out_shape], out_shape, scratch,
    )


def group_sum(value):
    total = value.astype(F32)
    for r in range(1, lax.axis_size("grp")):
        total = total + flip(value, "grp", r).astype(F32)
    return total.astype(BF)


def local(
    tokens,
    cotangent,
    lengths,
    attention_norm_gain,
    feedforward_norm_gain,
    query_weight,
    keyvalue_weight,
    output_weight,
    gate_up_weight,
    down_weight,
    adapter_width_factor,
    query_up_factor,
    keyvalue_up_factor,
    output_input_factor,
    query_feature_weight,
    key_feature_weight,
):
    batches, rows, model = tokens.shape
    n_seq, n_grp = lax.axis_size("seq"), lax.axis_size("grp")
    group_index, seq_index = lax.axis_index("grp"), lax.axis_index("seq")
    share = rows // n_grp
    rank = adapter_width_factor.shape[2]
    depth, q_width = query_weight.shape
    kv_heads = key_feature_weight.shape[0]
    kv_width = kv_heads * PAIR
    per = query_feature_weight.shape[0] // kv_heads
    hidden_width = down_weight.shape[0]
    gain_attn = attention_norm_gain.astype(F32)[None]
    gain_mlp = feedforward_norm_gain.astype(F32)[None]

    sources = lax.dynamic_index_in_dim(
        jnp.asarray(ring_sources(n_seq), jnp.int32), seq_index, 0, False
    )
    info = jnp.concatenate(
        [jnp.stack([seq_index * (rows // STRETCH), group_index, seq_index]).astype(jnp.int32), sources]
    )

    kv_shard = (
        keyvalue_weight.reshape(depth, 2, kv_heads, STRETCH)
        .transpose(2, 1, 3, 0)
        .reshape(kv_width, depth)
    )
    adapters = adapter_width_factor.transpose(0, 2, 1)
    pad = jnp.zeros((rank, depth), BF)
    in_ring = Ring(
        jnp.concatenate(
            [
                query_weight.T, adapters[:3].reshape(3 * rank, depth), pad, kv_shard,
                output_weight, adapters[3], pad,
            ],
            axis=0,
        )
    )
    down_t = down_weight.T
    half_shards = [
        jnp.concatenate(
            [
                gate_up_weight[:, 0, first : first + size],
                gate_up_weight[:, 1, first : first + size],
                down_t[:, first : first + size],
            ],
            axis=1,
        )
        for first, size in pieces_of(hidden_width)
    ]
    ring_a, ring_c = [Ring(shard) for shard in half_shards]
    kv_parts = keyvalue_up_factor.reshape(2, rank, kv_heads, STRETCH)
    kv_up = jnp.zeros((2, rank, kv_heads, 2, STRETCH), BF)
    kv_up = kv_up.at[0, :, :, 0].set(kv_parts[0]).at[1, :, :, 1].set(kv_parts[1])
    kv_up = kv_up.reshape(2 * rank, kv_width)
    kv_up = jnp.concatenate(
        [jnp.zeros((rank, kv_width), BF), kv_up, jnp.zeros((rank, kv_width), BF)]
    )
    q_up = jnp.concatenate([query_up_factor, jnp.zeros((3 * rank, q_width), BF)])
    q_up_t = q_up.T
    o_in = jnp.concatenate([output_input_factor, jnp.zeros((q_width, rank), BF)], axis=1)
    maps_t = query_feature_weight.transpose(0, 2, 1).reshape(kv_heads, per, STRETCH, STRETCH)
    query_maps = jnp.zeros((kv_heads, per, STRETCH, per, STRETCH), BF)
    for g in range(per):
        query_maps = query_maps.at[:, g, :, g, :].set(maps_t[:, g])
    query_maps = query_maps.reshape(kv_heads, per * STRETCH, per * STRETCH)
    key_maps = jnp.concatenate(
        [key_feature_weight.transpose(0, 2, 1), jnp.zeros((kv_heads, STRETCH, STRETCH), BF)], axis=2
    )

    normed_rows = []
    for batch in range(batches):
        x = tokens[batch].astype(F32)
        factor = lax.rsqrt(jnp.mean(x * x, axis=-1, keepdims=True) + EPS)
        normed_rows.append((x * factor * gain_attn).astype(BF))
    in_ring.hop()
    in_ring.hop()
    table = run_layout(info, lengths, rows // STRETCH)
    table, query_maps, key_maps, kv_up, q_up_t, normed_rows[0] = in_ring.tie(
        table, query_maps, key_maps, kv_up, q_up_t, normed_rows[0]
    )
    in_ring.hop()
    normed_rows[1] = in_ring.tie(normed_rows[1])[0]
    while in_ring.done < in_ring.hops():
        in_ring.hop()
    ring_a.hop(*in_ring.parts[-2:])
    weight_in, weight_out = run_assemble(
        info, in_ring, [q_width + 32 + kv_width, q_width + 2 * rank]
    )
    far_out = far_gather(weight_out)

    saved = []
    for batch in range(batches):
        normed = normed_rows[batch]
        q, kv, ve, mids, phi_key, states, ends = run_project(
            table, batch, normed, weight_in, q_up_t, kv_up, key_maps
        )
        saved.append([q, kv, ve, mids, normed, phi_key, states, ends])
    ends = jnp.stack([item[7] for item in saved])
    (ends,) = ring_a.tie(ends)
    fars = exchange(table, ends, 1)
    for item in saved:
        item[7] = fars
    far_out = [far_out[0]] + [after(far, *fars[1:]) for far in far_out[1:]]
    weights_out = near_gather(far_out)
    ring_a.hop(*fars[1:])

    attended, att_sets, far_mlp, mlp_ins = [], [], [], []
    for batch in range(batches):
        q, kv, ve, mids, normed, phi_key, states, fars = saved[batch]
        if batch:
            q = after(q, att)
        att, weights, phi, sums, inverse = run_forward(
            info, table, batch, q, kv, ve, query_maps, o_in, states, fars
        )
        atts = group_exchange([att[r] for r in range(n_grp)])
        att_sets.append([att, *atts[1:]])
        attended.append([att, weights, phi, sums, inverse])
    att_sets[0][0], att_sets[1][0] = ring_a.tie(att_sets[0][0], att_sets[1][0])
    ring_a.hop()
    for batch in range(batches):
        if batch:
            att_sets[1][0] = after(att_sets[1][0], mlp_in)
        resid, mlp_in, mid = run_residual(
            info, batch, tokens, gain_mlp, att_sets[batch], weights_out
        )
        attended[batch] += [resid, mid]
        if batch:
            mlp_in, *far_mlp[0][1:] = ring_a.tie(mlp_in, *far_mlp[0][1:])
            ring_a.hop()
        else:
            mlp_in, *att_sets[1][2:] = lax.optimization_barrier((mlp_in, *att_sets[1][2:]))
        far_mlp.append(far_gather(mlp_in))
    ring_a.finish()
    ring_c.hop(*ring_a.parts[-2:])
    far_mlp[1] = list(lax.optimization_barrier((*far_mlp[1], *ring_a.parts[-2:])))[: len(far_mlp[1])]
    far_mlp[0][0] = after(far_mlp[0][0], *far_mlp[1][1:])
    for batch in range(batches):
        mlp_ins.append(near_gather(far_mlp[batch]))

    sizes = [size for _, size in pieces_of(hidden_width)]
    partial = [None] * batches
    every = list(range(n_grp))
    partial[0] = list(
        run_mlp(info, 0, mlp_ins[0], every, cotangent, [ring_a], None, sizes[:1])
    )
    partial[0][0], mlp_ins[1][0] = ring_c.tie(partial[0][0], mlp_ins[1][0])
    ring_c.hop()
    far_in = far_gather(after(weight_in, partial[0][0], *mlp_ins[1][2:]))
    partial[1] = list(
        run_mlp(info, 1, mlp_ins[1], every, cotangent, [ring_a], None, sizes[:1])
    )
    (partial[1][0],) = ring_c.tie(partial[1][0])
    ring_c.hop()
    ring_c.finish()
    far_in, partial[0][0] = lax.optimization_barrier((far_in, partial[0][0]))
    weights_in = near_gather(far_in)
    partial[0] = list(
        run_mlp(info, 0, mlp_ins[0], every, cotangent, [ring_c], partial[0], sizes[1:])
    )
    started = [scatter_start(partial[0][:n_grp])]
    started[0][0][0], partial[1][0] = lax.optimization_barrier((started[0][0][0], partial[1][0]))
    def run_branch_of(batch, summands):
        resid, mid = attended[batch][5:]
        d_resid, wide, *d_out = run_branch(
            info, batch, cotangent, resid, gain_mlp, mid, summands, weights_out
        )
        return d_resid, wide, group_exchange(d_out)

    def run_backward_of(batch, q, d_outs, sums_back):
        _, kv, ve, mids, normed, phi_key, states, fars = saved[batch]
        att, weights, phi, sums, inverse = attended[batch][:5]
        d_q, d_kv, d_states, ends, *sums_back = run_backward(
            info, table, batch, q, kv, ve, query_maps, o_in, att, weights, phi, sums, inverse, fars,
            d_outs, sums_back,
        )
        return [d_q, None, d_kv, d_states], ends, sums_back

    def run_keys_of(batch, kv, gone, sums_keys):
        _, _, ve, mids, normed, phi_key, states, _ = saved[batch]
        d_q, d_qs, d_kv, d_states, fars = gone
        rest, *sums_keys = run_keys(
            info, table, batch, kv, ve, key_maps, phi_key, d_kv, d_states, d_q, q_up, kv_up, fars,
            sums_keys,
        )
        rests = group_exchange([rest[r] for r in range(n_grp)])
        return [rest, *rests[1:]], sums_keys

    def run_adapters_of(batch, d_q, rest, d_outs):
        return run_adapters(
            info, d_q, rest, saved[batch][3], saved[batch][4], attended[batch][0], d_outs
        )

    def run_tokens_of(batch, d_resid, gone, rests, prev):
        d_q, d_qs = gone[:2]
        return run_tokens(
            info, batch, tokens, gain_attn, d_resid, [d_q, *d_qs[1:]], rests, weights_in, prev
        )

    def finish_rows(batch, *ready):
        blocks = partial[batch][n_grp:]
        blocks[0] = after(blocks[0], *ready)
        blocks[1], blocks[-1] = after(blocks[1], *ready), after(blocks[-1], *ready)
        return scatter_start(blocks)

    def rows_of(batch, summands):
        total = attended[batch][5]
        for summand in summands:
            total = total + summand.astype(F32)
        return total.astype(BF)

    low = n_grp // 2
    upper = run_mlp(
        info, 1, mlp_ins[1][low:], every[low:], cotangent, [ring_c], partial[1], sizes[1:]
    )
    summands_a = scatter_end(*started[0])
    crossed = [flip(upper[far + 1 - low], "grp", 1) for far in range(low, n_grp, 2)]
    crossed[0], summands_a[-1] = lax.optimization_barrier((crossed[0], summands_a[-1]))
    far_b = [
        (upper[far - low].astype(F32) + there.astype(F32)).astype(BF)
        for far, there in zip(range(low, n_grp, 2), crossed)
    ]
    attended[0][6] = after(attended[0][6], far_b[0])
    d_resid_a, wide_a, d_outs_a = run_branch_of(0, summands_a)
    partial[1][0] = after(partial[1][0], d_resid_a)
    lower = list(
        run_mlp(info, 1, mlp_ins[1][:low], every[:low], cotangent, [ring_c], partial[1], sizes[1:])
    )
    late_b = scatter_end(far_b, [])
    lower[1], late_b[-1] = lax.optimization_barrier((lower[1], late_b[-1]))
    near_b = [lower[0], flip(lower[1], "grp", 1)]
    early_b = [far_pair(lower[far], lower[far + 1]) for far in range(2, low, 2)]
    summands_b = near_b + scatter_end(early_b, []) + late_b
    partial[1] = [None] * n_grp + list(lower[low:]) + list(upper[low:])
    attended[1][6] = after(attended[1][6], *d_outs_a[2:])
    d_resid_b, wide_b, d_outs_b = run_branch_of(1, summands_b)
    gone_a, ends_a, sums_back = run_backward_of(
        0, after(saved[0][0], d_resid_b), d_outs_a, None
    )
    blocks = partial[0][n_grp:]
    crossed = [flip(after(blocks[r + 1], d_resid_b), "grp", 1) for r in range(0, n_grp, 2)]
    crossed[-1] = after(crossed[-1], gone_a[0], *d_outs_b[2:])
    fars_a = [
        (blocks[r].astype(F32) + crossed[r // 2].astype(F32)).astype(BF)
        for r in range(2, n_grp, 2)
    ]
    rows_a = scatter_end(fars_a, [blocks[0], crossed[0]])
    gone_b, ends_b, sums_back = run_backward_of(
        1, after(saved[1][0], gone_a[0], *fars_a), d_outs_b, sums_back
    )
    fars = exchange(table, jnp.stack([ends_a, ends_b]), -1)
    gone_a.append(fars)
    gone_b.append(fars)
    for gone in (gone_a, gone_b):
        held = after(gone[0], gone_b[0])
        gone[1] = group_exchange([held[r] for r in range(n_grp)])
    kv_a, rows_a[-1] = lax.optimization_barrier((after(saved[0][1], gone_b[0]), rows_a[-1]))
    rests_a, sums_keys = run_keys_of(0, kv_a, gone_a, None)
    kv_b = after(saved[1][1], rests_a[0])
    kv_b = after(kv_b, *gone_a[1][1:], *gone_b[1][1:])
    rests_b, sums_keys = run_keys_of(1, kv_b, gone_b, sums_keys)
    sums_a = run_adapters_of(
        0, after(gone_a[0], rests_b[0]), rests_a[0], d_outs_a
    )
    fars_b, nears_b = finish_rows(1, rests_b[0])
    sums_b = run_adapters_of(
        1, after(gone_b[0], sums_a[0], *rests_a[1:]), rests_b[0], d_outs_b
    )

    (early,) = run_plain(
        functools.partial(pack_early_kernel, per), "pack_early", [],
        [sums_back[0], sums_a[1], sums_b[1]],
        [sds((STRETCH * kv_heads * per // 2 + 16 * (q_width // PAIR), PAIR), BF)],
    )
    late_rows = 16 * (q_width // PAIR) + (16 + STRETCH) * kv_heads
    wide_a = after(wide_a, fars_b[0])
    rows_b = scatter_end(fars_b, nears_b)
    wide, late = run_plain(
        functools.partial(pack_late_kernel, q_width), "pack_late", [],
        [sums_a[0], sums_b[0], sums_keys[0], sums_a[2], sums_b[2], wide_a, wide_b],
        [sds((32 * (model // PAIR), PAIR), BF), sds((late_rows, PAIR), BF)],
    )
    wide = group_sum(wide)
    wide = after(wide, *rests_b[1:])
    first = early.shape[0]
    columns = model // (n_seq * n_grp)
    value, bits = jnp.concatenate([early, wide, late]), n_seq.bit_length() - 1
    grad_tokens, held = None, [d_resid_a, d_resid_b]
    for step in range(bits):
        there = flip(value, "seq", 1 << step)
        batch = step - (bits - 2)
        if batch >= 0:
            gone, rests = ((gone_a, rests_a), (gone_b, rests_b))[batch]
            grad_tokens = run_tokens_of(
                batch, after(held[batch], value), gone, rests, grad_tokens
            )
            there, grad_tokens = lax.optimization_barrier((there, grad_tokens))
            if batch == 0:
                held[1], rows_b[-1] = lax.optimization_barrier((held[1], rows_b[-1]))
        if step < bits - 1:
            value = (value.astype(F32) + there.astype(F32)).astype(BF)
    packed = (value, there)
    block_rows = [rows_of(0, rows_a), rows_of(1, rows_b)]
    wide, q_grad, kv_grad, oin_grad, query_grad, key_grad = run_plain(
        functools.partial(unpack_kernel, n_grp, columns), "unpack", [info],
        [packed[0][:first], packed[1][:first], packed[0][first:], packed[1][first:]],
        [
            sds((columns, 32), F32), sds((rank, q_width), F32),
            sds((2, rank, kv_heads * STRETCH), F32), sds((rank, q_width), F32),
            sds(query_feature_weight.shape, F32), sds(key_feature_weight.shape, F32),
        ],
        [pltpu.VMEM((PAIR, 32), F32)],
    )
    return (
        jnp.stack(block_rows),
        grad_tokens,
        wide.reshape(columns, 4, rank).transpose(1, 0, 2),
        q_grad,
        kv_grad,
        oin_grad.T,
        query_grad,
        key_grad,
    )


def solution(mesh):
    return jax.shard_map(
        local,
        mesh=mesh,
        in_specs=(
            P(None, "seq", None),
            P(None, "seq", None),
            P(),
            P(),
            P(),
            P("seq", "grp"),
            P("seq", None, "grp"),
            P("grp", "seq"),
            P("seq", None, "grp"),
            P("grp", "seq"),
            P(None, "seq", None),
            P(None, "grp"),
            P(None, None, "grp"),
            P("grp", None),
            P("grp", None, None),
            P("grp", None, None),
        ),
        out_specs=(
            P(None, ("seq", "grp"), None),
            P(None, ("seq", "grp"), None),
            P(None, ("seq", "grp"), None),
            P(None, "grp"),
            P(None, None, "grp"),
            P("grp", None),
            P("grp", None, None),
            P("grp", None, None),
        ),
        check_vma=False,
    )
```

```python
import functools
import math

import jax
import jax.numpy as jnp
from jax import lax
from jax.experimental import pallas as pl
from jax.experimental.pallas import tpu as pltpu
from jax.sharding import PartitionSpec as P

STRETCH = 64
PAIR = 2 * STRETCH
WIN = 3 * STRETCH
EXT = 80
EPS = 1e-05
ADAPTER_SCALE = 2.0
BF = jnp.bfloat16
F32 = jnp.float32
VMEM_LIMIT = 58 * 1024 * 1024
CHUNK = 256
ROW_TILE = 512
LATE_COST = 2000000
SMALL_LIMIT = 32 * 1024 * 1024
LARGE = ("feed_forward", "project_states", "attention_forward", "residual", "branch_gradient")


def dotg(left, right, lc, rc):
    return lax.dot_general(left, right, (((lc,), (rc,)), ((), ())), preferred_element_type=F32)


def ring_order(count):
    if count % 8:
        return list(range(count))
    deep, wide = 4, count // 4
    path = [z * wide for z in range(deep)]
    for step, z in enumerate(reversed(range(deep))):
        ys = list(range(1, wide))
        path += [z * wide + y for y in (ys if step % 2 == 0 else ys[::-1])]
    return path


def ring_offsets(count):
    out = [0]
    for distance in range(1, (count + 1) // 2):
        out += [-distance, distance]
    return out + [count // 2]


def ring_sources(count):
    order = ring_order(count)
    return [[order[(order.index(s) + o) % count] for o in ring_offsets(count)] for s in range(count)]


def ring_cut(rows):
    return (rows // 2 + 15) // 16 * 16


def ring_layout(count, rows):
    cut = ring_cut(rows)
    return [(q, 0, rows) for q in range(count - 1)] + [
        (count - 1, 0, cut), (count - 1, cut, rows - cut),
    ]


def pieces_of(width):
    first = width // (2 * CHUNK) * CHUNK
    return [(0, first), (first, width - first)]


class Ring:
    def __init__(self, shard):
        self.count = lax.axis_size("seq")
        self.order = ring_order(self.count)
        self.parts = [shard]
        self.ahead = self.back = shard
        self.done = 0

    def move(self, value, step):
        pairs = [(self.order[i], self.order[(i + step) % self.count]) for i in range(self.count)]
        return lax.ppermute(value, "seq", pairs)

    def hop(self, *after):
        self.ahead, self.back, *_ = lax.optimization_barrier((self.ahead, self.back, *after))
        self.done += 1
        if self.done < (self.count + 1) // 2:
            self.ahead, self.back = self.move(self.ahead, 1), self.move(self.back, -1)
            self.parts += [self.ahead, self.back]
        else:
            cut = ring_cut(self.ahead.shape[0])
            self.parts += [self.move(self.ahead[:cut], 1), self.move(self.back[cut:], -1)]

    def hops(self):
        return (self.count + 1) // 2

    def tie(self, *values):
        self.ahead, self.back, *values = lax.optimization_barrier((self.ahead, self.back, *values))
        return values

    def finish(self):
        while self.done < self.hops():
            self.hop()
        return self


def after(value, *others):
    return lax.optimization_barrier((value, *others))[0]


def flip(value, axis, bit):
    count = lax.axis_size(axis)
    return lax.ppermute(value, axis, [(i, i ^ bit) for i in range(count)])


def shifted(value, axis, steps):
    count = lax.axis_size(axis)
    first, last = max(0, -steps), min(count, count - steps)
    return lax.ppermute(value, axis, [(i, i + steps) for i in range(first, last)])


def group_gather(share):
    count = lax.axis_size("grp")
    out = []
    for far in range(0, count, 2):
        mine = share if far == 0 else flip(share, "grp", far)
        out += [mine, flip(mine, "grp", 1)]
    return out


def far_gather(share):
    return [share] + [flip(share, "grp", far) for far in range(2, lax.axis_size("grp"), 2)]


def near_gather(fars):
    out = []
    for far in fars:
        out += [far, flip(far, "grp", 1)]
    return out


def group_exchange(blocks):
    return [blocks[0]] + [flip(blocks[r], "grp", r) for r in range(1, len(blocks))]


def far_pair(here, there):
    return (here.astype(F32) + flip(there, "grp", 1).astype(F32)).astype(BF)


def scatter_start(blocks):
    count = len(blocks)
    fars = []
    for far in range(2, count, 2):
        fars.append(far_pair(blocks[far], blocks[far + 1]))
    return fars, [blocks[0], flip(blocks[1], "grp", 1)]


def scatter_end(fars, nears):
    return nears + [flip(far, "grp", 2 * (i + 1)) for i, far in enumerate(fars)]


def exchange(table, ends, sign):
    count = lax.axis_size("seq")
    wide = max(1, count // 4)
    here = [flip(ends, "seq", j) for j in range(1, wide)]
    near, full = run_layer(table, [ends, *here], sign)
    out = here + [shifted(near, "seq", sign * wide)]
    return out + [shifted(full, "seq", sign * r * wide) for r in range(2, count // wide)]


VALID, ONE, TWO = range(3)
FULL, INNER, NEXT, LAYER_FULL, LAYER_INNER, LAYER_NEXT = range(6)
TABLE_ROWS = 15


def side_row(sign, row):
    return 3 + row + (0 if sign > 0 else 6)


def table_width(blocks, count):
    return max(blocks + 4, 2 * count)


def layout_kernel(blocks, wide, count, info, lens, out):
    width = table_width(blocks, count)
    base, seq = info[0], info[2]
    z, y = seq // wide, seq % wide
    for batch in range(lens.shape[0]):
        starts, ends, at = [], [], 0
        for i in range(lens.shape[1]):
            length = lens[batch, i]
            starts.append(at)
            ends.append(at * STRETCH + length)
            at = at + ((length + STRETCH - 1) >> 6)

        def owner(c):
            total = -1
            for start in starts:
                total = total + jnp.where(start <= c, 1, 0)
            return total

        def put(row, i, value):
            out[(batch * TABLE_ROWS + row) * width + i] = value

        owned = [owner(base + c) for c in range(-3, blocks + 3)]
        for i in range(blocks + 4):
            c = base + i - 1
            end = 0
            for start, stop in zip(starts, ends):
                end = jnp.where(start <= c, stop, end)
            put(VALID, i, jnp.clip(end - c * STRETCH, 0, STRETCH))
            put(ONE, i, jnp.where(owned[i + 2] == owned[i + 1], 1, 0))
            put(TWO, i, jnp.where(owned[i + 2] == owned[i], 1, 0))
        for sign in (1, -1):
            edge = base - 1 if sign > 0 else base + blocks
            outer, inner = owner(edge), owner(edge - sign)
            end_of = lambda device: device * blocks + (blocks - 1 if sign > 0 else 0)
            last = wide - 1 if sign > 0 else 0
            first = wide - 1 - last
            layer_end = end_of(z * wide + last)
            layer_outer, layer_inner = owner(layer_end), owner(layer_end - sign)
            for j in range(wide):
                source = z * wide + (y ^ j)
                far = (seq - source) * sign
                there = owner(end_of(source))
                put(side_row(sign, FULL), j, jnp.where((far > 0) & (there == outer), 1, 0))
                put(side_row(sign, INNER), j, jnp.where((far > 1) & (there == inner), 1, 0))
                put(side_row(sign, NEXT), j, jnp.where(far == 1, 1, 0))
                put(side_row(sign, LAYER_FULL), j, jnp.where(there == layer_outer, 1, 0))
                outermost = (y ^ j) == last
                put(side_row(sign, LAYER_NEXT), j, jnp.where(outermost, 1, 0))
                put(
                    side_row(sign, LAYER_INNER), j,
                    jnp.where((there == layer_inner) & (~outermost), 1, 0),
                )
            for r in range(1, count // wide):
                layer = z - sign * r
                inside = (layer >= 0) & (layer < count // wide)
                there = owner(end_of(layer * wide + last))
                i = wide + r
                direct = (y == first) if r == 1 else (y != y)
                put(side_row(sign, FULL), i, jnp.where(inside & (there == outer), 1, 0))
                put(
                    side_row(sign, INNER), i,
                    jnp.where(inside & (there == inner) & (~direct), 1, 0),
                )
                put(side_row(sign, NEXT), i, jnp.where(inside & direct, 1, 0))


class Slots:
    def __init__(self, table, batch, blocks, count):
        self.table, self.batch, self.width = table, batch, table_width(blocks, count)

    def at(self, row, i):
        return self.table[(self.batch * TABLE_ROWS + row) * self.width + i]

    def valid(self, c):
        return self.at(VALID, c + 1)

    def one(self, c):
        return self.at(ONE, c + 1)

    def weight_one(self, c):
        return self.one(c).astype(F32)

    def weight_two(self, c):
        return self.at(TWO, c + 1).astype(F32)


def entering(slots, arrays, wide, count, sign, place, near_k):
    inner = outer = jnp.zeros((EXT, PAIR), F32)
    rows = jnp.zeros((arrays[0].shape[2] - 2 * EXT, PAIR), F32)
    row = lambda name, i: slots.at(side_row(sign, name), i).astype(F32)
    for r in range(1, count // wide + wide - 1):
        layer = r >= wide
        i = r + 1 if layer else r
        array = arrays[r - 1]
        if r > wide:
            full = array[place, near_k].astype(F32)
        else:
            full = array[place, near_k, EXT : 2 * EXT].astype(F32)
            inner = inner + row(NEXT, i) * array[place, near_k, :EXT].astype(F32)
            rows = rows + row(NEXT, i) * array[place, near_k, 2 * EXT :].astype(F32)
        outer = outer + row(FULL, i) * full
        inner = inner + row(INNER, i) * full
    return inner, outer, rows


def layer_kernel(sign, blocks, count, wide, table, *refs):
    ends, (near_ref, full_ref) = refs[:wide], refs[wide:]
    for batch in range(near_ref.shape[0]):
        slots = Slots(table, batch, blocks, count)
        row = lambda name, i: slots.at(side_row(sign, name), i).astype(F32)
        for k in range(near_ref.shape[1]):
            full = inner = jnp.zeros((EXT, PAIR), F32)
            rows = jnp.zeros((near_ref.shape[2] - 2 * EXT, PAIR), F32)
            for j in range(wide):
                value = ends[j][batch, k, EXT : 2 * EXT].astype(F32)
                full = full + row(LAYER_FULL, j) * value
                inner = inner + row(LAYER_INNER, j) * value
                inner = inner + row(LAYER_NEXT, j) * ends[j][batch, k, :EXT].astype(F32)
                rows = rows + row(LAYER_NEXT, j) * ends[j][batch, k, 2 * EXT :].astype(F32)
            near_ref[batch, k, :EXT] = inner.astype(BF)
            near_ref[batch, k, EXT : 2 * EXT] = full.astype(BF)
            near_ref[batch, k, 2 * EXT :] = rows.astype(BF)
            full_ref[batch, k] = full.astype(BF)


def half_mask(shape):
    return (lax.broadcasted_iota(jnp.int32, shape, 1) & (PAIR - 1)) < STRETCH


def feature_softmax(u):
    top = jnp.exp(u - jnp.max(u, axis=0, keepdims=True))
    bottom = jnp.exp(jnp.min(u, axis=0, keepdims=True) - u)
    top = top * (1.0 / jnp.sum(top, axis=0, keepdims=True))
    bottom = bottom * (1.0 / jnp.sum(bottom, axis=0, keepdims=True))
    return jnp.concatenate([top, bottom], axis=0)


def feature_back(phi, d_phi):
    top, bottom = phi[:STRETCH].astype(F32), phi[STRETCH:].astype(F32)
    a, b = d_phi[:STRETCH], d_phi[STRETCH:]
    return top * (a - jnp.sum(top * a, axis=0, keepdims=True)) - bottom * (
        b - jnp.sum(bottom * b, axis=0, keepdims=True)
    )


def assemble_kernel(parts_of, width, splits, info, *refs):
    ins, outs = refs[: len(parts_of)], refs[len(parts_of) :]
    for (q, first, rows), ref in zip(parts_of, ins):
        column = pl.ds(pl.multiple_of(info[3 + q] * width, width), width)
        at = 0
        for out, size in zip(outs, splits):
            low, high = max(at, first), min(at + size, first + rows)
            if low < high:
                out[low - at : high - at, column] = ref[low - first : high - first, :]
            at += size


def project_kernel(
    batch, q_width, blocks, count, table, normed_ref, w_ref, up_ref, kv_up_ref, wk_ref,
    q_ref, kv_ref, ve_ref, mid_ref, phi_ref, st_ref, ends_ref, carry,
):
    step = pl.program_id(0)
    rows = normed_ref.shape[0]
    width = kv_ref.shape[1]
    heads = width // PAIR

    @pl.when(step == 0)
    def _():
        carry[...] = jnp.zeros_like(carry)

    normed = normed_ref[...]
    product = dotg(w_ref[...], normed, 1, 1)
    mixed = product[: q_width + 32]
    mids = mixed[q_width:].astype(BF)
    mid_ref[...] = mids
    query = mixed[:q_width] + ADAPTER_SCALE * dotg(up_ref[...], mids, 1, 0)
    q_ref[...] = query.astype(BF)
    kv_all = jnp.transpose(product[q_width + 32 :]) + ADAPTER_SCALE * dotg(
        mids, kv_up_ref[...], 0, 0
    )
    kv_all = kv_all.astype(BF)
    kv_ref[...] = kv_all

    slots = Slots(table, batch, blocks, count)
    lane = lax.broadcasted_iota(jnp.int32, (1, PAIR), 1)
    low = lane < STRETCH
    inside = lane & (STRETCH - 1)
    wide = lax.broadcasted_iota(jnp.int32, (PAIR, PAIR), 1)
    for sub in range(rows // PAIR):
        block = 2 * (step * (rows // PAIR) + sub)
        one_a, one_b = slots.weight_one(block), slots.weight_one(block + 1)
        valid = inside < jnp.where(low, slots.valid(block), slots.valid(block + 1))
        valid = jnp.where(valid, 1.0, 0.0)
        valid_low = jnp.where(low, valid, 0.0)
        valid_high = valid - valid_low
        at = sub * PAIR
        for k in range(heads):
            kv = kv_all[at : at + PAIR, k * PAIR : (k + 1) * PAIR]
            moved = pltpu.roll(kv.astype(F32), STRETCH, 1)
            ve = jnp.where(
                wide < STRETCH, moved, jnp.where(wide < STRETCH + 2, 1.0, 0.0)
            ).astype(BF)
            ve_ref[at : at + PAIR, k * PAIR : (k + 1) * PAIR] = ve
            if sub == rows // PAIR - 1:
                ends_ref[k, 2 * EXT : 2 * EXT + STRETCH] = kv[STRETCH:]
                ends_ref[k, 2 * EXT + STRETCH :] = ve[STRETCH:]
            phi = feature_softmax(dotg(wk_ref[k], kv, 1, 1))
            phi_ref[k * PAIR : (k + 1) * PAIR, at : at + PAIR] = (phi * valid).astype(BF)
            first = dotg(ve, (phi * valid_low).astype(BF), 0, 1)[:EXT]
            second = dotg(ve, (phi * valid_high).astype(BF), 0, 1)[:EXT]
            st_ref[sub, k, :EXT] = first
            st_ref[sub, k, EXT:] = second
            mid = carry[k] * one_a + first
            tail = mid * one_b + second
            carry[k] = tail
            ends_ref[k, :EXT] = mid.astype(BF)
            ends_ref[k, EXT : 2 * EXT] = tail.astype(BF)


def window_mask(slots, block):
    lane = lax.broadcasted_iota(jnp.int32, (1, PAIR), 1)
    low = lane < STRETCH
    before = slots.valid(block - 1) * slots.one(block)
    own = slots.valid(block)
    limits = [
        jnp.where(low, before, 0),
        jnp.where(low, jnp.minimum(lane + 1, own), own * slots.one(block + 1)),
        jnp.where(low, 0, jnp.minimum(lane - STRETCH + 1, slots.valid(block + 1))),
    ]
    row = lax.broadcasted_iota(jnp.int32, (STRETCH, PAIR), 0)
    return jnp.concatenate([jnp.where(row < limit, 1.0, 0.0) for limit in limits], axis=0)


def fill_window(k, kv_ref, ve_ref, rows, kv_all, ve_all):
    cols = slice(k * PAIR, (k + 1) * PAIR)
    kv_all[:STRETCH, cols] = rows[:STRETCH].astype(BF)
    ve_all[:STRETCH, cols] = rows[STRETCH:].astype(BF)
    kv_all[STRETCH:, cols] = kv_ref[:, cols]
    ve_all[STRETCH:, cols] = ve_ref[:, cols]


def forward_kernel(
    batch, per, blocks, wide, count, n_far, scale, info, table, q_ref, kv_ref, ve_ref,
    wq_ref, oin_ref, st_ref, *refs,
):
    fars = refs[:n_far]
    att_ref, w_ref, phi_ref, s_ref, r_ref, carry, kv_all, ve_all = refs[n_far:]
    step = pl.program_id(0)
    heads = kv_ref.shape[1] // PAIR
    slots = Slots(table, batch, blocks, count)
    block = 2 * step

    @pl.when(step == 0)
    def _():
        for k in range(heads):
            inner, outer, rows = entering(slots, fars, wide, count, 1, batch, k)
            fill_window(k, kv_ref, ve_ref, rows, kv_all, ve_all)
            carry[k, 0] = inner
            carry[k, 1] = outer

    one_a, one_b = slots.weight_one(block), slots.weight_one(block + 1)
    two_a, two_b = slots.weight_two(block), slots.weight_two(block + 1)
    mask = window_mask(slots, block)
    mask = jnp.concatenate([mask] * per, axis=1)
    lanes = per * PAIR
    low = half_mask((EXT, lanes))
    rows = pl.ds(pl.multiple_of(step * PAIR, PAIR), WIN)
    out_mid = jnp.zeros((16, PAIR), F32)
    for k in range(heads):
        kv = kv_all[rows, k * PAIR : (k + 1) * PAIR]
        ve = ve_all[rows, k * PAIR : (k + 1) * PAIR]
        base = k * per * STRETCH
        stacked = q_ref[base : base + per * STRETCH, :]
        q = jnp.concatenate(
            [stacked[g * STRETCH : (g + 1) * STRETCH] for g in range(per)], axis=1
        )
        q = jnp.concatenate([q, jnp.zeros_like(q)], axis=0)
        scores = dotg(kv, q, 1, 0)
        weights = (jnp.exp2(scores * scale) * mask).astype(BF)
        w_ref[0, k] = weights
        mixed = dotg(wq_ref[k], stacked, 1, 0)
        phi = jnp.concatenate(
            [
                feature_softmax(mixed[g * STRETCH : (g + 1) * STRETCH]).astype(BF)
                for g in range(per)
            ],
            axis=1,
        )
        phi_ref[0, k] = phi
        older, old = carry[k, 0], carry[k, 1]
        states = jnp.concatenate([older * two_a, old * two_b], axis=0).astype(BF)
        s_ref[0, k] = states
        linear = dotg(states, phi, 1, 0)
        total = dotg(ve, weights, 0, 0)[:EXT] + jnp.where(low, linear[:EXT], linear[EXT:])
        inverse = 1.0 / total[STRETCH : STRETCH + 1]
        att = (total[:STRETCH] * inverse).astype(BF)
        att = jnp.concatenate([att[:, g * PAIR : (g + 1) * PAIR] for g in range(per)], axis=0)
        att_ref[0, base : base + per * STRETCH, :] = att
        out_mid = out_mid + dotg(oin_ref[base : base + per * STRETCH, :], att, 0, 0)
        for g in range(per):
            r_ref[0, k * per + g : k * per + g + 1, :] = inverse[:, g * PAIR : (g + 1) * PAIR]
        current = old * one_a + st_ref[0, k, :EXT]
        carry[k, 0] = current
        carry[k, 1] = current * one_b + st_ref[0, k, EXT:]
    att_ref[0, heads * per * STRETCH :, :] = (ADAPTER_SCALE * out_mid).astype(BF)


def residual_kernel(n_grp, info, x_ref, gain_ref, *refs):
    atts, weights = refs[:n_grp], refs[n_grp : 2 * n_grp]
    resid_ref, low_ref, mid_ref, buffer, sems = refs[2 * n_grp :]
    copies = [
        pltpu.make_async_copy(weights[r], buffer.at[r], sems.at[r]) for r in range(n_grp)
    ]
    for copy in copies:
        copy.start()
    q_width = buffer.shape[1] - 16
    resid_ref[...] = x_ref[0].astype(F32)
    mid = jnp.zeros(mid_ref.shape, F32)
    for r in range(n_grp):
        copies[r].wait()
        att = atts[r][0] if len(atts[r].shape) == 3 else atts[r][...]
        mid = mid + att[q_width:].astype(F32)
        resid_ref[...] += dotg(att, buffer[r], 0, 0)
    mid_ref[...] = mid.astype(BF)
    resid = resid_ref[...]
    factor = lax.rsqrt(jnp.mean(resid * resid, axis=1, keepdims=True) + EPS)
    low_ref[...] = (resid * factor * gain_ref[...]).astype(BF)


def branch_kernel(n_grp, n_sum, info, dy_ref, resid_ref, gain_ref, mid_ref, *refs):
    summands, refs = refs[:n_sum], refs[n_sum:]
    weights, refs = refs[:n_grp], refs[n_grp:]
    d_resid_ref, wide_ref, refs = refs[0], refs[1], refs[2:]
    outs, (buffer, sems) = refs[:n_grp], refs[n_grp:]
    copies = [
        pltpu.make_async_copy(weights[r], buffer.at[r], sems.at[r]) for r in range(n_grp)
    ]
    for copy in copies:
        copy.start()
    d_in = summands[0][...].astype(F32)
    for summand in summands[1:]:
        d_in = d_in + summand[...].astype(F32)
    resid = resid_ref[...]
    factor = lax.rsqrt(jnp.mean(resid * resid, axis=1, keepdims=True) + EPS)
    e = gain_ref[...] * d_in
    slope = factor * factor * factor * jnp.mean(resid * e, axis=1, keepdims=True)
    d_resid = dy_ref[0].astype(F32) + factor * e - resid * slope
    d_resid_ref[...] = d_resid
    low = d_resid.astype(BF)
    wide_ref[...] = dotg(mid_ref[...], low, 1, 0)
    for r in range(n_grp):
        copies[r].wait()
        outs[r][...] = dotg(buffer[r], low, 1, 1).astype(BF)


def tokens_kernel(n_grp, info, x_ref, gain_ref, d_resid_ref, *refs):
    dqs, rests, weights = refs[:n_grp], refs[n_grp : 2 * n_grp], refs[2 * n_grp : 3 * n_grp]
    out_ref, buffer, total, sems = refs[3 * n_grp :][-4:]
    copies = [
        pltpu.make_async_copy(weights[r], buffer.at[r], sems.at[r]) for r in range(n_grp)
    ]
    for copy in copies:
        copy.start()
    for r in range(n_grp):
        copies[r].wait()
        d_q = dqs[r][0] if len(dqs[r].shape) == 3 else dqs[r][...]
        rest = rests[r][0] if len(rests[r].shape) == 3 else rests[r][...]
        part = dotg(jnp.concatenate([d_q, rest], axis=0), buffer[r], 0, 0)
        if r:
            total[...] += part
        else:
            total[...] = part
    x = x_ref[0].astype(F32)
    factor = lax.rsqrt(jnp.mean(x * x, axis=1, keepdims=True) + EPS)
    e = gain_ref[...] * total[...]
    slope = factor * factor * factor * jnp.mean(x * e, axis=1, keepdims=True)
    out_ref[0] = d_resid_ref[...] + factor * e - x * slope


def mlp_kernel(
    batch, rels, layout, sizes, first_half, info, *refs,
):
    n_parts = len(layout)
    n_grp = len(rels)
    xs, refs = refs[:n_grp], refs[n_grp:]
    dy_hbm, refs = refs[0], refs[1:]
    part_sets = []
    for _ in sizes:
        part_sets.append(refs[:n_parts])
        refs = refs[n_parts:]
    n_prev = 0 if first_half else 2
    prevs, refs = refs[:n_prev], refs[n_prev:]
    n_out = 2 if first_half else 2 * n_grp
    outs, refs = refs[:n_out], refs[n_out:]
    x, dy, w, acc_out, acc_in, sem, wsem = refs[:7]
    j, n = pl.program_id(0), pl.num_programs(0)
    slot = j % 2
    share = xs[0].shape[0]
    rows_all = x.shape[0]
    depth = layout[0][2]

    def loads(jj, s, which):
        copies = []
        first_step = sum(sizes[:which]) // CHUNK
        for (q, first, rows), part in zip(layout, part_sets[which]):
            to = pl.ds(pl.multiple_of(info[3 + q] * depth + first, 16), rows)
            for kind in range(3):
                column = pl.multiple_of(kind * sizes[which] + (jj - first_step) * CHUNK, CHUNK)
                copies.append(
                    pltpu.make_async_copy(
                        part.at[:, pl.ds(column, CHUNK)],
                        w.at[s, to, pl.ds(kind * CHUNK, CHUNK)],
                        wsem.at[s],
                    )
                )
        return copies

    def start_loads(jj, s):
        for which in range(len(sizes)):
            low, high = sum(sizes[:which]) // CHUNK, sum(sizes[: which + 1]) // CHUNK

            @pl.when((jj >= low) & (jj < high))
            def _(which=which):
                for copy in loads(jj, s, which):
                    copy.start()

    per_tile = ROW_TILE // share

    def inputs(tile):
        copies = []
        for r in range(tile * per_tile, (tile + 1) * per_tile):
            rows = pl.ds(r * share, share)
            copies.append(pltpu.make_async_copy(xs[r], x.at[rows], sem.at[tile]))
            there = pl.ds(pl.multiple_of((info[1] ^ rels[r]) * share, share), share)
            copies.append(pltpu.make_async_copy(dy_hbm.at[batch, there], dy.at[rows], sem.at[tile]))
        return copies

    tiles = rows_all // ROW_TILE

    def earlier():
        part = pl.ds(rels[0] * share, rows_all)
        return [
            pltpu.make_async_copy(prev.at[part], refs[7 + i], sem.at[tiles])
            for i, prev in enumerate(prevs)
        ]

    def results():
        if first_half:
            return [
                pltpu.make_async_copy(x, outs[0], sem.at[0]),
                pltpu.make_async_copy(dy, outs[1], sem.at[1]),
            ]
        copies = []
        for r in range(n_grp):
            rows = pl.ds(r * share, share)
            copies.append(pltpu.make_async_copy(x.at[rows], outs[r], sem.at[0]))
            copies.append(pltpu.make_async_copy(dy.at[rows], outs[n_grp + r], sem.at[0]))
        return copies

    @pl.when(j == 0)
    def _():
        for copy in inputs(0):
            copy.start()
        start_loads(j, 0)
        for tile in range(1, tiles):
            for copy in inputs(tile):
                copy.start()
        for copy in earlier():
            copy.start()

    @pl.when(j + 1 < n)
    def _():
        start_loads(j + 1, 1 - slot)

    for copy in loads(0, slot, 0):
        copy.wait()
    gate_up_w = w.at[slot, :, pl.ds(0, 2 * CHUNK)]
    down_w = w.at[slot, :, pl.ds(2 * CHUNK, CHUNK)]

    def body(tile, start, end):
        rows = pl.ds(pl.multiple_of(tile * ROW_TILE, ROW_TILE), ROW_TILE)
        if start:
            for i in range(per_tile):
                part = pl.ds(pl.multiple_of(tile * ROW_TILE + i * share, share), share)
                pltpu.make_async_copy(xs[0], x.at[part], sem.at[tile]).wait()
                pltpu.make_async_copy(xs[0], dy.at[part], sem.at[tile]).wait()
        gate_up = dotg(x[rows, :], gate_up_w[...], 1, 0)
        d_hidden = dotg(dy[rows, :], down_w[...], 1, 0)
        gate, up = gate_up[:, :CHUNK], gate_up[:, CHUNK:]
        sig = 1.0 / (1.0 + jnp.exp(-gate))
        act = gate * sig
        hidden = (act * up).astype(BF)
        d_gate = (d_hidden * up * (sig + act * (1.0 - sig))).astype(BF)
        d_up = (d_hidden * act).astype(BF)
        out = dotg(hidden, down_w[...], 1, 1)
        d_in = dotg(jnp.concatenate([d_gate, d_up], axis=1), gate_up_w[...], 1, 1)
        if start:
            acc_out[rows, :] = out
            acc_in[rows, :] = d_in
        elif not end:
            acc_out[rows, :] += out
            acc_in[rows, :] += d_in
        else:
            out, d_in = acc_out[rows, :] + out, acc_in[rows, :] + d_in
            if not first_half:
                d_in = d_in + refs[7][rows, :].astype(F32)
                out = out + refs[8][rows, :].astype(F32)
            x[rows, :] = d_in.astype(BF)
            dy[rows, :] = out.astype(BF)
        return 0

    @pl.when(j == 0)
    def _():
        lax.fori_loop(0, tiles, lambda i, c: body(i, True, False), 0)

    @pl.when((j > 0) & (j < n - 1))
    def _():
        lax.fori_loop(0, tiles, lambda i, c: body(i, False, False), 0)

    @pl.when(j == n - 1)
    def _():
        for copy in earlier():
            copy.wait()
        lax.fori_loop(0, tiles, lambda i, c: body(i, False, True), 0)
        for copy in results():
            copy.start()
        for copy in results():
            copy.wait()


def backward_kernel(
    batch, per, pairs, n_grp, has_prev, count, wide, n_far, scale, info, table, q_ref, kv_ref, ve_ref, wq_ref,
    oin_ref, att_ref, w_ref, phi_ref, s_ref, r_ref, *refs,
):
    fars, refs = refs[:n_far], refs[n_far:]
    blocks_in, refs = refs[:n_grp], refs[n_grp:]
    prevs, refs = (refs[:1], refs[1:]) if has_prev else (None, refs)
    (
        dq_ref, dkv_ref, ds_ref, ends_ref, map_ref, carry, kv_all, ve_all, d_outs, sem,
    ) = refs
    step = pl.program_id(0)
    pair = pairs - 1 - step
    heads = kv_ref.shape[1] // PAIR
    slots = Slots(table, batch, 2 * pairs, count)
    block = 2 * pair
    q_width = q_ref.shape[0]
    per_block = blocks_in[0].shape[1] // PAIR

    @pl.when(step == 0)
    def _():
        copies = []
        for r in range(n_grp):
            for i in range(per_block):
                copies.append(
                    pltpu.make_async_copy(
                        blocks_in[r].at[:, pl.ds(i * PAIR, PAIR)],
                        d_outs.at[(info[1] ^ r) * per_block + i],
                        sem,
                    )
                )
        for copy in copies:
            copy.start()
        for k in range(heads):
            rows = entering(slots, fars, wide, count, 1, batch, k)[2]
            fill_window(k, kv_ref, ve_ref, rows, kv_all, ve_all)
        carry[...] = jnp.zeros_like(carry)
        dkv_ref[...] = jnp.zeros_like(dkv_ref)
        map_ref[...] = prevs[0][...] if has_prev else jnp.zeros_like(map_ref)
        for copy in copies:
            copy.wait()
    one_b = slots.weight_one(block + 1)
    one_c = slots.weight_one(block + 2)
    lanes = per * PAIR
    low = half_mask((EXT, lanes))
    rows = pl.ds(pl.multiple_of(pair * PAIR, PAIR), WIN)
    d_out = d_outs[pair]
    back_out = ADAPTER_SCALE * d_out[q_width:]
    d_att_all = d_out[:q_width].astype(F32) + dotg(oin_ref[...], back_out, 1, 0)
    for k in range(heads):
        kv = kv_all[rows, k * PAIR : (k + 1) * PAIR]
        ve = ve_all[rows, k * PAIR : (k + 1) * PAIR]
        base = k * per * STRETCH

        def side(value):
            return jnp.concatenate(
                [value[g * STRETCH : (g + 1) * STRETCH] for g in range(per)], axis=1
            )

        stacked = q_ref[base : base + per * STRETCH, :]
        q = side(stacked)
        d_att = side(d_att_all[base : base + per * STRETCH])
        att = side(att_ref[0, base : base + per * STRETCH, :]).astype(F32)
        inverse = jnp.concatenate(
            [r_ref[0, k * per + g : k * per + g + 1, :] for g in range(per)], axis=1
        )
        ratio = d_att * inverse
        d_den = -jnp.sum(ratio * att, axis=0, keepdims=True)
        d_high = d_den.astype(BF).astype(F32)
        row = lax.broadcasted_iota(jnp.int32, (EXT - STRETCH, lanes), 0)
        extra = jnp.where(row == 0, d_high, jnp.where(row == 1, d_den - d_high, 0.0))
        ratio_ext = jnp.concatenate([ratio, extra], axis=0)
        ratio_low = ratio_ext.astype(BF)
        weights = w_ref[0, k]
        padded = jnp.concatenate([ratio_low, jnp.zeros((PAIR - EXT, lanes), BF)], axis=0)
        d_weights = dotg(ve, padded, 1, 0)
        d_scores = (d_weights * weights.astype(F32)).astype(BF)
        d_query = dotg(kv, d_scores, 0, 0)[:STRETCH] * scale
        zeros = jnp.zeros((STRETCH, lanes), BF)
        q_scaled = (q.astype(F32) * scale).astype(BF)
        d_kv = dotg(d_scores, jnp.concatenate([q_scaled, zeros], axis=0), 1, 1) + dotg(
            weights, jnp.concatenate([zeros, ratio_low[:STRETCH]], axis=0), 1, 1
        )
        dkv_ref[rows, k * PAIR : (k + 1) * PAIR] += d_kv
        phi = phi_ref[0, k]
        both = jnp.concatenate(
            [jnp.where(low, ratio_ext, 0.0), jnp.where(low, 0.0, ratio_ext)], axis=0
        ).astype(BF)
        d_phi = dotg(s_ref[0, k], both, 0, 0)
        d_state = dotg(both, phi, 1, 1)
        ds_ref[0, k] = d_state
        d_mixed = feature_back(phi, d_phi).astype(BF)
        d_mixed = jnp.concatenate(
            [d_mixed[:, g * PAIR : (g + 1) * PAIR] for g in range(per)], axis=0
        )
        d_stacked = jnp.concatenate(
            [d_query[:, g * PAIR : (g + 1) * PAIR] for g in range(per)], axis=0
        ) + dotg(wq_ref[k], d_mixed, 0, 0)
        dq_ref[0, base : base + per * STRETCH, :] = d_stacked.astype(BF)
        map_ref[k] += dotg(stacked, d_mixed, 1, 1)
        rest = d_state[EXT:] + one_c * carry[k]
        head = d_state[:EXT] + one_b * rest
        carry[k] = head
        ends_ref[k, :EXT] = rest.astype(BF)
        ends_ref[k, EXT : 2 * EXT] = head.astype(BF)

    @pl.when(step == pairs - 1)
    def _():
        for k in range(heads):
            ends_ref[k, 2 * EXT :] = dkv_ref[:STRETCH, k * PAIR : (k + 1) * PAIR].astype(BF)


def keys_kernel(
    batch, pairs, per_block, wide_y, count, n_far, has_prev, info, table, kv_ref, ve_ref, wk_ref,
    phi_ref, dkv_ref, ds_ref, dq_ref, q_up_ref, kv_up_ref, *refs,
):
    fars, refs = refs[:n_far], refs[n_far:]
    prevs, refs = (refs[:1], refs[1:]) if has_prev else (None, refs)
    out_ref, map_ref, carry, back = refs
    step = pl.program_id(0)
    pair = pairs - 1 - step
    heads = kv_ref.shape[1] // PAIR
    slots = Slots(table, batch, 2 * pairs, count)
    block = 2 * pair

    @pl.when(step == 0)
    def _():
        for k in range(heads):
            inner, outer, back[k] = entering(slots, fars, wide_y, count, -1, batch, k)
            carry[k, 0] = outer
            carry[k, 1] = inner
        map_ref[...] = prevs[0][...] if has_prev else jnp.zeros_like(map_ref)

    one_b = slots.weight_one(block + 1)
    one_c = slots.weight_one(block + 2)
    two_c = slots.weight_two(block + 2)
    two_d = slots.weight_two(block + 3)
    row = lax.broadcasted_iota(jnp.int32, (PAIR, PAIR), 0)
    lane = lax.broadcasted_iota(jnp.int32, (PAIR, PAIR), 1)
    last = jnp.where(step == 0, 1.0, 0.0)
    rows = pl.ds(pl.multiple_of(pair * PAIR + STRETCH, STRETCH), PAIR)
    d_kvs = []
    for k in range(heads):
        kv = kv_ref[:, k * PAIR : (k + 1) * PAIR]
        ve = ve_ref[:, k * PAIR : (k + 1) * PAIR].astype(F32)
        next_one, next_two = carry[k, 0], carry[k, 1]
        pad = jnp.zeros((PAIR - EXT, PAIR), F32)
        grads = jnp.concatenate([next_one * two_c, pad, next_two * two_d, pad], axis=0).astype(BF)
        both = jnp.concatenate(
            [jnp.where(row < STRETCH, ve, 0.0), jnp.where(row < STRETCH, 0.0, ve)], axis=1
        ).astype(BF)
        d_phi = dotg(grads, both, 0, 1)
        phi = phi_ref[k * PAIR : (k + 1) * PAIR, :]
        d_both = dotg(phi, grads, 0, 1)
        d_value = jnp.where(row < STRETCH, d_both[:, :PAIR], d_both[:, PAIR:])
        d_value = jnp.where(lane < STRETCH, 0.0, pltpu.roll(d_value, STRETCH, 1))
        d_mixed = feature_back(phi, d_phi).astype(BF)
        d_key = dotg(d_mixed, wk_ref[k], 0, 0)
        map_ref[k] += dotg(kv, d_mixed, 0, 1)
        total = dkv_ref[rows, k * PAIR : (k + 1) * PAIR] + d_value + d_key
        returned = back[k] * last
        total = total + jnp.concatenate([jnp.zeros_like(returned), returned], axis=0)
        d_kvs.append(jnp.transpose(total).astype(BF))
        state = ds_ref[0, k]
        rest = state[EXT:] + one_c * next_one
        carry[k, 1] = rest
        carry[k, 0] = state[:EXT] + one_b * rest
    d_kv = jnp.concatenate(d_kvs, axis=0)
    lanes = pl.ds(pl.multiple_of(pair % per_block * PAIR, PAIR), PAIR)
    out_ref[(pair // per_block) ^ info[1], 32:, lanes] = d_kv

    @pl.when(step == pairs - 1)
    def _():
        for r in range(out_ref.shape[0]):
            back_in = dotg(q_up_ref[...], dq_ref[r], 1, 0) + dotg(
                kv_up_ref[...], out_ref[r, 32:, :], 1, 0
            )
            out_ref[r, :32, :] = (ADAPTER_SCALE * back_in).astype(BF)


def adapter_kernel(
    n_grp, info, dq_ref, rest_ref, mid_ref, normed_ref, att_ref, *refs
):
    blocks_in, (up_ref, oin_ref, wide_ref) = refs[:n_grp], refs[n_grp:]
    share = blocks_in[0].shape[1]
    q_width = dq_ref.shape[1]
    for r in range(n_grp):
        there = pl.ds(pl.multiple_of((info[1] ^ r) * share, share), share)
        mids = mid_ref[:, there]
        rest = rest_ref[r]
        both = jnp.concatenate([dq_ref[r], rest], axis=0)
        up = dotg(mids, both, 1, 1)
        oin = dotg(ADAPTER_SCALE * blocks_in[r][q_width:], att_ref[r, :q_width, :], 1, 1)
        wide = dotg(rest[:32], normed_ref[there, :], 1, 0)
        up_ref[...] = up if r == 0 else up_ref[...] + up
        oin_ref[...] = oin if r == 0 else oin_ref[...] + oin
        wide_ref[...] = wide if r == 0 else wide_ref[...] + wide


def pack_early_kernel(per, map_ref, oin_a, oin_b, out_ref):
    heads = map_ref.shape[0]
    at = 0
    for k in range(heads):
        for g in range(0, per, 2):
            pair = [
                map_ref[k, h * STRETCH : (h + 1) * STRETCH, h * STRETCH : (h + 1) * STRETCH]
                for h in (g, g + 1)
            ]
            out_ref[at : at + STRETCH, :] = jnp.concatenate(pair, axis=1).astype(BF)
            at += STRETCH
    oin = oin_a[...] + oin_b[...]
    for c in range(oin.shape[1] // PAIR):
        out_ref[at : at + 16, :] = oin[:, c * PAIR : (c + 1) * PAIR].astype(BF)
        at += 16


def pack_late_kernel(
    q_width, up_a, up_b, key_ref, wide_in_a, wide_in_b, wide_out_a, wide_out_b, wide_ref, out_ref
):
    for c in range(wide_in_a.shape[1] // PAIR):
        cols = slice(c * PAIR, (c + 1) * PAIR)
        wide_in = wide_in_a[:24, cols] + wide_in_b[:24, cols]
        wide_out = wide_out_a[:8, cols] + wide_out_b[:8, cols]
        wide_ref[c * 32 : (c + 1) * 32, :] = jnp.concatenate([wide_in, wide_out], axis=0).astype(BF)
    up = ADAPTER_SCALE * (up_a[...] + up_b[...])
    at = 0
    for c in range(q_width // PAIR):
        out_ref[at : at + 16, :] = up[:16, c * PAIR : (c + 1) * PAIR].astype(BF)
        at += 16
    for k in range(key_ref.shape[0]):
        first = q_width + 32 + k * PAIR
        out_ref[at : at + 16, :] = up[8:24, first : first + PAIR].astype(BF)
        at += 16
    for k in range(key_ref.shape[0]):
        block = key_ref[k, :STRETCH, :]
        out_ref[at : at + STRETCH, :] = jnp.concatenate([block, block], axis=1).astype(BF)
        at += STRETCH


def unpack_kernel(
    n_grp, columns, info, early_a, early_b, late_a, late_b,
    wide_ref, q_ref, kv_ref, oin_ref, map_ref, key_ref, turned,
):
    early = early_a[...].astype(F32) + early_b[...].astype(F32)
    at = 0
    for h in range(0, map_ref.shape[0], 2):
        map_ref[h] = early[at : at + STRETCH, :STRETCH]
        map_ref[h + 1] = early[at : at + STRETCH, STRETCH:]
        at += STRETCH
    for c in range(oin_ref.shape[1] // PAIR):
        oin_ref[:, c * PAIR : (c + 1) * PAIR] = early[at : at + 8, :]
        at += 16
    first = (info[2] * n_grp + info[1]) * columns
    rows = pl.ds(pl.multiple_of((first // PAIR) * 32, 32), 32)
    sums = late_a[rows, :].astype(F32) + late_b[rows, :].astype(F32)
    turned[...] = jnp.transpose(sums)
    wide_ref[...] = turned[pl.ds(pl.multiple_of(first % PAIR, 8), columns), :]
    at = late_a.shape[0] - sum(
        [q_ref.shape[1] // PAIR * 16, key_ref.shape[0] * 16, key_ref.shape[0] * STRETCH]
    )
    late = late_a[at:, :].astype(F32) + late_b[at:, :].astype(F32)
    at = 0
    for c in range(q_ref.shape[1] // PAIR):
        q_ref[:, c * PAIR : (c + 1) * PAIR] = late[at : at + 8, :]
        at += 16
    for k in range(key_ref.shape[0]):
        cols = slice(k * STRETCH, (k + 1) * STRETCH)
        kv_ref[0, :, cols] = late[at : at + 8, :STRETCH]
        kv_ref[1, :, cols] = late[at + 8 : at + 16, STRETCH:]
        at += 16
    for k in range(key_ref.shape[0]):
        key_ref[k] = late[at : at + STRETCH, :STRETCH]
        at += STRETCH


def whole(shape):
    return pl.BlockSpec(shape, lambda i, *_: (0,) * len(shape))


def anywhere():
    return pl.BlockSpec(memory_space=pl.ANY)


def sds(shape, kind):
    return jax.ShapeDtypeStruct(shape, kind)


def call(
    kernel, name, grid, scalars, ins, in_specs, out_specs, out_shape, scratch=(), alias=None,
    cost=1024,
):
    return pl.pallas_call(
        kernel,
        grid_spec=pltpu.PrefetchScalarGridSpec(
            num_scalar_prefetch=len(scalars),
            grid=(grid,),
            in_specs=in_specs,
            out_specs=out_specs,
            scratch_shapes=list(scratch),
        ),
        out_shape=out_shape,
        input_output_aliases=alias or {},
        cost_estimate=pl.CostEstimate(flops=0, transcendentals=0, bytes_accessed=cost),
        compiler_params=pltpu.CompilerParams(
            dimension_semantics=("arbitrary",),
            vmem_limit_bytes=VMEM_LIMIT if name in LARGE else SMALL_LIMIT,
        ),
        name=name,
    )(*scalars, *ins)


def run_assemble(info, ring, splits):
    shape = ring.parts[0].shape
    parts_of = ring_layout(ring.count, shape[0])
    outs = [(size, shape[1] * ring.count) for size in splits]
    return call(
        functools.partial(assemble_kernel, parts_of, shape[1], splits), "assemble", 1, [info],
        ring.parts, [whole(part.shape) for part in ring.parts], [whole(out) for out in outs],
        [sds(out, BF) for out in outs],
    )


def run_layout(info, lens, blocks):
    count = lax.axis_size("seq")
    size = lens.shape[0] * TABLE_ROWS * table_width(blocks, count)
    return call(
        functools.partial(layout_kernel, blocks, max(1, count // 4), count), "layout", 1,
        [info, lens], [], [], pl.BlockSpec(memory_space=pltpu.SMEM), sds((size,), jnp.int32),
    )


def run_layer(table, ends, sign):
    count = lax.axis_size("seq")
    batches, heads = ends[0].shape[:2]
    full = sds((batches, heads, EXT, PAIR), BF)
    out = [sds(ends[0].shape, BF), full]
    per_batch = table.shape[0] // batches // TABLE_ROWS
    blocks = max(per_batch - 4, 0)
    return call(
        functools.partial(layer_kernel, sign, blocks, count, len(ends)), "layer", 1, [table], ends,
        [whole(item.shape) for item in ends], [whole(item.shape) for item in out], out,
    )


def run_project(table, batch, normed, weight, q_up, kv_up, maps):
    rows, model = normed.shape
    heads = maps.shape[0]
    width = heads * PAIR
    q_width = weight.shape[0] - 32 - width
    tile = 4 * PAIR
    pairs = rows // PAIR
    return call(
        functools.partial(
            project_kernel, batch, q_width, rows // STRETCH, lax.axis_size("seq")
        ),
        "project_states", rows // tile, [table],
        [normed, weight, q_up, kv_up, maps],
        [
            pl.BlockSpec((tile, model), lambda i, *_: (i, 0)),
            whole(weight.shape), whole(q_up.shape), whole(kv_up.shape), whole(maps.shape),
        ],
        [
            pl.BlockSpec((q_width, tile), lambda i, *_: (0, i)),
            pl.BlockSpec((tile, width), lambda i, *_: (i, 0)),
            pl.BlockSpec((tile, width), lambda i, *_: (i, 0)),
            pl.BlockSpec((32, tile), lambda i, *_: (0, i)),
            pl.BlockSpec((width, tile), lambda i, *_: (0, i)),
            pl.BlockSpec((4, heads, 2 * EXT, PAIR), lambda i, *_: (i, 0, 0, 0)),
            whole((heads, 2 * PAIR + 32, PAIR)),
        ],
        [
            sds((q_width, rows), BF),
            sds((rows, width), BF),
            sds((rows, width), BF),
            sds((32, rows), BF),
            sds((width, rows), BF),
            sds((pairs, heads, 2 * EXT, PAIR), F32),
            sds((heads, 2 * PAIR + 32, PAIR), BF),
        ],
        [pltpu.VMEM((heads, EXT, PAIR), F32)],
    )


def run_forward(info, table, batch, q, kv, ve, maps, o_in, states, fars):
    q_width, rows = q.shape
    width = kv.shape[1]
    heads, pairs = width // PAIR, rows // PAIR
    per = q_width // STRETCH // heads
    count = lax.axis_size("seq")
    wide = max(1, count // 4)
    scale = STRETCH ** (-0.5) * math.log2(math.e)
    step = lambda *shape: pl.BlockSpec((1,) + shape, lambda i, *_: (i,) + (0,) * len(shape))
    column = lambda n: pl.BlockSpec((n, PAIR), lambda i, *_: (0, i))
    share = rows // lax.axis_size("grp")
    return call(
        functools.partial(
            forward_kernel, batch, per, rows // STRETCH, wide, count, len(fars), scale
        ),
        "attention_forward", pairs, [info, table],
        [q, kv, ve, maps, o_in, states, *fars],
        [
            column(q_width), whole(kv.shape), whole(ve.shape),
            whole(maps.shape), whole(o_in.shape), step(heads, 2 * EXT, PAIR),
            *[whole(far.shape) for far in fars],
        ],
        [
            block_spec(q_width + 16, share, lambda i: i), step(heads, WIN, per * PAIR),
            step(heads, PAIR, per * PAIR), step(heads, 2 * EXT, PAIR), step(heads * per, PAIR),
        ],
        [
            sds((rows // share, q_width + 16, share), BF),
            sds((pairs, heads, WIN, per * PAIR), BF),
            sds((pairs, heads, PAIR, per * PAIR), BF),
            sds((pairs, heads, 2 * EXT, PAIR), BF),
            sds((pairs, heads * per, PAIR), F32),
        ],
        [
            pltpu.VMEM((heads, 2, EXT, PAIR), F32),
            pltpu.VMEM((rows + STRETCH, width), BF),
            pltpu.VMEM((rows + STRETCH, width), BF),
        ],
        cost=LATE_COST,
    )


def block_spec(height, share, pair_of):
    per_block = share // PAIR
    return pl.BlockSpec(
        (1, height, PAIR),
        lambda i, info, *_: ((pair_of(i) // per_block) ^ info[1], 0, pair_of(i) % per_block),
    )


def own_spec(batch, share, model):
    return pl.BlockSpec((1, share, model), lambda i, info: (batch, info[1], 0))


def front(array):
    if len(array.shape) == 2:
        return whole(array.shape)
    return pl.BlockSpec((1,) + array.shape[1:], lambda i, *_: (0, 0, 0))


def run_residual(info, batch, tokens, gain, atts, weights):
    n_grp = len(atts)
    model = tokens.shape[2]
    share = atts[0].shape[-1]
    return call(
        functools.partial(residual_kernel, n_grp), "residual", 1, [info],
        [tokens, gain, *atts, *weights],
        [own_spec(batch, share, model), whole(gain.shape), *[front(att) for att in atts]]
        + [anywhere()] * n_grp,
        [whole((share, model)), whole((share, model)), whole((16, share))],
        [sds((share, model), F32), sds((share, model), BF), sds((16, share), BF)],
        [
            pltpu.VMEM((n_grp,) + weights[0].shape, BF),
            pltpu.SemaphoreType.DMA((n_grp,)),
        ],
    )


def run_branch(info, batch, cotangent, resid, gain, mid, summands, weights):
    n_grp = len(weights)
    share, model = resid.shape
    out = (weights[0].shape[0], share)
    return call(
        functools.partial(branch_kernel, n_grp, len(summands)), "branch_gradient", 1, [info],
        [cotangent, resid, gain, mid, *summands, *weights],
        [
            own_spec(batch, share, model), whole(resid.shape), whole(gain.shape),
            whole(mid.shape), *[whole(resid.shape) for _ in summands],
        ]
        + [anywhere()] * n_grp,
        [whole((share, model)), whole((16, model))] + [whole(out)] * n_grp,
        [sds((share, model), F32), sds((16, model), F32)] + [sds(out, BF)] * n_grp,
        [
            pltpu.VMEM((n_grp,) + weights[0].shape, BF),
            pltpu.SemaphoreType.DMA((n_grp,)),
        ],
        cost=LATE_COST,
    )


def run_tokens(info, batch, tokens, gain, d_resid, dqs, rests, weights, prev):
    n_grp = len(weights)
    batches, _, model = tokens.shape
    share = d_resid.shape[0]
    ins = [tokens, gain, d_resid, *dqs, *rests, *weights]
    specs = [
        own_spec(batch, share, model), whole(gain.shape), whole(d_resid.shape),
        *[front(a) for a in [*dqs, *rests]],
    ] + [anywhere()] * n_grp
    alias = {}
    if prev is not None:
        alias = {len(ins) + 1: 0}
        ins.append(prev)
        specs.append(anywhere())
    return call(
        functools.partial(tokens_kernel, n_grp), "token_gradient", 1, [info], ins, specs,
        pl.BlockSpec((1, share, model), lambda i, *_: (batch, 0, 0)),
        sds((batches, share, model), F32),
        [
            pltpu.VMEM((n_grp,) + weights[0].shape, BF),
            pltpu.VMEM((share, model), F32),
            pltpu.SemaphoreType.DMA((n_grp,)),
        ],
        alias,
        LATE_COST,
    )


def run_mlp(info, batch, xs, rels, cotangent, rings, prevs, sizes):
    n_grp = len(xs)
    share, model = xs[0].shape
    rows = share * n_grp
    depth = rings[0].parts[0].shape[0]
    layout = ring_layout(rings[0].count, depth)
    first = prevs is None
    prevs = [] if first else list(prevs)
    ins = [*xs, cotangent, *[part for ring in rings for part in ring.parts], *prevs]
    if first:
        out_shape = [sds((rows, model), BF)] * 2
    else:
        out_shape = [sds((share, model), BF)] * (2 * n_grp)
    scratch = [
        pltpu.VMEM((rows, model), BF),
        pltpu.VMEM((rows, model), BF),
        pltpu.VMEM((2, model, 3 * CHUNK), BF),
        pltpu.VMEM((rows, model), F32),
        pltpu.VMEM((rows, model), F32),
        pltpu.SemaphoreType.DMA((rows // ROW_TILE + 1,)),
        pltpu.SemaphoreType.DMA((2,)),
    ] + [pltpu.VMEM((rows, model), BF) for _ in prevs]
    return call(
        functools.partial(mlp_kernel, batch, rels, layout, sizes, first),
        "feed_forward", sum(sizes) // CHUNK, [info], ins, [anywhere()] * len(ins),
        [anywhere()] * len(out_shape), out_shape, scratch,
    )


def run_backward(
    info, table, batch, q, kv, ve, maps, o_in, att, weights, phi, states, inverse, fars, d_outs, prevs,
):
    q_width, rows = q.shape
    width = kv.shape[1]
    heads, pairs = width // PAIR, rows // PAIR
    per = q_width // STRETCH // heads
    share = rows // len(d_outs)
    count = lax.axis_size("seq")
    rev = lambda i: pairs - 1 - i
    step = lambda *shape: pl.BlockSpec((1,) + shape, lambda i, *_: (rev(i),) + (0,) * len(shape))
    column = lambda n: pl.BlockSpec((n, PAIR), lambda i, *_: (0, rev(i)))
    prevs = list(prevs or [])
    sums = [sds(maps.shape, F32)]
    return call(
        functools.partial(
            backward_kernel, batch, per, pairs, len(d_outs), bool(prevs), count, max(1, count // 4),
            len(fars), STRETCH ** (-0.5),
        ),
        "attention_backward", pairs, [info, table],
        [q, kv, ve, maps, o_in, att, weights, phi, states, inverse, *fars, *d_outs, *prevs],
        [
            column(q_width), whole(kv.shape), whole(ve.shape),
            whole(maps.shape), whole(o_in.shape), block_spec(q_width + 16, share, rev),
            step(heads, WIN, per * PAIR), step(heads, PAIR, per * PAIR),
            step(heads, 2 * EXT, PAIR), step(heads * per, PAIR),
            *[whole(far.shape) for far in fars], *[anywhere() for _ in d_outs],
            *[whole(prev.shape) for prev in prevs],
        ],
        [
            block_spec(q_width, share, rev), whole((rows + STRETCH, width)), step(heads, 2 * EXT, PAIR),
            whole((heads, 2 * EXT + STRETCH, PAIR)), *[whole(item.shape) for item in sums],
        ],
        [
            sds((rows // share, q_width, share), BF),
            sds((rows + STRETCH, width), F32),
            sds((pairs, heads, 2 * EXT, PAIR), F32),
            sds((heads, 2 * EXT + STRETCH, PAIR), BF),
            *sums,
        ],
        [
            pltpu.VMEM((heads, EXT, PAIR), F32),
            pltpu.VMEM((rows + STRETCH, width), BF),
            pltpu.VMEM((rows + STRETCH, width), BF),
            pltpu.VMEM((pairs, q_width + 16, PAIR), BF),
            pltpu.SemaphoreType.DMA,
        ],
        cost=LATE_COST,
    )


def run_keys(
    info, table, batch, kv, ve, maps, phi, d_kv, d_states, d_q, q_up, kv_up, fars, prevs,
):
    width, rows = phi.shape
    heads, pairs = width // PAIR, rows // PAIR
    n_grp, q_width, share = d_q.shape
    count = lax.axis_size("seq")
    wide = max(1, count // 4)
    rev = lambda i: pairs - 1 - i
    column = lambda n: pl.BlockSpec((n, PAIR), lambda i, *_: (0, rev(i)))
    lines = lambda n: pl.BlockSpec((PAIR, n), lambda i, *_: (rev(i), 0))
    prevs = list(prevs or [])
    sums = [sds((heads, PAIR, STRETCH), F32)]
    return call(
        functools.partial(
            keys_kernel, batch, pairs, share // PAIR, wide, count, len(fars), bool(prevs)
        ),
        "attention_keys", pairs, [info, table],
        [
            kv, ve, maps, phi, d_kv, d_states, d_q, q_up, kv_up, *fars, *prevs,
        ],
        [
            lines(width), lines(width), whole(maps.shape), column(width), whole(d_kv.shape),
            pl.BlockSpec((1, heads, 2 * EXT, PAIR), lambda i, *_: (rev(i), 0, 0, 0)),
            whole(d_q.shape), whole(q_up.shape), whole(kv_up.shape),
            *[whole(far.shape) for far in fars], *[whole(prev.shape) for prev in prevs],
        ],
        [whole((n_grp, 32 + width, share)), *[whole(item.shape) for item in sums]],
        [sds((n_grp, 32 + width, share), BF), *sums],
        [pltpu.VMEM((heads, 2, EXT, PAIR), F32), pltpu.VMEM((heads, STRETCH, PAIR), F32)],
        cost=LATE_COST,
    )


def run_adapters(info, d_q, rest, mids, normed, att, d_outs):
    model = normed.shape[1]
    ins = [d_q, rest, mids, normed, att, *d_outs]
    out_shape = [
        sds((32, d_q.shape[1] + rest.shape[1]), F32), sds((16, d_q.shape[1]), F32),
        sds((32, model), F32),
    ]
    return call(
        functools.partial(adapter_kernel, len(d_outs)),
        "adapter_gradients", 1, [info], ins, [whole(item.shape) for item in ins],
        [whole(item.shape) for item in out_shape], out_shape,
        cost=LATE_COST,
    )


def run_plain(kernel, name, scalars, ins, out_shape, scratch=()):
    return call(
        kernel, name, 1, scalars, ins, [whole(item.shape) for item in ins],
        [whole(item.shape) for item in out_shape], out_shape, scratch,
    )


def group_sum(value):
    total = value.astype(F32)
    for r in range(1, lax.axis_size("grp")):
        total = total + flip(value, "grp", r).astype(F32)
    return total.astype(BF)


def local(
    tokens,
    cotangent,
    lengths,
    attention_norm_gain,
    feedforward_norm_gain,
    query_weight,
    keyvalue_weight,
    output_weight,
    gate_up_weight,
    down_weight,
    adapter_width_factor,
    query_up_factor,
    keyvalue_up_factor,
    output_input_factor,
    query_feature_weight,
    key_feature_weight,
):
    batches, rows, model = tokens.shape
    n_seq, n_grp = lax.axis_size("seq"), lax.axis_size("grp")
    group_index, seq_index = lax.axis_index("grp"), lax.axis_index("seq")
    share = rows // n_grp
    rank = adapter_width_factor.shape[2]
    depth, q_width = query_weight.shape
    kv_heads = key_feature_weight.shape[0]
    kv_width = kv_heads * PAIR
    per = query_feature_weight.shape[0] // kv_heads
    hidden_width = down_weight.shape[0]
    gain_attn = attention_norm_gain.astype(F32)[None]
    gain_mlp = feedforward_norm_gain.astype(F32)[None]

    sources = lax.dynamic_index_in_dim(
        jnp.asarray(ring_sources(n_seq), jnp.int32), seq_index, 0, False
    )
    info = jnp.concatenate(
        [jnp.stack([seq_index * (rows // STRETCH), group_index, seq_index]).astype(jnp.int32), sources]
    )

    kv_shard = (
        keyvalue_weight.reshape(depth, 2, kv_heads, STRETCH)
        .transpose(2, 1, 3, 0)
        .reshape(kv_width, depth)
    )
    adapters = adapter_width_factor.transpose(0, 2, 1)
    pad = jnp.zeros((rank, depth), BF)
    in_ring = Ring(
        jnp.concatenate(
            [
                query_weight.T, adapters[:3].reshape(3 * rank, depth), pad, kv_shard,
                output_weight, adapters[3], pad,
            ],
            axis=0,
        )
    )
    down_t = down_weight.T
    half_shards = [
        jnp.concatenate(
            [
                gate_up_weight[:, 0, first : first + size],
                gate_up_weight[:, 1, first : first + size],
                down_t[:, first : first + size],
            ],
            axis=1,
        )
        for first, size in pieces_of(hidden_width)
    ]
    ring_a, ring_c = [Ring(shard) for shard in half_shards]
    kv_parts = keyvalue_up_factor.reshape(2, rank, kv_heads, STRETCH)
    kv_up = jnp.zeros((2, rank, kv_heads, 2, STRETCH), BF)
    kv_up = kv_up.at[0, :, :, 0].set(kv_parts[0]).at[1, :, :, 1].set(kv_parts[1])
    kv_up = kv_up.reshape(2 * rank, kv_width)
    kv_up = jnp.concatenate(
        [jnp.zeros((rank, kv_width), BF), kv_up, jnp.zeros((rank, kv_width), BF)]
    )
    q_up = jnp.concatenate([query_up_factor, jnp.zeros((3 * rank, q_width), BF)])
    q_up_t = q_up.T
    o_in = jnp.concatenate([output_input_factor, jnp.zeros((q_width, rank), BF)], axis=1)
    maps_t = query_feature_weight.transpose(0, 2, 1).reshape(kv_heads, per, STRETCH, STRETCH)
    query_maps = jnp.zeros((kv_heads, per, STRETCH, per, STRETCH), BF)
    for g in range(per):
        query_maps = query_maps.at[:, g, :, g, :].set(maps_t[:, g])
    query_maps = query_maps.reshape(kv_heads, per * STRETCH, per * STRETCH)
    key_maps = jnp.concatenate(
        [key_feature_weight.transpose(0, 2, 1), jnp.zeros((kv_heads, STRETCH, STRETCH), BF)], axis=2
    )

    normed_rows = []
    for batch in range(batches):
        x = tokens[batch].astype(F32)
        factor = lax.rsqrt(jnp.mean(x * x, axis=-1, keepdims=True) + EPS)
        normed_rows.append((x * factor * gain_attn).astype(BF))
    in_ring.hop()
    in_ring.hop()
    table = run_layout(info, lengths, rows // STRETCH)
    table, query_maps, key_maps, kv_up, q_up_t, normed_rows[0] = in_ring.tie(
        table, query_maps, key_maps, kv_up, q_up_t, normed_rows[0]
    )
    in_ring.hop()
    normed_rows[1] = in_ring.tie(normed_rows[1])[0]
    while in_ring.done < in_ring.hops():
        in_ring.hop()
    ring_a.hop(*in_ring.parts[-2:])
    weight_in, weight_out = run_assemble(
        info, in_ring, [q_width + 32 + kv_width, q_width + 2 * rank]
    )
    far_out = far_gather(weight_out)

    saved = []
    for batch in range(batches):
        normed = normed_rows[batch]
        q, kv, ve, mids, phi_key, states, ends = run_project(
            table, batch, normed, weight_in, q_up_t, kv_up, key_maps
        )
        saved.append([q, kv, ve, mids, normed, phi_key, states, ends])
    ends = jnp.stack([item[7] for item in saved])
    (ends,) = ring_a.tie(ends)
    fars = exchange(table, ends, 1)
    for item in saved:
        item[7] = fars
    far_out = [far_out[0]] + [after(far, *fars[1:]) for far in far_out[1:]]
    weights_out = near_gather(far_out)
    ring_a.hop(*fars[1:])

    attended, att_sets, far_mlp, mlp_ins = [], [], [], []
    for batch in range(batches):
        q, kv, ve, mids, normed, phi_key, states, fars = saved[batch]
        if batch:
            q = after(q, att)
        att, weights, phi, sums, inverse = run_forward(
            info, table, batch, q, kv, ve, query_maps, o_in, states, fars
        )
        atts = group_exchange([att[r] for r in range(n_grp)])
        att_sets.append([att, *atts[1:]])
        attended.append([att, weights, phi, sums, inverse])
    att_sets[0][1], att_sets[1][1] = ring_a.tie(att_sets[0][1], att_sets[1][1])
    ring_a.hop()
    for batch in range(batches):
        if batch:
            att_sets[1][0] = after(att_sets[1][0], mlp_in)
        resid, mlp_in, mid = run_residual(
            info, batch, tokens, gain_mlp, att_sets[batch], weights_out
        )
        attended[batch] += [resid, mid]
        if batch:
            mlp_in, *far_mlp[0][1:] = ring_a.tie(mlp_in, *far_mlp[0][1:])
            ring_a.hop()
        else:
            mlp_in, *att_sets[1][2:] = lax.optimization_barrier((mlp_in, *att_sets[1][2:]))
        far_mlp.append(far_gather(mlp_in))
    ring_a.finish()
    ring_c.hop(*ring_a.parts[-2:])
    far_mlp[1] = list(lax.optimization_barrier((*far_mlp[1], *ring_a.parts[-2:])))[: len(far_mlp[1])]
    far_mlp[0][0] = after(far_mlp[0][0], *far_mlp[1][1:])
    for batch in range(batches):
        mlp_ins.append(near_gather(far_mlp[batch]))

    sizes = [size for _, size in pieces_of(hidden_width)]
    partial = [None] * batches
    every = list(range(n_grp))
    partial[0] = list(
        run_mlp(info, 0, mlp_ins[0], every, cotangent, [ring_a], None, sizes[:1])
    )
    partial[0][0], mlp_ins[1][0] = ring_c.tie(partial[0][0], mlp_ins[1][0])
    ring_c.hop()
    far_in = far_gather(after(weight_in, partial[0][0], *mlp_ins[1][2:]))
    partial[1] = list(
        run_mlp(info, 1, mlp_ins[1], every, cotangent, [ring_a], None, sizes[:1])
    )
    (partial[1][0],) = ring_c.tie(partial[1][0])
    ring_c.hop()
    ring_c.finish()
    far_in, partial[0][0] = lax.optimization_barrier((far_in, partial[0][0]))
    weights_in = near_gather(far_in)
    partial[0] = list(
        run_mlp(info, 0, mlp_ins[0], every, cotangent, [ring_c], partial[0], sizes[1:])
    )
    started = [scatter_start(partial[0][:n_grp])]
    started[0][0][0], partial[1][0] = lax.optimization_barrier((started[0][0][0], partial[1][0]))
    def run_branch_of(batch, summands):
        resid, mid = attended[batch][5:]
        d_resid, wide, *d_out = run_branch(
            info, batch, cotangent, resid, gain_mlp, mid, summands, weights_out
        )
        return d_resid, wide, group_exchange(d_out)

    def run_backward_of(batch, q, d_outs, sums_back):
        _, kv, ve, mids, normed, phi_key, states, fars = saved[batch]
        att, weights, phi, sums, inverse = attended[batch][:5]
        d_q, d_kv, d_states, ends, *sums_back = run_backward(
            info, table, batch, q, kv, ve, query_maps, o_in, att, weights, phi, sums, inverse, fars,
            d_outs, sums_back,
        )
        return [d_q, None, d_kv, d_states], ends, sums_back

    def run_keys_of(batch, kv, gone, sums_keys):
        _, _, ve, mids, normed, phi_key, states, _ = saved[batch]
        d_q, d_qs, d_kv, d_states, fars = gone
        rest, *sums_keys = run_keys(
            info, table, batch, kv, ve, key_maps, phi_key, d_kv, d_states, d_q, q_up, kv_up, fars,
            sums_keys,
        )
        rests = group_exchange([rest[r] for r in range(n_grp)])
        return [rest, *rests[1:]], sums_keys

    def run_adapters_of(batch, d_q, rest, d_outs):
        return run_adapters(
            info, d_q, rest, saved[batch][3], saved[batch][4], attended[batch][0], d_outs
        )

    def run_tokens_of(batch, d_resid, gone, rests, prev):
        d_q, d_qs = gone[:2]
        return run_tokens(
            info, batch, tokens, gain_attn, d_resid, [d_q, *d_qs[1:]], rests, weights_in, prev
        )

    def finish_rows(batch, *ready):
        blocks = partial[batch][n_grp:]
        blocks[0] = after(blocks[0], *ready)
        blocks[1], blocks[-1] = after(blocks[1], *ready), after(blocks[-1], *ready)
        return scatter_start(blocks)

    def rows_of(batch, summands):
        total = attended[batch][5]
        for summand in summands:
            total = total + summand.astype(F32)
        return total.astype(BF)

    low = n_grp // 2
    upper = run_mlp(
        info, 1, mlp_ins[1][low:], every[low:], cotangent, [ring_c], partial[1], sizes[1:]
    )
    summands_a = scatter_end(*started[0])
    crossed = [flip(upper[far + 1 - low], "grp", 1) for far in range(low, n_grp, 2)]
    crossed[0], summands_a[-1] = lax.optimization_barrier((crossed[0], summands_a[-1]))
    far_b = [
        (upper[far - low].astype(F32) + there.astype(F32)).astype(BF)
        for far, there in zip(range(low, n_grp, 2), crossed)
    ]
    attended[0][6] = after(attended[0][6], far_b[0])
    d_resid_a, wide_a, d_outs_a = run_branch_of(0, summands_a)
    partial[1][0] = after(partial[1][0], d_resid_a)
    lower = list(
        run_mlp(info, 1, mlp_ins[1][:low], every[:low], cotangent, [ring_c], partial[1], sizes[1:])
    )
    late_b = scatter_end(far_b, [])
    lower[1], late_b[-1] = lax.optimization_barrier((after(lower[1], *d_outs_a[2:]), late_b[-1]))
    near_b = [lower[0], flip(lower[1], "grp", 1)]
    early_b = [far_pair(lower[far], lower[far + 1]) for far in range(2, low, 2)]
    summands_b = near_b + scatter_end(early_b, []) + late_b
    partial[1] = [None] * n_grp + list(lower[low:]) + list(upper[low:])
    d_resid_b, wide_b, d_outs_b = run_branch_of(1, summands_b)
    gone_a, ends_a, sums_back = run_backward_of(
        0, after(saved[0][0], d_resid_b), d_outs_a, None
    )
    blocks = partial[0][n_grp:]
    crossed = [flip(after(blocks[r + 1], d_resid_b), "grp", 1) for r in range(0, n_grp, 2)]
    crossed[-1] = after(crossed[-1], gone_a[0], *d_outs_b[2:])
    fars_a = [
        (blocks[r].astype(F32) + crossed[r // 2].astype(F32)).astype(BF)
        for r in range(2, n_grp, 2)
    ]
    rows_a = scatter_end(fars_a, [blocks[0], crossed[0]])
    gone_b, ends_b, sums_back = run_backward_of(
        1, after(saved[1][0], gone_a[0], *fars_a), d_outs_b, sums_back
    )
    fars = exchange(table, jnp.stack([ends_a, ends_b]), -1)
    gone_a.append(fars)
    gone_b.append(fars)
    for gone in (gone_a, gone_b):
        held = after(gone[0], gone_b[0])
        gone[1] = group_exchange([held[r] for r in range(n_grp)])
    kv_a, rows_a[-1] = lax.optimization_barrier((after(saved[0][1], gone_b[0]), rows_a[-1]))
    rests_a, sums_keys = run_keys_of(0, kv_a, gone_a, None)
    kv_b = after(saved[1][1], rests_a[0])
    kv_b = after(kv_b, *gone_a[1][1:], *gone_b[1][1:])
    rests_b, sums_keys = run_keys_of(1, kv_b, gone_b, sums_keys)
    sums_a = run_adapters_of(
        0, after(gone_a[0], rests_b[0]), rests_a[0], d_outs_a
    )
    fars_b, nears_b = finish_rows(1, rests_b[0])
    sums_b = run_adapters_of(
        1, after(gone_b[0], sums_a[0], *rests_a[1:]), rests_b[0], d_outs_b
    )

    (early,) = run_plain(
        functools.partial(pack_early_kernel, per), "pack_early", [],
        [sums_back[0], sums_a[1], sums_b[1]],
        [sds((STRETCH * kv_heads * per // 2 + 16 * (q_width // PAIR), PAIR), BF)],
    )
    late_rows = 16 * (q_width // PAIR) + (16 + STRETCH) * kv_heads
    wide_a = after(wide_a, fars_b[0])
    rows_b = scatter_end(fars_b, nears_b)
    wide, late = run_plain(
        functools.partial(pack_late_kernel, q_width), "pack_late", [],
        [sums_a[0], sums_b[0], sums_keys[0], sums_a[2], sums_b[2], wide_a, wide_b],
        [sds((32 * (model // PAIR), PAIR), BF), sds((late_rows, PAIR), BF)],
    )
    wide = group_sum(wide)
    wide = after(wide, *rests_b[1:])
    first = early.shape[0]
    columns = model // (n_seq * n_grp)
    value, bits = jnp.concatenate([early, wide, late]), n_seq.bit_length() - 1
    grad_tokens, held = None, [d_resid_a, d_resid_b]
    for step in range(bits):
        there = flip(value, "seq", 1 << step)
        batch = step - (bits - 2)
        if batch >= 0:
            gone, rests = ((gone_a, rests_a), (gone_b, rests_b))[batch]
            grad_tokens = run_tokens_of(
                batch, after(held[batch], value), gone, rests, grad_tokens
            )
            there, grad_tokens = lax.optimization_barrier((there, grad_tokens))
            if batch == 0:
                held[1], rows_b[-1] = lax.optimization_barrier((held[1], rows_b[-1]))
        if step < bits - 1:
            value = (value.astype(F32) + there.astype(F32)).astype(BF)
    packed = (value, there)
    block_rows = [rows_of(0, rows_a), rows_of(1, rows_b)]
    wide, q_grad, kv_grad, oin_grad, query_grad, key_grad = run_plain(
        functools.partial(unpack_kernel, n_grp, columns), "unpack", [info],
        [packed[0][:first], packed[1][:first], packed[0][first:], packed[1][first:]],
        [
            sds((columns, 32), F32), sds((rank, q_width), F32),
            sds((2, rank, kv_heads * STRETCH), F32), sds((rank, q_width), F32),
            sds(query_feature_weight.shape, F32), sds(key_feature_weight.shape, F32),
        ],
        [pltpu.VMEM((PAIR, 32), F32)],
    )
    return (
        jnp.stack(block_rows),
        grad_tokens,
        wide.reshape(columns, 4, rank).transpose(1, 0, 2),
        q_grad,
        kv_grad,
        oin_grad.T,
        query_grad,
        key_grad,
    )


def solution(mesh):
    return jax.shard_map(
        local,
        mesh=mesh,
        in_specs=(
            P(None, "seq", None),
            P(None, "seq", None),
            P(),
            P(),
            P(),
            P("seq", "grp"),
            P("seq", None, "grp"),
            P("grp", "seq"),
            P("seq", None, "grp"),
            P("grp", "seq"),
            P(None, "seq", None),
            P(None, "grp"),
            P(None, None, "grp"),
            P("grp", None),
            P("grp", None, None),
            P("grp", None, None),
        ),
        out_specs=(
            P(None, ("seq", "grp"), None),
            P(None, ("seq", "grp"), None),
            P(None, ("seq", "grp"), None),
            P(None, "grp"),
            P(None, None, "grp"),
            P("grp", None),
            P("grp", None, None),
            P("grp", None, None),
        ),
        check_vma=False,
    )
```
